32 devices in a mesh: rows: 16 (over z, y, x), branch: 2 (over core).
Axes of the slice: x: 2, y: 2, z: 4, core: 2. Of those that a mesh axis runs over, the one named last changes fastest.
Arguments:
- node_states: bfloat16 [2, 32768, 512], P(None, 'rows'), may hold values from -6 to 6
- serve: int32 [2, 2048], P(None, 'rows'), may hold values from 0 to 2047
- neighbors: int32 [2, 32768, 8], P(None, 'rows'), may hold values from 0 to 127
- alpha: float32 [2, 32768, 8], P(None, 'rows'), may hold values from 0.05 to 0.4
- live: int32 [2, 16], P(None, 'rows'), may hold values from 1 to 2048, as said below
- lam: float32 [2, 32768], P(None, 'rows'), may hold values from 0.5 to 2
- labels: int32 [2, 32768], P(None, 'rows'), may hold values from 0 to 40
- link_pair: int32 [2, 32768], P(None, 'rows'), may hold values from 0 to 127
- mats: float32 [2, 2, 2, 512, 512], P(None, None, 'branch', 'rows'), may hold values from -0.25 to 0.25
- mats_m: float32 [2, 2, 2, 512, 512], P(None, None, 'branch', 'rows'), may hold values from -3.90625e-06 to 3.90625e-06
- mats_v: float32 [2, 2, 2, 512, 512], P(None, None, 'branch', 'rows'), may hold values from 9.536743e-13 to 3.8146973e-12
- basis: float32 [2, 2, 2, 512, 512], P(None, None, 'branch'), as said below
- bias: float32 [2, 2, 512], P(None, 'branch', 'rows'), may hold values from -0.6 to 0.6
- bias_m: float32 [2, 2, 512], P(None, 'branch', 'rows'), may hold values from -3.90625e-05 to 3.90625e-05
- bias_v: float32 [2, 2, 512], P(None, 'branch', 'rows'), may hold values from 9.536743e-11 to 3.8146972e-10
- head: float32 [513, 41], replicated, may hold values from -0.25 to 0.25
- head_m: float32 [513, 41], replicated, may hold values from -3.90625e-05 to 3.90625e-05
- head_v: float32 [513, 41], replicated, may hold values from 9.536743e-11 to 3.8146972e-10
Outputs:
- loss_parts: float32 [2], replicated
- grad_norm: float32 [], replicated
- mats_new: float32 [2, 2, 2, 512, 512], P(None, None, 'branch', 'rows')
- mats_low: bfloat16 [2, 2, 2, 512, 512], P(None, None, 'branch', 'rows')
- mats_m_new: float32 [2, 2, 2, 512, 512], P(None, None, 'branch', 'rows')
- mats_v_new: float32 [2, 2, 2, 512, 512], P(None, None, 'branch', 'rows')
- bias_new: float32 [2, 2, 512], P(None, 'branch', 'rows')
- bias_m_new: float32 [2, 2, 512], P(None, 'branch', 'rows')
- bias_v_new: float32 [2, 2, 512], P(None, 'branch', 'rows')
- head_new: float32 [513, 41], replicated
- head_m_new: float32 [513, 41], replicated
- head_v_new: float32 [513, 41], replicated
The draws below stay inside these ranges and needn't reach their ends.
Inputs may be any that keep to these rules, and one draw needn't show every extreme that they name: `serve`: device p's entries d * 8 to d * 8 + 7 of a micro-batch name rows of p's own block of 2048 rows that device d reads. `neighbors`: slots of the reading device's table. `link_pair`: slots of the reading device's table. A device's live rows are its first ones; the last device along rows has all 2048 rows live in every micro-batch. `basis`: each matrix is orthogonal.
All inputs are finite; a program needn't handle non-finite values.
Results may differ from the reference program's by a relative error of at most 0.0038.
Values may be sent and summed in bfloat16 or wider, within the bound.
No kernel may reach another device: no remote copies, remote signals or barrier semaphores. Data moves between devices by JAX's collectives and lax.ppermute only.
A program may use at most 192 MiB of HBM per device.

```python
import math
import jax
import jax.numpy as jnp
from jax import lax

H = 512
C = 41
LAYERS = 2
MB = 2
DEG = 8
CAP = 8
STEP = 5
R_DEV = 2048
NODES = 32768
SLOTS = 128
N_ROWS = 16


def draw_live(key, part):
    device = jnp.arange(N_ROWS, dtype=jnp.int32)
    base = R_DEV // 4 + 3 * R_DEV * (device + 1) // (4 * N_ROWS)
    cut = jax.random.randint(key, (MB, N_ROWS), 0, R_DEV // 8 + 1)
    count = jnp.clip(base[None, :] - cut, 1, R_DEV)
    return jnp.where(device[None, :] == N_ROWS - 1, R_DEV, count).astype(jnp.int32)


def draw_basis(key, part):
    count = LAYERS * 4
    index = jnp.arange(H, dtype=jnp.int32)
    freq = index.astype(jnp.float32)[:, None]
    place = (2.0 * index.astype(jnp.float32) + 1.0)[None, :]
    table = jnp.cos(jnp.pi * freq * place / (2.0 * H)) * jnp.sqrt(2.0 / H)
    table = jnp.where(index[:, None] == 0, jnp.sqrt(1.0 / H), table).astype(jnp.float32)
    key_perm = jax.random.fold_in(key, 11)
    key_left = jax.random.fold_in(key, 12)
    key_right = jax.random.fold_in(key, 13)
    order = jax.random.permutation(key_perm, jnp.broadcast_to(index, (count, H)), axis=1, independent=True)
    mixed = table[order]
    left = (2 * jax.random.randint(key_left, (count, H, 1), 0, 2) - 1).astype(jnp.float32)
    right = (2 * jax.random.randint(key_right, (count, 1, H), 0, 2) - 1).astype(jnp.float32)
    return (left * mixed * right).reshape(LAYERS, 2, 2, H, H).astype(jnp.float32)


def set_ends(values, own_key, smallest, top_value):
    dims = values.shape
    spot = [jax.random.randint(jax.random.fold_in(own_key, axis), (), 0, dims[axis]) for axis in range(len(dims))]
    values = values.at[tuple(spot)].set(smallest)
    longest = dims.index(max(dims))
    spot[longest] = (spot[longest] + 1) % dims[longest]
    return values.at[tuple(spot)].set(top_value)


def level_of(own_key, shape, shards, least, high):
    def one(dim, blocks):
        steps = jax.random.uniform(jax.random.fold_in(jax.random.fold_in(own_key, 6), dim), (blocks,), jnp.float32, least / len(shards), high / len(shards))
        return jnp.repeat(jnp.exp(steps), shape[dim] // blocks).reshape((-1,) + (1,) * (len(shape) - dim - 1))

    level = one(*shards[0])
    for cut in shards[1:]:
        level = level * one(*cut)
    return level


def normal_values(stream_key, extent, spread, most, shards=(), kind=jnp.bfloat16):
    gain = level_of(stream_key, extent, shards, -0.22, 0.18) if shards else 1.0
    array = jax.random.normal(stream_key, extent, jnp.float32) * spread * gain
    return jnp.minimum(jnp.maximum(array, -most), most).astype(kind)


def setup_inputs(seed: int = 0) -> dict:
    arg_keys = jax.random.split(jax.random.key(seed), 19)
    node_states = normal_values(arg_keys[0], (MB, NODES, H), 1.0, 6.0, ((1, 16),))
    serve = set_ends(jax.random.randint(arg_keys[1], (MB, N_ROWS * SLOTS), 0, R_DEV), jax.random.fold_in(arg_keys[1], 1), 0, R_DEV - 1).astype(jnp.int32)
    neighbors = set_ends(jax.random.randint(arg_keys[2], (MB, NODES, DEG), 0, SLOTS), jax.random.fold_in(arg_keys[2], 1), 0, SLOTS - 1).astype(jnp.int32)
    alpha = jnp.clip(jnp.exp(math.log(0.4) - 2.0794415 * jax.random.uniform(arg_keys[3], (MB, NODES, DEG), jnp.float32) ** level_of(arg_keys[3], (MB, NODES, DEG), ((1, 16),), -0.2, 0.2)), 0.05, 0.4)
    live = draw_live(jax.random.fold_in(arg_keys[18], 71), 0)
    lam = jnp.clip(jnp.exp(math.log(2.0) - 1.3862944 * jax.random.uniform(arg_keys[5], (MB, NODES), jnp.float32) ** level_of(arg_keys[5], (MB, NODES), ((1, 16),), -0.2, 0.2)), 0.5, 2.0)
    labels = set_ends(jax.random.randint(arg_keys[6], (MB, NODES), 0, C), jax.random.fold_in(arg_keys[6], 1), 0, C - 1).astype(jnp.int32)
    link_pair = set_ends(jax.random.randint(arg_keys[7], (MB, NODES), 0, SLOTS), jax.random.fold_in(arg_keys[7], 1), 0, SLOTS - 1).astype(jnp.int32)
    mats = normal_values(arg_keys[8], (LAYERS, 2, 2, H, H), H ** -0.5, 0.25, ((2, 2), (3, 16)), jnp.float32)
    mats_m = normal_values(arg_keys[9], (LAYERS, 2, 2, H, H), (0.0005 / H), 3.906250185536919e-06, ((2, 2), (3, 16)), jnp.float32)
    mats_v = jnp.clip(jnp.exp(math.log(3.814697255993815e-12) - 1.3862944 * jax.random.uniform(arg_keys[10], (LAYERS, 2, 2, H, H), jnp.float32) ** level_of(arg_keys[10], (LAYERS, 2, 2, H, H), ((2, 2), (3, 16)), -0.2, 0.2)), 9.536743139984538e-13, 3.814697255993815e-12)
    basis = draw_basis(jax.random.fold_in(arg_keys[18], 71), 0)
    bias = normal_values(arg_keys[12], (LAYERS, 2, H), 0.1, 0.6, ((1, 2), (2, 16)), jnp.float32)
    bias_m = normal_values(arg_keys[13], (LAYERS, 2, H), (0.005 / H), 3.9062499126885086e-05, ((1, 2), (2, 16)), jnp.float32)
    bias_v = jnp.clip(jnp.exp(math.log(3.8146971692576415e-10) - 1.3862944 * jax.random.uniform(arg_keys[14], (LAYERS, 2, H), jnp.float32) ** level_of(arg_keys[14], (LAYERS, 2, H), ((1, 2), (2, 16)), -0.2, 0.2)), 9.536742923144104e-11, 3.8146971692576415e-10)
    head = normal_values(arg_keys[15], (H + 1, C), H ** -0.5, 0.25, (), jnp.float32)
    head_m = normal_values(arg_keys[16], (H + 1, C), (0.005 / H), 3.9062499126885086e-05, (), jnp.float32)
    head_v = jnp.clip(jnp.exp(jax.random.uniform(arg_keys[17], (H + 1, C), jnp.float32, math.log(9.536742923144104e-11), math.log(3.8146971692576415e-10))), 9.536742923144104e-11, 3.8146971692576415e-10)
    return dict(node_states=node_states, serve=serve, neighbors=neighbors, alpha=alpha, live=live, lam=lam, labels=labels, link_pair=link_pair, mats=mats, mats_m=mats_m, mats_v=mats_v, basis=basis, bias=bias, bias_m=bias_m, bias_v=bias_v, head=head, head_m=head_m, head_v=head_v)


LINK = 4.0
CLIP = 0.001
EPSN = 1e-06
BETA = 0.5
EPSA = 1e-08
LR_MAT = 0.02
LR_BIAS = 0.05
LR_HEAD = 0.02
DECAY = 0.01
HIGH = lax.Precision.HIGHEST

@jax.custom_vjp
def low(v):
    return lax.optimization_barrier(v.astype(jnp.bfloat16)).astype(jnp.float32)

@jax.custom_vjp
def low_back(v):
    return v

def low_keep(v):
    return (low(v), None)

def low_pass(kept, grad):
    return (grad,)

def back_keep(v):
    return (v, None)

def back_low(kept, grad):
    return (low(grad),)
low.defvjp(low_keep, low_pass)
low_back.defvjp(back_keep, back_low)

def matmul(left, right):
    return jnp.dot(left.astype(jnp.float32), right.astype(jnp.float32), precision=HIGH, preferred_element_type=jnp.float32)

def slot_rows(serve_m):
    table = serve_m.reshape(N_ROWS, N_ROWS, CAP).transpose(1, 0, 2)
    owner = jnp.arange(N_ROWS, dtype=jnp.int32)[None, :, None] * R_DEV
    return (owner + table).reshape(N_ROWS * SLOTS).astype(jnp.int32)

def micro(params, states, serve_m, nbr_m, alpha_m, live_m, lam_m, label_m, pair_m):
    mats, bias, head = params
    w_low = low(mats)
    b_low = low(bias)
    head_low = low(head[:H])
    rows = slot_rows(serve_m)
    device = jnp.arange(NODES, dtype=jnp.int32) // R_DEV
    base = device * SLOTS
    x = states
    for layer in range(LAYERS):
        x_low = low(x)
        slots = low_back(x_low[rows])
        agg = jnp.zeros((NODES, H), jnp.float32)
        for k in range(DEG):
            agg = agg + alpha_m[:, k:k + 1] * slots[base + nbr_m[:, k]]
        agg = low(agg)
        h_self = low(low_back(matmul(x_low, w_low[layer, 0, 0]) + b_low[layer, 0]))
        h_nbr = low(low_back(matmul(agg, w_low[layer, 0, 1]) + b_low[layer, 1]))
        pre = low_back(matmul(h_self, w_low[layer, 1, 0]) + matmul(h_nbr, w_low[layer, 1, 1]))
        act = jax.nn.gelu(pre)
        x = act * lax.rsqrt(lax.optimization_barrier(jnp.sum(act * act, axis=1, keepdims=True)) + EPSN)
    y_low = low(x)
    logits = low_back(matmul(y_low, head_low) + head[H])
    picked = jnp.take_along_axis(logits, label_m[:, None], axis=1)[:, 0]
    cross = jax.nn.logsumexp(logits, axis=1) - picked
    link_slots = low_back(y_low[rows])
    partner = link_slots[base + pair_m]
    score = lax.optimization_barrier(jnp.sum(y_low * partner, axis=1))
    valid = jnp.arange(NODES, dtype=jnp.int32) % R_DEV < live_m[device]
    weight = jnp.where(valid, lam_m, 0.0)
    return (jnp.sum(weight * (cross + jax.nn.softplus(-LINK * score))), jnp.sum(weight))

def adamw(old, first, second, grad, rate):
    first_new = BETA * first + (1.0 - BETA) * grad
    second_new = BETA * second + (1.0 - BETA) * grad * grad
    step = first_new / (1.0 - BETA ** STEP) / (jnp.sqrt(second_new / (1.0 - BETA ** STEP)) + EPSA)
    return (old - rate * (step + DECAY * old), first_new, second_new)

def reference(node_states, serve, neighbors, alpha, live, lam, labels, link_pair, mats, mats_m, mats_v, basis, bias, bias_m, bias_v, head, head_m, head_v):

    def total(params):
        loss_sum = jnp.float32(0.0)
        for m in range(MB):
            part, _ = micro(params, node_states[m].astype(jnp.float32), serve[m], neighbors[m], alpha[m], live[m], lam[m], labels[m], link_pair[m])
            loss_sum = loss_sum + part
        return loss_sum
    loss_sum, pull = jax.vjp(total, (mats, bias, head))
    grad_mats, grad_bias, grad_head = pull(jnp.float32(1.0))[0]
    weight_sum = jnp.float32(0.0)
    for m in range(MB):
        device = jnp.arange(NODES, dtype=jnp.int32) // R_DEV
        valid = jnp.arange(NODES, dtype=jnp.int32) % R_DEV < live[m][device]
        weight_sum = weight_sum + jnp.sum(jnp.where(valid, lam[m], 0.0))
    grad_mats = grad_mats / weight_sum
    grad_bias = grad_bias / weight_sum
    grad_head = grad_head / weight_sum
    squares = jnp.sum(grad_mats * grad_mats) + jnp.sum(grad_bias * grad_bias) + jnp.sum(grad_head * grad_head)
    grad_norm = jnp.sqrt(squares)
    factor = jnp.minimum(1.0, CLIP / grad_norm)
    grad_mats = grad_mats * factor
    grad_bias = grad_bias * factor
    grad_head = grad_head * factor
    rotated = jnp.einsum('lkbij,lkbjo->lkbio', grad_mats, basis, precision=HIGH)
    first_new = BETA * mats_m + (1.0 - BETA) * rotated
    second_new = BETA * mats_v + (1.0 - BETA) * rotated * rotated
    update = first_new / (1.0 - BETA ** STEP) / (jnp.sqrt(second_new / (1.0 - BETA ** STEP)) + EPSA)
    turned = jnp.einsum('lkbio,lkbjo->lkbij', update, basis, precision=HIGH)
    mats_new = mats - LR_MAT * (turned + DECAY * mats)
    bias_new, bias_m_new, bias_v_new = adamw(bias, bias_m, bias_v, grad_bias, LR_BIAS)
    head_new, head_m_new, head_v_new = adamw(head, head_m, head_v, grad_head, LR_HEAD)
    loss_parts = jnp.stack([loss_sum, weight_sum])
    return (loss_parts, grad_norm, mats_new, mats_new.astype(jnp.bfloat16), first_new, second_new, bias_new, bias_m_new, bias_v_new, head_new, head_m_new, head_v_new)
```

```python
import jax
import jax.numpy as jnp
from jax import lax
from jax.sharding import Mesh
from jax.sharding import PartitionSpec as P

STEP = 5
LINK = 4.0
CLIP = 0.001
EPSN = 1e-06
BETA = 0.5
EPSA = 1e-08
LR_MAT = 0.02
LR_BIAS = 0.05
LR_HEAD = 0.02
DECAY = 0.01
HIGH = lax.Precision.HIGHEST
WIDE = jnp.float32
NARROW = jnp.bfloat16
GELU_A = 0.7978845608028654
GELU_B = 0.044715
SWAP = [(0, 1), (1, 0)]


def halves(value):
    top = lax.reduce_precision(value, 8, 7)
    return top.astype(NARROW), (value - top).astype(NARROW)


def mm(left, right, dims=((1,), (0,))):
    return lax.dot_general(left, right, (dims, ((), ())), preferred_element_type=WIDE)


def activate(pre):
    act = jax.nn.gelu(pre)
    return act * lax.rsqrt(jnp.sum(act * act, axis=1, keepdims=True) + EPSN)


def pad_rows(rows, unit):
    extra = -rows.shape[-2] % unit
    widths = [(0, 0)] * (rows.ndim - 2) + [(0, extra), (0, 0)]
    return jnp.pad(rows, widths)


def pad_lanes(rows, width):
    return jnp.pad(rows, [(0, 0)] * (rows.ndim - 1) + [(0, width - rows.shape[-1])])


def forward(rows_in, edges, table, w_in_self, b_self, b_nbr, w_proj_self, w_proj_nbr):
    hid_self = (mm(rows_in, w_in_self) + b_self).astype(NARROW)
    hid_nbr = (mm(edges, jnp.concatenate([table, table], 0)) + b_nbr).astype(NARROW)
    pre = mm(hid_self, w_proj_self) + mm(hid_nbr, w_proj_nbr)
    return hid_self, hid_nbr, pre, activate(pre).astype(NARROW)


def backward(d_out, pre, hid_self, hid_nbr, w_proj_self, w_proj_nbr):
    _, pull = jax.vjp(activate, pre)
    d_pre = pull(d_out)[0].astype(NARROW)
    rows = ((0,), (0,))
    g_self = mm(hid_self, d_pre, rows)
    g_nbr = mm(hid_nbr, d_pre, rows)
    d_self = mm(d_pre, w_proj_self, ((1,), (1,))).astype(NARROW)
    d_nbr = mm(d_pre, w_proj_nbr, ((1,), (1,))).astype(NARROW)
    return g_self, g_nbr, d_self, d_nbr


def adamw(old, first, second, grad, rate):
    first_new = BETA * first + (1.0 - BETA) * grad
    second_new = BETA * second + (1.0 - BETA) * grad * grad
    step = first_new / (1.0 - BETA**STEP) / (jnp.sqrt(second_new / (1.0 - BETA**STEP)) + EPSA)
    return (old - rate * (step + DECAY * old), first_new, second_new)


def local(
    far,
    near,
    node_states,
    serve,
    neighbors,
    alpha,
    live,
    lam,
    labels,
    link_pair,
    mats,
    mats_m,
    mats_v,
    basis,
    bias,
    bias_m,
    bias_v,
    head,
    head_m,
    head_v,
):
    n = far * near
    micro = lax.axis_index("branch")
    both = ("far", "near")
    rows_dev, width = node_states.shape[1:]
    classes = head.shape[1]
    depth, kinds, _, shard, _ = mats.shape
    slots = serve.shape[1]
    cap = slots // n

    def pick(value):
        return lax.dynamic_index_in_dim(value, micro, 0, keepdims=False)

    def by_branch(own, other):
        return jnp.where(micro == 0, own, other), jnp.where(micro == 0, other, own)

    states = pick(node_states)
    serve_m = pick(serve)
    nbr_m = pick(neighbors)
    alpha_m = pick(alpha)
    pair_m = pick(link_pair)
    lane = jnp.arange(slots, dtype=jnp.int32)[None, :]
    edge = jnp.zeros((rows_dev, slots), WIDE)
    for k in range(nbr_m.shape[1]):
        edge = edge + jnp.where(nbr_m[:, k : k + 1] == lane, alpha_m[:, k : k + 1], 0.0)
    edges = jnp.concatenate(halves(edge), 1)
    pairs = pair_m[:, None] == lane
    states_s = states[serve_m]
    edges_s = edges[serve_m]

    low = mats.astype(NARROW).reshape(depth * kinds * shard, width)
    low_bias = pad_lanes(bias.astype(NARROW).reshape(1, depth * shard), width)
    own_rows = depth * kinds * shard
    send = jnp.concatenate(
        [
            jnp.broadcast_to(low[None], (far,) + low.shape),
            states_s.reshape(far, near * cap, width),
            jnp.broadcast_to(pad_rows(low_bias, 16)[None], (far, 16, width)),
        ],
        1,
    )
    got = lax.all_to_all(send, "far", 0, 0, tiled=True)
    far_mats = got[:, :own_rows].reshape(far, depth, kinds * shard, width)
    far_slots = got[:, own_rows : own_rows + near * cap].reshape(far, near, cap, width)
    far_bias = got[:, own_rows + near * cap]

    def spread(rows):
        return jnp.broadcast_to(rows[None], (near,) + rows.shape)

    part = far * kinds * shard
    send = jnp.concatenate(
        [
            spread(far_mats[:, 0].reshape(part, width)),
            far_slots.transpose(1, 0, 2, 3).reshape(near, far * cap, width),
            spread(pad_rows(far_bias, 16)),
        ],
        1,
    )
    got = lax.all_to_all(send, "near", 0, 0, tiled=True)
    got_bias = got[:, part + far * cap : part + far * cap + far, : depth * shard]
    slot_rows = [
        got[:, part : part + far * cap].reshape(near, far, cap, width).transpose(1, 0, 2, 3).reshape(slots, width)
    ]
    first = got[:, :part]
    second = lax.all_to_all(spread(far_mats[:, 1].reshape(part, width)), "near", 0, 0, tiled=True)
    weights = []
    for rows in (first, second):
        own = rows.reshape(near, far, kinds, shard, width).transpose(2, 1, 0, 3, 4).reshape(kinds, width, width)
        other = lax.ppermute(own, "branch", SWAP)
        weights.append(by_branch(own, other))
    own_bias = got_bias.reshape(near, far, depth, shard).transpose(2, 1, 0, 3).reshape(depth, width)
    biases = by_branch(own_bias, lax.ppermute(own_bias, "branch", SWAP))

    kept = []
    x, xs = states, states_s
    for layer in range(depth):
        if layer:
            slot_rows.append(lax.all_to_all(xs, both, 0, 0, tiled=True))
        (self_w, nbr_w) = weights[layer]
        b_self, b_nbr = (b[layer].astype(WIDE) for b in biases)
        table = mm(slot_rows[layer], nbr_w[0]).astype(NARROW)
        args = (table, self_w[0], b_self, b_nbr, self_w[1], nbr_w[1])
        copy = forward(xs, edges_s, *args)
        full = forward(x, edges, *args)
        kept.append((x, xs, copy, full))
        xs, x = copy[3], full[3]
    link_rows = lax.all_to_all(xs, both, 0, 0, tiled=True)

    share = -(-(classes + 1) // n)
    wide_classes = share * n
    head_low = jnp.pad(head[:width].astype(NARROW), ((0, 0), (0, wide_classes - classes)))
    head_bias = jnp.pad(head[width], (0, wide_classes - classes), constant_values=-1e30)
    logits = mm(x, head_low) + head_bias
    label_m = pick(labels)
    onehot = label_m[:, None] == jnp.arange(wide_classes, dtype=jnp.int32)[None, :]
    valid = jnp.arange(rows_dev, dtype=jnp.int32) < pick(live)[0]
    weight = jnp.where(valid, pick(lam), 0.0)
    cross = jax.nn.logsumexp(logits, axis=1) - jnp.sum(jnp.where(onehot, logits, 0.0), axis=1)
    d_logits = (weight[:, None] * (jax.nn.softmax(logits, axis=1) - onehot.astype(WIDE))).astype(NARROW)
    score = jnp.sum(jnp.where(pairs, mm(x, link_rows, ((1,), (1,))), 0.0), axis=1)
    loss_sum = jnp.sum(weight * (cross + jax.nn.softplus(-LINK * score)))
    weight_sum = jnp.sum(weight)
    d_score = -LINK * weight * jax.nn.sigmoid(-LINK * score)
    d_pairs = jnp.where(pairs, d_score[:, None], 0.0).astype(NARROW)
    drive = jnp.concatenate([d_logits, d_pairs], 1)
    sums = mm(drive, x, ((0,), (0,)))
    d_link = sums[wide_classes:].astype(NARROW)
    d_bias = jnp.sum(d_logits.astype(WIDE), axis=0)[:classes]
    last = jnp.concatenate([d_bias, loss_sum[None], weight_sum[None]])
    head_rows = jnp.concatenate(
        [sums[:classes], jnp.pad(last, (0, width - last.shape[0]))[None], sums[classes + 1 : wide_classes]], 0
    )
    both_parts = jnp.concatenate([h.reshape(n, share, width) for h in halves(head_rows)], 1)
    send = jnp.concatenate([d_link.reshape(n, cap, width), pad_rows(both_parts, 8)], 1)
    got = lax.all_to_all(send, both, 0, 0, tiled=True)
    dxs = got[:, :cap].reshape(slots, width).astype(WIDE)
    mine = jnp.sum(got[:, cap : cap + 2 * share].astype(WIDE), 0)
    mine = mine[:share] + mine[share:]
    mine = mine + lax.ppermute(mine, "branch", SWAP)
    mine = pad_rows(jnp.concatenate(halves(mine), 0), 8)

    dx = mm(drive, jnp.concatenate([head_low.T, link_rows], 0))
    shards = [None] * depth
    shard_bias = [None] * depth
    rows = ((0,), (0,))
    for layer in reversed(range(depth)):
        x, xs, copy, full = kept[layer]
        (self_w, nbr_w) = weights[layer]
        g_full = backward(dx, full[2], full[0], full[1], self_w[1], nbr_w[1])
        g_copy = backward(dxs, copy[2], copy[0], copy[1], self_w[1], nbr_w[1])
        spread_back = mm(edges, g_full[3], rows) + mm(edges_s, g_copy[3], rows)
        d_table = jnp.concatenate(halves(spread_back[:slots] + spread_back[slots:]), 0)
        if layer:
            back = mm(d_table, nbr_w[0], ((1,), (1,)))
            d_slots = (back[:slots] + back[slots:]).astype(NARROW).reshape(n, cap, width)
            send = jnp.concatenate([d_slots, jnp.broadcast_to(mine[None], (n,) + mine.shape)], 1)
            got = lax.all_to_all(send, both, 0, 0, tiled=True)
            dx = mm(g_full[2], self_w[0], ((1,), (1,)))
            dxs = mm(g_copy[2], self_w[0], ((1,), (1,))) + got[:, :cap].reshape(slots, width).astype(WIDE)
            whole = got[:, cap : cap + 2 * share].astype(WIDE)
            head_sum = (whole[:, :share] + whole[:, share:]).reshape(wide_classes, width)
        twice = jnp.concatenate([slot_rows[layer]] * 2, 0)
        g_self = jnp.stack([mm(x, g_full[2], rows) + mm(xs, g_copy[2], rows), g_full[0] + g_copy[0]])
        g_nbr = jnp.stack([mm(twice, d_table, rows), g_full[1] + g_copy[1]])
        db_self = jnp.sum(g_full[2].astype(WIDE), 0) + jnp.sum(g_copy[2].astype(WIDE), 0)
        db_nbr = jnp.sum(g_full[3].astype(WIDE), 0) + jnp.sum(g_copy[3].astype(WIDE), 0)

        def pack(g, db):
            return jnp.concatenate([g.reshape(kinds * width, width), pad_rows(db[None], 16)], 0)

        own, other = by_branch(pack(g_self, db_self), pack(g_nbr, db_nbr))
        total = own + lax.ppermute(other.astype(NARROW), "branch", SWAP).astype(WIDE)
        body = total[: kinds * width].reshape(kinds, far, near, shard, width).transpose(2, 0, 1, 3, 4)
        tail = total[kinds * width].reshape(far, near, shard).transpose(1, 0, 2)
        send = jnp.concatenate(
            [body.reshape(near, kinds * far * shard, width), pad_rows(pad_lanes(tail, width), 16)], 1
        ).astype(NARROW)
        got = jnp.sum(lax.all_to_all(send, "near", 0, 0, tiled=True).astype(WIDE), 0)
        body = got[: kinds * far * shard].reshape(kinds, far, shard, width).transpose(1, 0, 2, 3)
        tail = got[kinds * far * shard : kinds * far * shard + far]
        send = jnp.concatenate(
            [body.reshape(far, kinds * shard, width), pad_rows(tail[:, None], 16)], 1
        ).astype(NARROW)
        got = jnp.sum(lax.all_to_all(send, "far", 0, 0, tiled=True).astype(WIDE), 0)
        shards[layer] = got[: kinds * shard].reshape(kinds, 1, shard, width)
        shard_bias[layer] = got[kinds * shard, :shard][None]
    sum_mats = jnp.stack(shards)
    sum_bias = jnp.stack(shard_bias)
    loss_sum = head_sum[classes, classes]
    weight_sum = head_sum[classes, classes + 1]
    sum_head = jnp.concatenate([head_sum[:classes].T, head_sum[classes : classes + 1, :classes]], 0)
    squares = jnp.sum(sum_mats * sum_mats) + jnp.sum(sum_bias * sum_bias)
    squares = lax.all_to_all(jnp.broadcast_to(squares, (2 * n, 8, 128)), both + ("branch",), 0, 0, tiled=True)
    squares = jnp.sum(squares[:, 0, 0]) + jnp.sum(sum_head * sum_head)
    grad_norm = jnp.sqrt(squares) / weight_sum
    factor = jnp.minimum(1.0, CLIP / grad_norm) / weight_sum
    rotated = jnp.einsum("lkbij,lkbjo->lkbio", sum_mats, basis, precision=HIGH) * factor
    first_new = BETA * mats_m + (1.0 - BETA) * rotated
    second_new = BETA * mats_v + (1.0 - BETA) * rotated * rotated
    update = first_new / (1.0 - BETA**STEP) / (jnp.sqrt(second_new / (1.0 - BETA**STEP)) + EPSA)
    turned = jnp.einsum("lkbio,lkbjo->lkbij", update, basis, precision=HIGH)
    mats_new = mats - LR_MAT * (turned + DECAY * mats)
    bias_new, bias_m_new, bias_v_new = adamw(bias, bias_m, bias_v, sum_bias * factor, LR_BIAS)
    head_new, head_m_new, head_v_new = adamw(head, head_m, head_v, sum_head * factor, LR_HEAD)
    return (
        jnp.stack([loss_sum, weight_sum]),
        grad_norm,
        mats_new,
        mats_new.astype(NARROW),
        first_new,
        second_new,
        bias_new,
        bias_m_new,
        bias_v_new,
        head_new,
        head_m_new,
        head_v_new,
    )


def solution(mesh):
    n = mesh.shape["rows"]
    near = 1 << (n.bit_length() // 2)
    far = n // near
    grid = Mesh(mesh.devices.reshape(far, near, 2), ("far", "near", "branch"))
    rows = ("far", "near")
    by_row = P(None, rows)
    by_row_last = P(None, rows, None)
    matrix = P(None, None, "branch", rows, None)
    vector = P(None, "branch", rows)

    def step(*arrays):
        return local(far, near, *arrays)

    return jax.shard_map(
        step,
        mesh=grid,
        in_specs=(by_row_last, by_row, by_row_last, by_row_last)
        + (by_row,) * 4
        + (matrix,) * 3
        + (P(None, None, "branch", None, None),)
        + (vector,) * 3
        + (P(),) * 3,
        out_specs=(P(), P()) + (matrix,) * 4 + (vector,) * 3 + (P(),) * 3,
        check_vma=False,
    )
```

```python
import functools

import jax
import jax.numpy as jnp
from jax import lax
from jax.experimental import pallas as pl
from jax.experimental.pallas import tpu as pltpu
from jax.sharding import Mesh
from jax.sharding import PartitionSpec as P

STEP = 5
LINK = 4.0
CLIP = 0.001
EPSN = 1e-06
BETA = 0.5
EPSA = 1e-08
LR_MAT = 0.02
LR_BIAS = 0.05
LR_HEAD = 0.02
DECAY = 0.01
HIGH = lax.Precision.HIGHEST
WIDE = jnp.float32
NARROW = jnp.bfloat16
GELU_A = 0.7978845608028654
GELU_B = 0.044715
LANES = 128
SWAP = [(0, 1), (1, 0)]


def halves(value):
    top = lax.reduce_precision(value, 8, 7)
    return top.astype(NARROW), (value - top).astype(NARROW)


def up(value, unit):
    return -(-value // unit) * unit


def pad_rows(rows, unit):
    extra = -rows.shape[-2] % unit
    return jnp.pad(rows, [(0, 0)] * (rows.ndim - 2) + [(0, extra), (0, 0)])


def split(value):
    top = value.astype(NARROW)
    return top, (value - top.astype(WIDE)).astype(NARROW)


def dot(left, right):
    return lax.dot_general(left, right, (((1,), (0,)), ((), ())), preferred_element_type=WIDE)


def dot_nt(left, right):
    return lax.dot_general(left, right, (((1,), (1,)), ((), ())), preferred_element_type=WIDE)


def dot_tn(left, right):
    return lax.dot_general(left, right, (((0,), (0,)), ((), ())), preferred_element_type=WIDE)


def unit_rows(pre):
    sq = pre * pre
    gate = 0.5 + 0.5 * jnp.tanh(pre * (GELU_A + GELU_A * GELU_B * sq))
    slope = gate * (1.0 + pre * (1.0 - gate) * (2.0 * GELU_A + 6.0 * GELU_A * GELU_B * sq))
    act = pre * gate
    inv = lax.rsqrt(jnp.sum(act * act, axis=1, keepdims=True) + EPSN)
    return (act * inv).astype(NARROW), slope * inv


def pull_rows(d_out, out, slope):
    wide = out.astype(WIDE)
    along = jnp.sum(wide * d_out, axis=1, keepdims=True)
    return (slope * (d_out - wide * along)).astype(NARROW)


def full(shape):
    return pl.BlockSpec(shape, lambda *_: (0,) * len(shape))


def when(flag, body):
    if isinstance(flag, bool):
        if flag:
            body()
    else:
        pl.when(flag)(body)


class Rows:
    def __init__(self, rows, slots):
        self.rows = rows
        self.whole = slots <= 256
        self.tile = min(rows, 512)
        self.count = rows // self.tile

    def at(self, i):
        return pl.ds(i * self.tile, self.tile)

    def down(self, ref, i):
        return ref.at[self.at(i)] if self.whole else ref

    def along(self, ref, i):
        return ref.at[:, self.at(i)] if self.whole else ref

    def under(self, ref, i):
        return ref.at[:, self.at(i)] if self.whole else ref

    def part(self, kind, ref, i):
        return ref if kind == FULL else ref.at[self.at(i)] if kind == DOWN else ref.at[:, self.at(i)]

    def spec(self, kind, shape):
        if kind == FULL:
            return full(shape)
        if kind == DOWN:
            return pl.BlockSpec((self.tile,) + shape[1:], lambda i, s: (i, 0))
        if kind == ALONG:
            return pl.BlockSpec((shape[0], self.tile), lambda i, s: (0, i))
        return pl.BlockSpec((shape[0], self.tile, shape[2]), lambda i, s: (0, i, 0))


FULL, DOWN, ALONG, UNDER = range(4)


def grid_kernel(make, walk, n_in, n_out, sel, *refs):
    i = pl.program_id(0)
    make(walk, sel, *refs)(i, i == 0, i == walk.count - 1)


def copy_kernel(make, walk, kinds, n_in, sel, *refs):
    count = len(kinds)
    far, near, rest = refs[:count], refs[count : 2 * count], refs[2 * count :]
    steps = make(walk, sel, *near, *rest[:-1])
    steps = steps if isinstance(steps, list) else [steps]
    sems = rest[-1]
    used = [0]

    def copy(k, i):
        pair = (walk.part(kinds[k], far[k], i), walk.part(kinds[k], near[k], i))
        used[0] += 1
        return pltpu.make_async_copy(*(pair if k < n_in else pair[::-1]), sems.at[used[0] - 1])

    def wanted(i, given):
        return [k for k in given if kinds[k] != FULL or i == (0 if k < n_in else walk.count - 1)]

    loads = [[copy(k, i) for k in wanted(i, range(n_in))] for i in range(walk.count)]
    for group in loads:
        for item in group:
            item.start()
    stores = []
    for n, step in enumerate(steps):
        for i in range(walk.count):
            for item in loads[i] if n == 0 else []:
                item.wait()
            step(i, i == 0, i == walk.count - 1)
            for k in wanted(i, range(n_in, count)) if n == len(steps) - 1 else []:
                stores.append(copy(k, i))
                stores[-1].start()
    for item in stores:
        item.wait()


def run(name, kernel, sel, ins, in_specs, outs, out_specs, scratch=(), flops=0, limit=20, grid=()):
    size = sum(a.size * a.dtype.itemsize for a in ins)
    size += sum(o.size * o.dtype.itemsize for o in (outs if isinstance(outs, list) else [outs]))
    return pl.pallas_call(
        kernel,
        out_shape=outs,
        grid_spec=pltpu.PrefetchScalarGridSpec(
            num_scalar_prefetch=1,
            grid=grid,
            in_specs=in_specs,
            out_specs=out_specs,
            scratch_shapes=list(scratch),
        ),
        compiler_params=pltpu.CompilerParams(
            dimension_semantics=("arbitrary",) * len(grid), vmem_limit_bytes=limit << 20
        ),
        name=name,
        cost_estimate=pl.CostEstimate(flops=flops, bytes_accessed=size, transcendentals=0),
    )(sel, *ins)


def stage(name, make, walk, sel, ins, outs, scratch=(), flops=0):
    kinds = [k for _, k in ins] + [k for *_, k in outs]
    arrays = [a for a, _ in ins]
    shapes = [shape_of(shape, dtype) for shape, dtype, _ in outs]
    n_in = len(ins)
    if not walk.whole:
        specs = [walk.spec(k, a.shape) for k, a in zip(kinds, arrays + shapes)]
        return run(
            name, functools.partial(grid_kernel, make, walk, n_in, len(outs)),
            sel, arrays, specs[:n_in], shapes, specs[n_in:], scratch, flops, 58, (walk.count,),
        )
    held = [pltpu.VMEM(a.shape, a.dtype) for a in arrays + shapes]
    copies = sum(1 if k == FULL else walk.count for k in kinds)
    hbm = pl.BlockSpec(memory_space=pltpu.HBM)
    return run(
        name, functools.partial(copy_kernel, make, walk, kinds, n_in),
        sel, arrays, [hbm] * n_in, shapes, [hbm] * len(outs),
        held + list(scratch) + [pltpu.SemaphoreType.DMA((copies,))], flops, 58,
    )


def shape_of(shape, dtype=NARROW):
    return jax.ShapeDtypeStruct(shape, dtype)


def serve_kernel(sel, states_ref, serve_ref, served_ref, held, sems):
    me = sel[0]
    part = held.shape[1]
    copies = []
    for i in range(held.shape[0]):
        copies.append(pltpu.make_async_copy(states_ref.at[me, pl.ds(i * part, part)], held.at[i], sems.at[i]))
        copies[-1].start()
    serve = serve_ref[pl.ds(me, 1)]
    row = lax.broadcasted_iota(jnp.int32, (part, serve.shape[1]), 0)
    total = None
    for i, copy in enumerate(copies):
        copy.wait()
        one = jnp.where(row == serve - i * part, 1.0, 0.0).astype(NARROW)
        value = dot_tn(one, held[i])
        total = value if total is None else total + value
    served_ref[...] = total.astype(NARROW)


def take_rows(sel, node_states, serve):
    _, rows, width = node_states.shape
    slots = serve.shape[1]
    return run(
        "serve",
        serve_kernel,
        sel,
        (node_states, serve),
        [pl.BlockSpec(memory_space=pltpu.HBM), full(serve.shape)],
        shape_of((slots, width)),
        full((slots, width)),
        [pltpu.VMEM((4, rows // 4, width), NARROW), pltpu.SemaphoreType.DMA((4,))],
        limit=12,
    )


def edge_kernel(sel, nbr_ref, alpha_ref, serve_ref, out_ref, served_ref, total):
    me = sel[0]
    slots = served_ref.shape[1]
    rows = nbr_ref.shape[2]
    tile = min(rows, 512)
    total[...] = jnp.zeros_like(total)
    lane = lax.broadcasted_iota(jnp.int32, (slots, tile), 0)
    row = lax.broadcasted_iota(jnp.int32, (tile, slots), 0)

    def step(i, carry):
        at = pl.ds(pl.multiple_of(i * tile, tile), tile)
        nbr, alpha = nbr_ref[me, :, at], alpha_ref[me, :, at]
        value = jnp.zeros((slots, tile), WIDE)
        for k in range(nbr.shape[0]):
            value = value + jnp.where(nbr[k : k + 1] == lane, alpha[k : k + 1], 0.0)
        top, rest = split(value)
        out_ref[:slots, at] = top
        out_ref[slots:, at] = rest
        one = jnp.where(row == serve_ref[pl.ds(me, 1)] - i * tile, 1.0, 0.0).astype(NARROW)
        total[...] += dot(out_ref[:, at], one)
        return carry

    lax.fori_loop(0, rows // tile, step, 0)
    served_ref[...] = total[...].astype(NARROW)


def make_edges(sel, neighbors, alpha, serve):
    _, deg, rows = neighbors.shape
    slots = serve.shape[1]
    shapes = [(2 * slots, rows), (2 * slots, slots)]
    return run(
        "edges",
        edge_kernel,
        sel,
        (neighbors, alpha, serve),
        [full(neighbors.shape), full(alpha.shape), full(serve.shape)],
        [shape_of(a) for a in shapes],
        [full(a) for a in shapes],
        [pltpu.VMEM((2 * slots, slots), WIDE)],
        limit=16 if slots <= 256 else 56,
    )


def by_place(value, me, axis):
    count = value.shape[axis]
    return jnp.concatenate(
        [lax.dynamic_slice_in_dim(value, lax.bitwise_xor(me, i), 1, axis) for i in range(count)], axis
    )


def twice(rows):
    return jnp.concatenate([rows, rows], 0)


def assemble_kernel(far, near, order, sel, *refs):
    out_ref, sems = refs[2 * near], refs[2 * near + 1]
    copies = []
    for half in range(2):
        slot = sel[0] if half == 0 else 1 - sel[0]
        for j in range(near):
            for f in range(far):
                copies.append(
                    pltpu.make_async_copy(
                        refs[half * near + j].at[f],
                        out_ref.at[slot, :, lax.bitwise_xor(sel[1], f) if order else f, lax.bitwise_xor(sel[2], j)],
                        sems.at[len(copies)],
                    )
                )
    for copy in copies:
        copy.start()
    for copy in copies:
        copy.wait()


def assemble(sel, own, other):
    near = len(own)
    far, kinds, shard, width = own[0].shape
    if shard % 16:
        own, other = (
            by_place(by_place(jnp.stack(w), sel[2], 0), sel[1], 1).transpose(2, 1, 0, 3, 4) for w in (own, other)
        )
        first = sel[0] == 0
        both = jnp.stack([jnp.where(first, own, other), jnp.where(first, other, own)])
    else:
        both = run(
            "assemble",
            functools.partial(assemble_kernel, far, near, True),
            sel,
            list(own) + list(other),
            [pl.BlockSpec(memory_space=pl.ANY)] * (2 * near),
            shape_of((2, kinds, far, near, shard, width)),
            pl.BlockSpec(memory_space=pl.ANY),
            [pltpu.SemaphoreType.DMA((2 * near * far,))],
            limit=4,
        )
    return both.reshape(2, kinds, far * near * shard, width)


def layer_rows(x, sums, w_ref, b_ref, h_ref):
    hs = (dot(x, w_ref[0, 0]) + b_ref[0:1]).astype(NARROW)
    hn = (sums + b_ref[1:2]).astype(NARROW)
    h_ref[0] = hs
    h_ref[1] = hn
    return unit_rows(dot(hs, w_ref[0, 1]) + dot(hn, w_ref[1, 1]))


def halo_step(walk, sel, x_ref, agg_ref, w_ref, b_ref, e_ref, h_ref, y_ref, m_ref, next_ref):
    def step(i, first, last):
        y, m = layer_rows(x_ref[...], dot(agg_ref[...], w_ref[1, 0]), w_ref, b_ref, h_ref)
        y_ref[...] = y
        m_ref[...] = m
        next_ref[...] = dot_tn(e_ref[...], twice(y)).astype(NARROW)

    return step


def halo_forward(sel, x, agg, weights, bias, edges_s):
    slots, width = x.shape
    walk = Rows(slots, slots)
    walk.tile, walk.count = slots, 1
    return stage(
        "halo",
        halo_step,
        walk,
        sel,
        [(a, FULL) for a in (x, agg, weights, bias, edges_s)],
        [
            ((2, slots, width), NARROW, FULL),
            ((slots, width), NARROW, FULL),
            ((slots, width), WIDE, FULL),
            ((slots, width), NARROW, FULL),
        ],
        flops=10 * slots * width * width,
    )


def forward_step(walk, sel, x_ref, e_ref, s_ref, w_ref, b_ref, *refs):
    has_head = len(refs) > 4
    if has_head:
        head_ref, hb_ref, label_ref, weight_ref, h_ref, y_ref, m_ref, dl_ref, st_ref, table = refs
    else:
        h_ref, y_ref, m_ref, table = refs

    def step(i, first, last):
        @functools.partial(when, first)
        def _():
            table[...] = twice(dot(s_ref[...], w_ref[1, 0]).astype(NARROW))
            if has_head:
                st_ref[...] = jnp.zeros_like(st_ref)

        sums = dot_tn(walk.along(e_ref, i)[...], table[...])
        y, m = layer_rows(walk.down(x_ref, i)[...], sums, w_ref, b_ref, walk.under(h_ref, i))
        walk.down(y_ref, i)[...] = y
        walk.down(m_ref, i)[...] = m
        if has_head:
            logits = dot_nt(head_ref[...], y) + hb_ref[...]
            label, weight = walk.along(label_ref, i)[...], walk.along(weight_ref, i)[...]
            hit = lax.broadcasted_iota(jnp.int32, logits.shape, 0) == label
            top = jnp.max(logits, axis=0, keepdims=True)
            power = jnp.exp(logits - top)
            total = jnp.sum(power, axis=0, keepdims=True)
            picked = jnp.sum(jnp.where(hit, logits, 0.0), axis=0, keepdims=True)
            cross = top + jnp.log(total) - picked
            dl = (power * (weight / total) - jnp.where(hit, weight, 0.0)).astype(NARROW)
            walk.along(dl_ref, i)[...] = dl
            ones = jnp.ones((8, walk.tile), NARROW)
            st_ref[0:1] += jnp.broadcast_to(jnp.sum(weight * cross, axis=1, keepdims=True), (1, LANES))
            st_ref[1:2] += dot_nt(ones, dl)[0:1]
            st_ref[2:3] += jnp.broadcast_to(jnp.sum(weight, axis=1, keepdims=True), (1, LANES))

    return step


def forward(walk, sel, x, edges, slot_rows, weights, bias, head=None):
    rows, width = x.shape
    slots = slot_rows.shape[0]
    ins = [(x, DOWN), (edges, ALONG), (slot_rows, FULL), (weights, FULL), (bias, FULL)]
    outs = [((2, rows, width), NARROW, UNDER), ((rows, width), NARROW, DOWN), ((rows, width), WIDE, DOWN)]
    if head is not None:
        ins += [(head[0], FULL), (head[1], FULL), (head[2], ALONG), (head[3], ALONG)]
        outs += [((LANES, rows), NARROW, ALONG), ((8, LANES), WIDE, FULL)]
    table = pltpu.VMEM((2 * slots, width), NARROW)
    return stage("rows_forward", forward_step, walk, sel, ins, outs, [table], 7 * rows * width * width)


def link_step(
    classes, walk, sel, x_ref, agg_ref, w_ref, b_ref, head_ref, st_ref, y_ref, dl_ref, weight_ref, pair_ref,
    d_ref, hl_ref, h_ref, dz_ref, ds_ref, dn_ref, hr_ref, slope, sums, extra,
):
    def step(i, first, last):
        @functools.partial(when, first)
        def _():
            y, m = layer_rows(x_ref[...], dot(agg_ref[...], w_ref[1, 0]), w_ref, b_ref, h_ref)
            hl_ref[:LANES] = head_ref[...]
            hl_ref[LANES:] = y
            slope[...] = m
            sums[...] = jnp.zeros_like(sums)
            extra[...] = jnp.zeros_like(extra)

        y = walk.down(y_ref, i)[...]
        near = dot_nt(hl_ref[LANES:], y)
        weight, pair = walk.along(weight_ref, i)[...], walk.along(pair_ref, i)[...]
        hit = lax.broadcasted_iota(jnp.int32, near.shape, 0) == pair
        arg = -LINK * jnp.sum(jnp.where(hit, near, 0.0), axis=0, keepdims=True)
        small = jnp.exp(-jnp.abs(arg))
        soft = jnp.maximum(arg, 0.0) + jnp.log(1.0 + small)
        sigmoid = jnp.where(arg >= 0.0, 1.0, small) / (1.0 + small)
        extra[0:1] += jnp.broadcast_to(jnp.sum(weight * soft, axis=1, keepdims=True), (1, LANES))
        d_score = -LINK * weight * sigmoid
        d_at = walk.along(d_ref, i)
        d_at[:LANES] = walk.along(dl_ref, i)[...]
        d_at[LANES:] = jnp.where(hit, d_score, 0.0).astype(NARROW)
        sums[...] += dot(d_at[...], y)

        @functools.partial(when, last)
        def _():
            dz = pull_rows(sums[LANES:], hl_ref[LANES:], slope[...])
            dz_ref[...] = dz
            ds_ref[...] = dot_nt(dz, w_ref[0, 1]).astype(NARROW)
            dn_ref[...] = dot_nt(dz, w_ref[1, 1]).astype(NARROW)
            hr_ref[...] = sums[:LANES]
            lane = lax.broadcasted_iota(jnp.int32, (1, LANES), 1)
            row = jnp.where(lane < classes, st_ref[1:2], 0.0)
            row = jnp.where(lane == classes, st_ref[0:1] + extra[0:1], row)
            row = jnp.where(lane == classes + 1, st_ref[2:3], row)
            hr_ref[classes : classes + 1, :LANES] = row

    return step


def link(walk, sel, classes, x, agg, weights, bias, head_t, stats, y, d_logits, weight, pair):
    slots, width = x.shape
    rows = y.shape[0]
    ins = [(a, FULL) for a in (x, agg, weights, bias, head_t, stats)]
    ins += [(y, DOWN), (d_logits, ALONG), (weight, ALONG), (pair, ALONG)]
    outs = [((LANES + slots, rows), NARROW, ALONG), ((LANES + slots, width), NARROW, FULL)]
    outs += [((2, slots, width), NARROW, FULL)] + [((slots, width), NARROW, FULL)] * 3
    outs += [((LANES, width), WIDE, FULL)]
    scratch = [
        pltpu.VMEM((slots, width), WIDE),
        pltpu.VMEM((LANES + slots, width), WIDE),
        pltpu.VMEM((8, LANES), WIDE),
    ]
    flops = 6 * rows * slots * width + 12 * slots * width * width
    return stage("link", functools.partial(link_step, classes), walk, sel, ins, outs, scratch, flops)


def add_sums(sums, dz, h, x, edges, w_ref):
    acc, bias_acc, spread_acc = sums
    acc[0, 1] += dot_tn(h[0], dz)
    acc[1, 1] += dot_tn(h[1], dz)
    ds = dot_nt(dz, w_ref[0, 1]).astype(NARROW)
    dn = dot_nt(dz, w_ref[1, 1]).astype(NARROW)
    acc[0, 0] += dot_tn(x, ds)
    spread_acc[...] += dot(edges, dn)
    bias_acc[0:1] += jnp.sum(ds.astype(WIDE), axis=0, keepdims=True)
    bias_acc[1:2] += jnp.sum(dn.astype(WIDE), axis=0, keepdims=True)
    return ds


def start_sums(sums, dz, h_ref, x, agg, ds, dn):
    acc, bias_acc, spread_acc = sums
    acc[0, 1] = dot_tn(h_ref[0], dz)
    acc[1, 1] = dot_tn(h_ref[1], dz)
    acc[0, 0] = dot_tn(x, ds)
    acc[1, 0] = dot_tn(agg, dn)
    spread_acc[...] = jnp.zeros_like(spread_acc)
    bias_acc[...] = jnp.zeros_like(bias_acc)
    bias_acc[0:1] = jnp.sum(ds.astype(WIDE), axis=0, keepdims=True)
    bias_acc[1:2] = jnp.sum(dn.astype(WIDE), axis=0, keepdims=True)


def finish_sums(me, sums, table, own_ref, other_ref, bo_ref, bx_ref):
    acc, bias_acc, spread_acc = sums
    slots = table.shape[0]
    spread = spread_acc[:slots] + spread_acc[slots:]
    top, rest = split(spread)
    acc[1, 0] += dot_tn(table, top) + dot_tn(table, rest)
    own_ref[...] = acc[me].astype(NARROW)
    other_ref[...] = acc[1 - me].astype(NARROW)
    bo_ref[...] = jnp.broadcast_to(bias_acc[pl.ds(me, 1)], bo_ref.shape)
    bx_ref[...] = jnp.broadcast_to(bias_acc[pl.ds(1 - me, 1)], bx_ref.shape)
    return spread


def back_last_step(
    walk, sel, y_ref, m_ref, x_ref, d_ref, e_ref, h_ref,
    hl_ref, w_ref, hh_ref, xh_ref, gh_ref, dzh_ref, dsh_ref, dnh_ref,
    own_ref, other_ref, bo_ref, bx_ref, dx_ref, sp_ref, *sums,
):
    def step(i, first, last):
        @functools.partial(when, first)
        def _():
            start_sums(sums, dzh_ref[...], hh_ref, xh_ref[...], gh_ref[...], dsh_ref[...], dnh_ref[...])

        d_out = dot_tn(walk.along(d_ref, i)[...], hl_ref[...])
        dz = pull_rows(d_out, walk.down(y_ref, i)[...], walk.down(m_ref, i)[...])
        ds = add_sums(
            sums, dz, walk.under(h_ref, i), walk.down(x_ref, i)[...], walk.along(e_ref, i)[...], w_ref
        )
        walk.down(dx_ref, i)[...] = dot_nt(ds, w_ref[0, 0])

        @functools.partial(when, last)
        def _():
            sp_ref[...] = finish_sums(sel[0], sums, xh_ref[...], own_ref, other_ref, bo_ref, bx_ref)

    return step


def back_first_step(
    walk, sel, y_ref, m_ref, x_ref, dx_ref, e_ref, h_ref,
    w_ref, hh_ref, xh_ref, gh_ref, up_ref, sp_ref, es_ref, ret_ref, dsh_ref, yh_ref, mh_ref,
    own_ref, other_ref, bo_ref, bx_ref, *sums,
):
    def step(i, first, last):
        @functools.partial(when, first)
        def _():
            slots = yh_ref.shape[0]
            back = dot(es_ref[...], ret_ref[...])
            top, rest = split(sp_ref[...] + back[:slots] + back[slots:])
            d_out = dot_nt(top, up_ref[1, 0]) + dot_nt(rest, up_ref[1, 0]) + dot_nt(dsh_ref[...], up_ref[0, 0])
            dz = pull_rows(d_out, yh_ref[...], mh_ref[...])
            ds = dot_nt(dz, w_ref[0, 1]).astype(NARROW)
            dn = dot_nt(dz, w_ref[1, 1]).astype(NARROW)
            start_sums(sums, dz, hh_ref, xh_ref[...], gh_ref[...], ds, dn)

        dz = pull_rows(walk.down(dx_ref, i)[...], walk.down(y_ref, i)[...], walk.down(m_ref, i)[...])
        add_sums(sums, dz, walk.under(h_ref, i), walk.down(x_ref, i)[...], walk.along(e_ref, i)[...], w_ref)

        @functools.partial(when, last)
        def _():
            finish_sums(sel[0], sums, xh_ref[...], own_ref, other_ref, bo_ref, bx_ref)

    return step


def sums_scratch(kinds, slots, width):
    return [
        pltpu.VMEM((2, kinds, width, width), WIDE),
        pltpu.VMEM((8, width), WIDE),
        pltpu.VMEM((2 * slots, width), WIDE),
    ]


def last_steps(
    classes, walk, sel, x_ref, e_ref, s_ref, w_ref, b_ref, head_ref, hb_ref, label_ref, weight_ref, pair_ref, agg_ref,
    own_ref, other_ref, bo_ref, bx_ref, dx_ref, sp_ref, ds_ref, dn_ref, hr_ref,
    table, h_ref, y_ref, m_ref, dl_ref, st_ref, d_ref, hl_ref, hh_ref, dz_ref, slope, sums, extra, *acc,
):
    return [
        forward_step(
            walk, sel, x_ref, e_ref, s_ref, w_ref, b_ref, head_ref, hb_ref, label_ref, weight_ref,
            h_ref, y_ref, m_ref, dl_ref, st_ref, table,
        ),
        link_step(
            classes, walk, sel, s_ref, agg_ref, w_ref, b_ref, head_ref, st_ref, y_ref, dl_ref, weight_ref, pair_ref,
            d_ref, hl_ref, hh_ref, dz_ref, ds_ref, dn_ref, hr_ref, slope, sums, extra,
        ),
        back_last_step(
            walk, sel, y_ref, m_ref, x_ref, d_ref, e_ref, h_ref,
            hl_ref, w_ref, hh_ref, s_ref, agg_ref, dz_ref, ds_ref, dn_ref,
            own_ref, other_ref, bo_ref, bx_ref, dx_ref, sp_ref, *acc,
        ),
    ]


def last_layer(walk, sel, classes, x, edges, slot_rows, weights, bias, head, pair, agg):
    rows, width = x.shape
    slots = slot_rows.shape[0]
    kinds = weights.shape[1]
    if not walk.whole:
        hidden, y, m, d_logits, stats = forward(walk, sel, x, edges, slot_rows, weights, bias, head)
        drive, drive_rows, hidden_h, dz_h, ds_h, dn_h, head_rows = link(
            walk, sel, classes, slot_rows, agg, weights, bias, head[0], stats, y, d_logits, head[3], pair
        )
        grads = backward(
            back_last_step, walk, sel, [y, m, x], drive, edges, hidden,
            [drive_rows, weights, hidden_h, slot_rows, agg, dz_h, ds_h, dn_h], slots, True,
        )
        return list(grads) + [ds_h, dn_h, head_rows]
    ins = [(x, DOWN), (edges, ALONG), (slot_rows, FULL), (weights, FULL), (bias, FULL), (head[0], FULL)]
    ins += [(head[1], FULL), (head[2], ALONG), (head[3], ALONG), (pair, ALONG), (agg, FULL)]
    outs = [((kinds, width, width), NARROW, FULL)] * 2 + [((8, width), WIDE, FULL)] * 2
    outs += [((rows, width), WIDE, DOWN), ((slots, width), WIDE, FULL)]
    outs += [((slots, width), NARROW, FULL)] * 2 + [((LANES, width), WIDE, FULL)]
    scratch = [
        pltpu.VMEM((2 * slots, width), NARROW),
        pltpu.VMEM((2, rows, width), NARROW),
        pltpu.VMEM((rows, width), NARROW),
        pltpu.VMEM((rows, width), WIDE),
        pltpu.VMEM((LANES, rows), NARROW),
        pltpu.VMEM((8, LANES), WIDE),
        pltpu.VMEM((LANES + slots, rows), NARROW),
        pltpu.VMEM((LANES + slots, width), NARROW),
        pltpu.VMEM((2, slots, width), NARROW),
        pltpu.VMEM((slots, width), NARROW),
        pltpu.VMEM((slots, width), WIDE),
        pltpu.VMEM((LANES + slots, width), WIDE),
        pltpu.VMEM((8, LANES), WIDE),
    ] + sums_scratch(kinds, slots, width)
    return stage("last_layer", functools.partial(last_steps, classes), walk, sel, ins, outs, scratch, 22 * rows * width * width)


def backward(make, walk, sel, rowed, drive, edges, hidden, halo, slots, is_last):
    rows, width = rowed[0].shape
    kinds = hidden.shape[0]
    outs = [((kinds, width, width), NARROW, FULL)] * 2 + [((8, width), WIDE, FULL)] * 2
    if is_last:
        outs += [((rows, width), WIDE, DOWN), ((slots, width), WIDE, FULL)]
    ins = [(a, DOWN) for a in rowed] + [(drive, ALONG if is_last else DOWN), (edges, ALONG), (hidden, UNDER)]
    ins += [(a, FULL) for a in halo]
    scratch = sums_scratch(kinds, slots, width)
    return stage("rows_backward", make, walk, sel, ins, outs, scratch, (13 if is_last else 11) * rows * width * width)


def extras(count):
    return up(2 * count + 2, 16)


def put_pairs(extra, pieces):
    extra[...] = jnp.zeros_like(extra)
    at = 0
    for piece in pieces:
        top = piece.astype(NARROW).astype(WIDE)
        count = piece.shape[0]
        extra[at : at + count] = top
        extra[at + count : at + 2 * count] = piece - top
        at += 2 * count


def pack_kernel(has_rows, sel, own_ref, got_ref, bo_ref, bg_ref, *refs):
    rows_ref, refs = (refs[0], refs[1:]) if has_rows else (None, refs)
    extra, outs = refs[-1], refs[:-1]
    kinds, far, _, shard, _ = own_ref.shape
    for j, out_ref in enumerate(outs):
        place = lax.bitwise_xor(sel[2], j)
        for f in range(far):
            for k in range(kinds):
                value = own_ref[k, f, place].astype(WIDE) + got_ref[k, f, place].astype(WIDE)
                at = (f * kinds + k) * shard
                out_ref[at : at + shard] = value.astype(NARROW)
        bias = bo_ref[0:1] + bg_ref[0:1]
        put_pairs(extra, [bias] if rows_ref is None else [rows_ref[place], bias])
        out_ref[far * kinds * shard :] = extra[...].astype(NARROW)


def pack(sel, far, near, own, got, bias_own, bias_got, head_rows=None):
    kinds, width, _ = own.shape
    shard = width // (far * near)
    count = 0 if head_rows is None else head_rows.shape[1]
    body = far * kinds * shard
    shape = (kinds, far, near, shard, width)
    if shard % 16:
        total = (own.astype(WIDE) + got.astype(WIDE)).reshape(shape).transpose(2, 1, 0, 3, 4).reshape(near, body, width)
        bias = bias_own[0:1] + bias_got[0:1]
        pieces = [total.astype(NARROW)]
        if count:
            pieces += list(halves(head_rows))
        pieces += [jnp.broadcast_to(h[None], (near, 1, width)) for h in halves(bias)]
        out = pad_rows(jnp.concatenate(pieces, 1), 16)
        out = by_place(out, sel[2], 0)
        return [out[j] for j in range(near)]
    ins = [own.reshape(shape), got.reshape(shape), bias_own, bias_got]
    if count:
        ins.append(head_rows)
    total = body + extras(count)
    return run(
        "pack",
        functools.partial(pack_kernel, count > 0),
        sel,
        ins,
        [full(a.shape) for a in ins],
        [shape_of((total, width))] * near,
        [full((total, width))] * near,
        [pltpu.VMEM((extras(count), width), WIDE)],
        limit=16,
    )


def middle_kernel(far, body, share, near, sel, *refs):
    out_ref, total, extra = refs[near:]
    value = refs[0][...].astype(WIDE)
    for ref in refs[1:near]:
        value = value + ref[...].astype(WIDE)
    total[...] = value
    count = far * share
    at = far * body
    bias = total[at + 2 * count : at + 2 * count + 1] + total[at + 2 * count + 1 : at + 2 * count + 2]
    for f in range(far):
        out_ref[f, :body] = total[f * body : (f + 1) * body].astype(NARROW)
        pieces = [bias]
        if share:
            low = at + f * share
            pieces = [total[low : low + share] + total[low + count : low + count + share], bias]
        put_pairs(extra, pieces)
        out_ref[f, body:] = extra[...].astype(NARROW)


def middle(sel, far, share, got):
    rows, width = got[0].shape
    near = len(got)
    count = far * share
    body = (rows - extras(count)) // far
    if body % 16:
        total = sum(g.astype(WIDE) for g in got)
        at = far * body
        pieces = [total[:at].reshape(far, body, width).astype(NARROW)]
        if share:
            value = total[at : at + count] + total[at + count : at + 2 * count]
            pieces += list(halves(value.reshape(far, share, width)))
        bias = total[at + 2 * count : at + 2 * count + 1] + total[at + 2 * count + 1 : at + 2 * count + 2]
        pieces += [jnp.broadcast_to(h[None], (far, 1, width)) for h in halves(bias)]
        out = jnp.concatenate(pieces, 1)
        return jnp.pad(out, ((0, 0), (0, body + extras(share) - out.shape[1]), (0, 0)))
    return run(
        "middle",
        functools.partial(middle_kernel, far, body, share, near),
        sel,
        list(got),
        [full(got[0].shape)] * near,
        shape_of((far, body + extras(share), width)),
        full((far, body + extras(share), width)),
        [pltpu.VMEM((rows, width), WIDE), pltpu.VMEM((extras(share), width), WIDE)],
        limit=16,
    )


def adamw(old, first, second, grad, rate):
    first_new = BETA * first + (1.0 - BETA) * grad
    second_new = BETA * second + (1.0 - BETA) * grad * grad
    step = first_new / (1.0 - BETA**STEP) / (jnp.sqrt(second_new / (1.0 - BETA**STEP)) + EPSA)
    return (old - rate * (step + DECAY * old), first_new, second_new)


def local(
    far,
    near,
    node_states,
    serve,
    neighbors,
    alpha,
    live,
    lam,
    labels,
    link_pair,
    mats,
    mats_m,
    mats_v,
    basis,
    bias,
    bias_m,
    bias_v,
    head,
    head_m,
    head_v,
):
    n = far * near
    branch = lax.axis_index("branch")
    both = ("far", "near")
    rows_dev, width = node_states.shape[1:]
    classes = head.shape[1]
    depth, kinds, _, shard, _ = mats.shape
    slots = serve.shape[1]
    cap = slots // n
    walk = Rows(rows_dev, slots)

    def pick(value):
        return lax.dynamic_index_in_dim(value, branch, 0, keepdims=False)

    def swap(value):
        return lax.ppermute(value, "branch", SWAP)

    def exchange(value, axes):
        return lax.all_to_all(value, axes, 0, 0, tiled=True)

    def hop(value, axis, size, k):
        return lax.ppermute(value, axis, [(i, i ^ k) for i in range(size)]) if k else value

    def spread(rows, count):
        return jnp.broadcast_to(rows[None], (count,) + rows.shape)

    places = (branch, lax.axis_index("far"), lax.axis_index("near"))
    sel = jnp.stack([p.astype(jnp.int32) for p in places])

    low = mats.astype(NARROW).reshape(depth, kinds, shard, width)

    def along_far(part):
        return jnp.stack([hop(part, "far", far, k) for k in range(far)])

    def along_near(pieces):
        return [hop(pieces, "near", near, k) for k in range(near)]

    def join(own):
        return assemble(sel, own, [swap(piece) for piece in own])

    far_0 = along_far(low[0])

    states_s = take_rows(sel, node_states, serve)
    low_bias = jnp.pad(bias.astype(NARROW).reshape(1, depth * shard), ((0, 7), (0, width - depth * shard)))
    send = jnp.concatenate([states_s.reshape(n, cap, width), spread(low_bias, n)], 1)
    got = exchange(send, both)
    serve, branch, far_0 = lax.optimization_barrier((serve, branch, far_0))
    near_0 = along_near(far_0)
    edges, edges_s = make_edges(sel, neighbors.transpose(0, 2, 1), alpha.transpose(0, 2, 1), serve)
    slots_0 = got[:, :cap].reshape(slots, width)
    own_bias = got[:, cap, : depth * shard].reshape(n, depth, shard).transpose(1, 0, 2).reshape(depth, width)
    other_bias = swap(own_bias)
    first = branch == 0
    biases = jnp.stack([jnp.where(first, own_bias, other_bias), jnp.where(first, other_bias, own_bias)], 1)
    biases = biases.astype(WIDE)
    x_0 = pick(node_states)
    agg = lax.dot_general(edges_s, twice(slots_0), (((0,), (0,)), ((), ())), preferred_element_type=WIDE)
    agg_0 = exchange(agg.astype(NARROW), both)

    part, edges_s = lax.optimization_barrier((low[1], edges_s))
    far_1, near_0 = lax.optimization_barrier((along_far(part), near_0))
    weights = [join(near_0)]
    near_1 = along_near(far_1)

    share = -(-(classes + 1) // n)
    head_t = jnp.pad(head[:width].astype(NARROW).T, ((0, LANES - classes), (0, 0)))
    head_bias = jnp.pad(head[width][:, None], ((0, LANES - classes), (0, 0)), constant_values=-1e30)
    weight = jnp.where(jnp.arange(rows_dev, dtype=jnp.int32) < pick(live)[0], pick(lam), 0.0)[None]

    h_h0, slots_1, m_h0, agg = halo_forward(sel, slots_0, agg_0, weights[0], biases[0], edges_s)
    agg, x_0 = lax.optimization_barrier((agg, x_0))
    agg_1 = exchange(agg, both)
    h_0, x_1, m_0 = forward(walk, sel, x_0, edges, slots_0, weights[0], biases[0])
    near_1, x_1 = lax.optimization_barrier((near_1, x_1))
    weights.append(join(near_1))
    own_1, other_1, bias_1, bias_x1, d_x, spread_1, ds_h1, dn_h1, head_rows = last_layer(
        walk, sel, classes, x_1, edges, slots_1, weights[1], biases[1],
        (head_t, head_bias, pick(labels)[None], weight), pick(link_pair)[None], agg_1,
    )
    returned = exchange(dn_h1, both)

    head_rows = head_rows[: n * share].reshape(near, far * share, width)
    packed = pack(sel, far, near, own_1, swap(other_1), bias_1, swap(bias_x1), head_rows)
    *packed, spread_1 = lax.optimization_barrier((*packed, spread_1))
    sums_1 = [hop(piece, "near", near, k) for k, piece in enumerate(packed)]
    own_0, other_0, bias_0, bias_x0 = backward(
        back_first_step, walk, sel, [x_1, m_0, x_0], d_x, edges, h_0,
        [weights[0], h_h0, slots_0, agg_0, weights[1], spread_1, edges_s, returned, ds_h1, slots_1, m_h0],
        slots, False,
    )
    own_0, other_0, bias_x0, sums_1 = lax.optimization_barrier((own_0, other_0, bias_x0, sums_1))
    packed = pack(sel, far, near, own_0, swap(other_0), bias_0, swap(bias_x0))
    sums_0 = [hop(piece, "near", near, k) for k, piece in enumerate(packed)]
    sums_1 = jnp.sum(exchange(middle(sel, far, share, sums_1), "far").astype(WIDE), 0)
    sums_0 = jnp.sum(exchange(middle(sel, far, 0, sums_0), "far").astype(WIDE), 0)
    body = kinds * shard
    mine = sums_1[body : body + share] + sums_1[body + share : body + 2 * share]

    at = body + 2 * share
    bias_sums = jnp.stack([sums_0[body] + sums_0[body + 1], sums_1[at] + sums_1[at + 1]])
    place = (lax.axis_index("far") * near + lax.axis_index("near")) * shard
    sum_bias = lax.dynamic_slice_in_dim(bias_sums, place, shard, 1)[:, None]
    sum_mats = jnp.stack([sums_0[:body], sums_1[:body]]).reshape(depth, kinds, 1, shard, width)
    squares = jnp.sum(sum_mats * sum_mats) + jnp.sum(sum_bias * sum_bias)
    parts = []
    for _ in range(3):
        parts.append(lax.reduce_precision(squares, 8, 7))
        squares = squares - parts[-1]
    row = jnp.pad(jnp.stack(parts)[None], ((0, 0), (0, width - 3))).astype(NARROW)
    send = pad_rows(jnp.concatenate(list(halves(mine)) + [row], 0), 8)
    whole = exchange(spread(send, 2 * n), both + ("branch",)).astype(WIDE)
    head_sum = jnp.sum((whole[:, :share] + whole[:, share : 2 * share]).reshape(far, near, 2, share, width), 2)
    head_sum = head_sum.transpose(1, 0, 2, 3).reshape(n * share, width)
    loss_sum = head_sum[classes, classes]
    weight_sum = head_sum[classes, classes + 1]
    sum_head = jnp.concatenate([head_sum[:classes].T, head_sum[classes : classes + 1, :classes]], 0)
    squares = jnp.sum(whole[:, 2 * share, :3]) + jnp.sum(sum_head * sum_head)
    grad_norm = jnp.sqrt(squares) / weight_sum
    factor = jnp.minimum(1.0, CLIP / grad_norm) / weight_sum
    rotated = jnp.einsum("lkbij,lkbjo->lkbio", sum_mats, basis, precision=HIGH) * factor
    first_new = BETA * mats_m + (1.0 - BETA) * rotated
    second_new = BETA * mats_v + (1.0 - BETA) * rotated * rotated
    update = first_new / (1.0 - BETA**STEP) / (jnp.sqrt(second_new / (1.0 - BETA**STEP)) + EPSA)
    turned = jnp.einsum("lkbio,lkbjo->lkbij", update, basis, precision=HIGH)
    mats_new = mats - LR_MAT * (turned + DECAY * mats)
    bias_new, bias_m_new, bias_v_new = adamw(bias, bias_m, bias_v, sum_bias * factor, LR_BIAS)
    head_new, head_m_new, head_v_new = adamw(head, head_m, head_v, sum_head * factor, LR_HEAD)
    return (
        jnp.stack([loss_sum, weight_sum]),
        grad_norm,
        mats_new,
        mats_new.astype(NARROW),
        first_new,
        second_new,
        bias_new,
        bias_m_new,
        bias_v_new,
        head_new,
        head_m_new,
        head_v_new,
    )


def solution(mesh):
    n = mesh.shape["rows"]
    near = 1 << (n.bit_length() // 2)
    far = n // near
    grid = Mesh(mesh.devices.reshape(far, near, 2), ("far", "near", "branch"))
    rows = ("far", "near")
    by_row = P(None, rows)
    by_row_last = P(None, rows, None)
    matrix = P(None, None, "branch", rows, None)
    vector = P(None, "branch", rows)
    return jax.shard_map(
        functools.partial(local, far, near),
        mesh=grid,
        in_specs=(by_row_last, by_row, by_row_last, by_row_last)
        + (by_row,) * 4
        + (matrix,) * 3
        + (P(None, None, "branch", None, None),)
        + (vector,) * 3
        + (P(),) * 3,
        out_specs=(P(), P()) + (matrix,) * 4 + (vector,) * 3 + (P(),) * 3,
        check_vma=False,
    )
```

```python
import functools

import jax
import jax.numpy as jnp
from jax import lax
from jax.experimental import pallas as pl
from jax.experimental.pallas import tpu as pltpu
from jax.sharding import Mesh
from jax.sharding import PartitionSpec as P

STEP = 5
LINK = 4.0
CLIP = 0.001
EPSN = 1e-06
BETA = 0.5
EPSA = 1e-08
LR_MAT = 0.02
LR_BIAS = 0.05
LR_HEAD = 0.02
DECAY = 0.01
HIGH = lax.Precision.HIGHEST
WIDE = jnp.float32
NARROW = jnp.bfloat16
GELU_A = 0.7978845608028654
GELU_B = 0.044715
LANES = 128
SWAP = [(0, 1), (1, 0)]


def halves(value):
    top = lax.reduce_precision(value, 8, 7)
    return top.astype(NARROW), (value - top).astype(NARROW)


def up(value, unit):
    return -(-value // unit) * unit


def pad_rows(rows, unit):
    extra = -rows.shape[-2] % unit
    return jnp.pad(rows, [(0, 0)] * (rows.ndim - 2) + [(0, extra), (0, 0)])


def split(value):
    top = value.astype(NARROW)
    return top, (value - top.astype(WIDE)).astype(NARROW)


def dot(left, right):
    return lax.dot_general(left, right, (((1,), (0,)), ((), ())), preferred_element_type=WIDE)


def dot_nt(left, right):
    return lax.dot_general(left, right, (((1,), (1,)), ((), ())), preferred_element_type=WIDE)


def dot_tn(left, right):
    return lax.dot_general(left, right, (((0,), (0,)), ((), ())), preferred_element_type=WIDE)


def unit_rows(pre):
    sq = pre * pre
    gate = 0.5 + 0.5 * jnp.tanh(pre * (GELU_A + GELU_A * GELU_B * sq))
    slope = gate * (1.0 + pre * (1.0 - gate) * (2.0 * GELU_A + 6.0 * GELU_A * GELU_B * sq))
    act = pre * gate
    inv = lax.rsqrt(jnp.sum(act * act, axis=1, keepdims=True) + EPSN)
    return (act * inv).astype(NARROW), slope * inv


def pull_rows(d_out, out, slope):
    wide = out.astype(WIDE)
    along = jnp.sum(wide * d_out, axis=1, keepdims=True)
    return (slope.astype(WIDE) * (d_out - wide * along)).astype(NARROW)


def full(shape):
    return pl.BlockSpec(shape, lambda *_: (0,) * len(shape))


def when(flag, body):
    if isinstance(flag, bool):
        if flag:
            body()
    else:
        pl.when(flag)(body)


class Rows:
    def __init__(self, rows, slots):
        self.rows = rows
        self.whole = slots <= 256
        self.tile = min(rows, 512)
        self.count = rows // self.tile

    def at(self, i):
        return pl.ds(i * self.tile, self.tile)

    def down(self, ref, i):
        return ref.at[self.at(i)] if self.whole else ref

    def along(self, ref, i):
        return ref.at[:, self.at(i)] if self.whole else ref

    def under(self, ref, i):
        return ref.at[:, self.at(i)] if self.whole else ref

    def part(self, kind, ref, i):
        return ref if kind in ONCE else ref.at[self.at(i)] if kind in (DOWN, PICK) else ref.at[:, self.at(i)]

    def source(self, kind, ref, i, sel):
        return ref.at[:, 0] if kind == LEAD else self.part(kind, ref.at[sel[0]] if kind == PICK else ref, i)

    def held(self, kind, shape):
        return shape[1:] if kind == PICK else shape[:1] + shape[2:] if kind == LEAD else shape

    def spec(self, kind, shape):
        if kind == FULL:
            return full(shape)
        if kind == LEAD:
            return pl.BlockSpec((shape[0], None) + shape[2:], lambda *_: (0,) * len(shape))
        if kind == PICK:
            return pl.BlockSpec((None, self.tile, shape[2]), lambda i, s: (s[0], i, 0))
        if kind == DOWN:
            return pl.BlockSpec((self.tile,) + shape[1:], lambda i, s: (i, 0))
        if kind == ALONG:
            return pl.BlockSpec((shape[0], self.tile), lambda i, s: (0, i))
        return pl.BlockSpec((shape[0], self.tile, shape[2]), lambda i, s: (0, i, 0))


FULL, DOWN, ALONG, UNDER, PICK, LEAD, PIECES, AGAIN = range(8)
ONCE = (FULL, LEAD, PIECES, AGAIN)


def grid_kernel(make, walk, n_in, n_out, sel, *refs):
    i = pl.program_id(0)
    make(walk, sel, *refs)(i, i == 0, i == walk.count - 1)


def piece_copies(sel, refs, out_ref):
    near = len(refs) // 2
    far, kinds, shard, _ = refs[0].shape
    pairs = []
    for half in range(2):
        slot = sel[0] if half == 0 else 1 - sel[0]
        for j in range(near):
            for f in range(far):
                place = lax.bitwise_xor(sel[1], f) * near + lax.bitwise_xor(sel[2], j)
                at = pl.ds(pl.multiple_of(place * shard, shard), shard)
                pairs += [(refs[half * near + j].at[f, k], out_ref.at[slot, k, at]) for k in range(kinds)]
    return pairs


def copy_kernel(make, walk, kinds, sizes, n_in, sel, *refs):
    count = len(kinds)
    far, at = [], 0
    for size in sizes:
        far.append(refs[at : at + size])
        at += size
    held = [k for k in range(count) if kinds[k] != AGAIN]
    near = dict(zip(held, refs[at : at + len(held)]))
    steps = make(walk, sel, *near.values(), *refs[at + len(held) : -1])
    steps = steps if isinstance(steps, list) else [steps]
    sems = refs[-1]
    used = [0]

    def copies(k, i):
        kind = kinds[k]
        if kind == PIECES:
            pairs = piece_copies(sel, far[k], near[k])
        elif kind == AGAIN:
            pairs = [(near[kinds.index(PIECES)], far[k][0])]
        else:
            pair = (walk.source(kind, far[k][0], i, sel), walk.part(kind, near[k], i))
            pairs = [pair if k < n_in else pair[::-1]]
        used[0] += len(pairs)
        return [
            pltpu.make_async_copy(*pair, sems.at[used[0] - len(pairs) + n]) for n, pair in enumerate(pairs)
        ]

    def wanted(i, given):
        chosen = []
        for k in given:
            if kinds[k] not in ONCE or i == (0 if k < n_in else walk.count - 1):
                chosen += copies(k, i)
        return chosen

    loads = [wanted(i, range(n_in)) for i in range(walk.count)]
    ahead = 2
    for group in loads[:ahead]:
        for item in group:
            item.start()
    stores = []
    results = [k for k in range(n_in, count) if kinds[k] != AGAIN]
    for n, step in enumerate(steps):
        for i in range(walk.count):
            for item in loads[i] if n == 0 else []:
                item.wait()
            for item in loads[i + ahead] if n == 0 and i + ahead < walk.count else []:
                item.start()
            if n == 0 and i == 0:
                stores = [item for k in range(n_in, count) if kinds[k] == AGAIN for item in copies(k, i)]
                for item in stores:
                    item.start()
            step(i, i == 0, i == walk.count - 1)
            for item in wanted(i, results) if n == len(steps) - 1 else []:
                item.start()
                stores.append(item)
    for item in stores:
        item.wait()


def run(name, kernel, sel, ins, in_specs, outs, out_specs, scratch=(), flops=0, limit=20, grid=()):
    size = sum(a.size * a.dtype.itemsize for a in ins)
    size += sum(o.size * o.dtype.itemsize for o in (outs if isinstance(outs, list) else [outs]))
    return pl.pallas_call(
        kernel,
        out_shape=outs,
        grid_spec=pltpu.PrefetchScalarGridSpec(
            num_scalar_prefetch=1,
            grid=grid,
            in_specs=in_specs,
            out_specs=out_specs,
            scratch_shapes=list(scratch),
        ),
        compiler_params=pltpu.CompilerParams(
            dimension_semantics=("arbitrary",) * len(grid), vmem_limit_bytes=limit << 20
        ),
        name=name,
        cost_estimate=pl.CostEstimate(flops=flops, bytes_accessed=size, transcendentals=0),
    )(sel, *ins)


def stage(name, make, walk, sel, ins, outs, scratch=(), flops=0):
    kinds = [k for _, k in ins] + [k for *_, k in outs]
    groups = [a if isinstance(a, list) else [a] for a, _ in ins]
    arrays = [a for group in groups for a in group]
    shapes = [shape_of(shape, dtype) for shape, dtype, _ in outs]
    n_in = len(ins)
    if not walk.whole:
        specs = [walk.spec(k, a.shape) for k, a in zip(kinds, arrays + shapes)]
        return run(
            name, functools.partial(grid_kernel, make, walk, n_in, len(outs)),
            sel, arrays, specs[:n_in], shapes, specs[n_in:], scratch, flops, 58, (walk.count,),
        )
    held, copies = [], 0
    for kind, group in zip(kinds, groups + [[a] for a in shapes]):
        shape = group[0].shape
        if kind == PIECES:
            far, parts, shard, width = shape
            shape = (2, parts, width, width)
            copies += len(group) * far * parts
        else:
            copies += 1 if kind in ONCE else walk.count
        if kind != AGAIN:
            held.append(pltpu.VMEM(walk.held(kind, shape), group[0].dtype))
    hbm = pl.BlockSpec(memory_space=pltpu.HBM)
    return run(
        name, functools.partial(copy_kernel, make, walk, kinds, [len(g) for g in groups] + [1] * len(outs), n_in),
        sel, arrays, [hbm] * len(arrays), shapes, [hbm] * len(outs),
        held + list(scratch) + [pltpu.SemaphoreType.DMA((copies,))], flops, 58,
    )


def shape_of(shape, dtype=NARROW):
    return jax.ShapeDtypeStruct(shape, dtype)


def serve_kernel(sel, states_ref, serve_ref, bias_ref, out_ref, held, sems):
    me = sel[0]
    part = held.shape[1]
    copies = []
    for i in range(held.shape[0]):
        copies.append(pltpu.make_async_copy(states_ref.at[me, pl.ds(i * part, part)], held.at[i], sems.at[i]))
        copies[-1].start()
    serve = serve_ref[pl.ds(me, 1)]
    row = lax.broadcasted_iota(jnp.int32, (part, serve.shape[1]), 0)
    total = None
    for i, copy in enumerate(copies):
        copy.wait()
        one = jnp.where(row == serve - i * part, 1.0, 0.0).astype(NARROW)
        value = dot_tn(one, held[i])
        total = value if total is None else total + value
    cap = serve.shape[1] // out_ref.shape[0]
    bias = bias_ref[...]
    for d in range(out_ref.shape[0]):
        out_ref[d] = jnp.concatenate([total[d * cap : (d + 1) * cap], bias], 0).astype(NARROW)


def take_rows(sel, node_states, serve, bias, n):
    _, rows, width = node_states.shape
    shape = (n, serve.shape[1] // n + bias.shape[0], width)
    return run(
        "serve",
        serve_kernel,
        sel,
        (node_states, serve, bias),
        [pl.BlockSpec(memory_space=pltpu.HBM), full(serve.shape), full(bias.shape)],
        shape_of(shape),
        full(shape),
        [pltpu.VMEM((4, rows // 4, width), NARROW), pltpu.SemaphoreType.DMA((4,))],
        limit=58,
    )


def edge_kernel(sel, nbr_ref, alpha_ref, serve_ref, out_ref, served_ref, total):
    me = sel[0]
    slots = served_ref.shape[1]
    rows = nbr_ref.shape[2]
    tile = min(rows, 512)
    total[...] = jnp.zeros_like(total)
    lane = lax.broadcasted_iota(jnp.int32, (slots, tile), 0)
    row = lax.broadcasted_iota(jnp.int32, (tile, slots), 0)

    def step(i, carry):
        at = pl.ds(pl.multiple_of(i * tile, tile), tile)
        nbr, alpha = nbr_ref[me, :, at], alpha_ref[me, :, at]
        value = jnp.zeros((slots, tile), WIDE)
        for k in range(nbr.shape[0]):
            value = value + jnp.where(nbr[k : k + 1] == lane, alpha[k : k + 1], 0.0)
        top, rest = split(value)
        out_ref[:slots, at] = top
        out_ref[slots:, at] = rest
        one = jnp.where(row == serve_ref[pl.ds(me, 1)] - i * tile, 1.0, 0.0).astype(NARROW)
        total[...] += dot(out_ref[:, at], one)
        return carry

    lax.fori_loop(0, rows // tile, step, 0)
    served_ref[...] = total[...].astype(NARROW)


def make_edges(sel, neighbors, alpha, serve):
    _, deg, rows = neighbors.shape
    slots = serve.shape[1]
    shapes = [(2 * slots, rows), (2 * slots, slots)]
    return run(
        "edges",
        edge_kernel,
        sel,
        (neighbors, alpha, serve),
        [full(neighbors.shape), full(alpha.shape), full(serve.shape)],
        [shape_of(a) for a in shapes],
        [full(a) for a in shapes],
        [pltpu.VMEM((2 * slots, slots), WIDE)],
        limit=16 if slots <= 256 else 56,
    )


def by_place(value, me, axis):
    count = value.shape[axis]
    return jnp.concatenate(
        [lax.dynamic_slice_in_dim(value, lax.bitwise_xor(me, i), 1, axis) for i in range(count)], axis
    )


def twice(rows):
    return jnp.concatenate([rows, rows], 0)


def assemble(sel, own, other):
    near = len(own)
    far, kinds, shard, width = own[0].shape
    own, other = (by_place(by_place(jnp.stack(w), sel[2], 0), sel[1], 1).transpose(2, 1, 0, 3, 4) for w in (own, other))
    first = sel[0] == 0
    both = jnp.stack([jnp.where(first, own, other), jnp.where(first, other, own)])
    return both.reshape(2, kinds, far * near * shard, width)


def layer_rows(x, sums, w_ref, b_ref, h_ref):
    hs = (dot(x, w_ref[0, 0]) + b_ref[0:1]).astype(NARROW)
    hn = (sums + b_ref[1:2]).astype(NARROW)
    h_ref[0] = hs
    h_ref[1] = hn
    return unit_rows(dot(hs, w_ref[0, 1]) + dot(hn, w_ref[1, 1]))


def halo_step(walk, sel, x_ref, agg_ref, w_ref, b_ref, e_ref, h_ref, y_ref, m_ref, next_ref):
    def step(i, first, last):
        y, m = layer_rows(x_ref[...], dot(agg_ref[...], w_ref[1, 0]), w_ref, b_ref, h_ref)
        y_ref[...] = y
        m_ref[...] = m
        next_ref[...] = dot_tn(e_ref[...], twice(y)).astype(NARROW)

    return step


def weights_in(weights):
    return (weights, PIECES if isinstance(weights, list) else FULL)


def weights_out(weights):
    if not isinstance(weights, list):
        return []
    _, kinds, _, width = weights[0].shape
    return [((2, kinds, width, width), NARROW, AGAIN)]


def halo_forward(sel, x, agg, weights, bias, edges_s):
    slots, width = x.shape
    walk = Rows(slots, slots)
    walk.tile, walk.count = slots, 1
    ins = [(x, FULL), (agg, FULL), weights_in(weights), (bias, FULL), (edges_s, FULL)]
    outs = [((2, slots, width), NARROW, FULL), ((slots, width), NARROW, FULL), ((slots, width), WIDE, FULL)]
    outs += [((slots, width), NARROW, FULL)] + weights_out(weights)
    out = stage("halo", halo_step, walk, sel, ins, outs, flops=10 * slots * width * width)
    return (*out[:4], out[4] if isinstance(weights, list) else weights)


def forward_step(walk, sel, x_ref, e_ref, s_ref, w_ref, b_ref, *refs):
    has_head = len(refs) > 4
    if has_head:
        head_ref, hb_ref, label_ref, weight_ref, h_ref, y_ref, m_ref, dl_ref, st_ref, table = refs
    else:
        h_ref, y_ref, m_ref, table = refs

    def step(i, first, last):
        @functools.partial(when, first)
        def _():
            table[...] = twice(dot(s_ref[...], w_ref[1, 0]).astype(NARROW))
            if has_head:
                st_ref[...] = jnp.zeros_like(st_ref)

        sums = dot_tn(walk.along(e_ref, i)[...], table[...])
        y, m = layer_rows(walk.down(x_ref, i)[...], sums, w_ref, b_ref, walk.under(h_ref, i))
        walk.down(y_ref, i)[...] = y
        walk.down(m_ref, i)[...] = m.astype(m_ref.dtype)
        if has_head:
            logits = dot_nt(head_ref[...], y) + hb_ref[...]
            label, weight = walk.along(label_ref, i)[...], walk.along(weight_ref, i)[...]
            hit = lax.broadcasted_iota(jnp.int32, logits.shape, 0) == label
            top = jnp.max(logits, axis=0, keepdims=True)
            power = jnp.exp(logits - top)
            total = jnp.sum(power, axis=0, keepdims=True)
            picked = jnp.sum(jnp.where(hit, logits, 0.0), axis=0, keepdims=True)
            cross = top + jnp.log(total) - picked
            dl = (power * (weight / total) - jnp.where(hit, weight, 0.0)).astype(NARROW)
            walk.along(dl_ref, i)[...] = dl
            ones = jnp.ones((8, walk.tile), NARROW)
            st_ref[0:1] += jnp.broadcast_to(jnp.sum(weight * cross, axis=1, keepdims=True), (1, LANES))
            st_ref[1:2] += dot_nt(ones, dl)[0:1]
            st_ref[2:3] += jnp.broadcast_to(jnp.sum(weight, axis=1, keepdims=True), (1, LANES))

    return step


def forward(walk, sel, x, edges, slot_rows, weights, bias, head=None):
    rows, width = x.shape[-2:]
    slots = slot_rows.shape[0]
    ins = [(x, DOWN if x.ndim == 2 else PICK), (edges, ALONG), (slot_rows, FULL), (weights, FULL), (bias, FULL)]
    outs = [((2, rows, width), NARROW, UNDER)] + [((rows, width), NARROW, DOWN)] * 2
    if head is not None:
        ins += [(head[0], FULL), (head[1], FULL), (head[2], ALONG), (head[3], ALONG)]
        outs += [((LANES, rows), NARROW, ALONG), ((8, LANES), WIDE, FULL)]
    table = pltpu.VMEM((2 * slots, width), NARROW)
    return stage("rows_forward", forward_step, walk, sel, ins, outs, [table], 7 * rows * width * width)


def link_step(
    classes, walk, sel, x_ref, agg_ref, w_ref, b_ref, head_ref, st_ref, y_ref, dl_ref, weight_ref, pair_ref,
    d_ref, hl_ref, h_ref, dz_ref, ds_ref, dn_ref, hr_ref, slope, sums, extra,
):
    def step(i, first, last):
        @functools.partial(when, first)
        def _():
            y, m = layer_rows(x_ref[...], dot(agg_ref[...], w_ref[1, 0]), w_ref, b_ref, h_ref)
            hl_ref[:LANES] = head_ref[...]
            hl_ref[LANES:] = y
            slope[...] = m
            sums[...] = jnp.zeros_like(sums)
            extra[...] = jnp.zeros_like(extra)

        y = walk.down(y_ref, i)[...]
        near = dot_nt(hl_ref[LANES:], y)
        weight, pair = walk.along(weight_ref, i)[...], walk.along(pair_ref, i)[...]
        hit = lax.broadcasted_iota(jnp.int32, near.shape, 0) == pair
        arg = -LINK * jnp.sum(jnp.where(hit, near, 0.0), axis=0, keepdims=True)
        small = jnp.exp(-jnp.abs(arg))
        soft = jnp.maximum(arg, 0.0) + jnp.log(1.0 + small)
        sigmoid = jnp.where(arg >= 0.0, 1.0, small) / (1.0 + small)
        extra[0:1] += jnp.broadcast_to(jnp.sum(weight * soft, axis=1, keepdims=True), (1, LANES))
        d_score = -LINK * weight * sigmoid
        d_at = walk.along(d_ref, i)
        d_at[:LANES] = walk.along(dl_ref, i)[...]
        d_at[LANES:] = jnp.where(hit, d_score, 0.0).astype(NARROW)
        sums[...] += dot(d_at[...], y)

        @functools.partial(when, last)
        def _():
            dz = pull_rows(sums[LANES:], hl_ref[LANES:], slope[...])
            dz_ref[...] = dz
            ds_ref[...] = dot_nt(dz, w_ref[0, 1]).astype(NARROW)
            dn_ref[...] = dot_nt(dz, w_ref[1, 1]).astype(NARROW)
            hr_ref[...] = sums[:LANES]
            lane = lax.broadcasted_iota(jnp.int32, (1, LANES), 1)
            row = jnp.where(lane < classes, st_ref[1:2], 0.0)
            row = jnp.where(lane == classes, st_ref[0:1] + extra[0:1], row)
            row = jnp.where(lane == classes + 1, st_ref[2:3], row)
            hr_ref[classes : classes + 1, :LANES] = row

    return step


def link(walk, sel, classes, x, agg, weights, bias, head_t, stats, y, d_logits, weight, pair):
    slots, width = x.shape
    rows = y.shape[0]
    ins = [(a, FULL) for a in (x, agg, weights, bias, head_t, stats)]
    ins += [(y, DOWN), (d_logits, ALONG), (weight, ALONG), (pair, ALONG)]
    outs = [((LANES + slots, rows), NARROW, ALONG), ((LANES + slots, width), NARROW, FULL)]
    outs += [((2, slots, width), NARROW, FULL)] + [((slots, width), NARROW, FULL)] * 3
    outs += [((LANES, width), WIDE, FULL)]
    scratch = [
        pltpu.VMEM((slots, width), WIDE),
        pltpu.VMEM((LANES + slots, width), WIDE),
        pltpu.VMEM((8, LANES), WIDE),
    ]
    flops = 6 * rows * slots * width + 12 * slots * width * width
    return stage("link", functools.partial(link_step, classes), walk, sel, ins, outs, scratch, flops)


def add_sums(sums, dz, h, x, edges, w_ref):
    acc, bias_acc, spread_acc = sums
    acc[0, 1] += dot_tn(h[0], dz)
    acc[1, 1] += dot_tn(h[1], dz)
    ds = dot_nt(dz, w_ref[0, 1]).astype(NARROW)
    dn = dot_nt(dz, w_ref[1, 1]).astype(NARROW)
    acc[0, 0] += dot_tn(x, ds)
    spread_acc[...] += dot(edges, dn)
    bias_acc[0:1] += jnp.sum(ds.astype(WIDE), axis=0, keepdims=True)
    bias_acc[1:2] += jnp.sum(dn.astype(WIDE), axis=0, keepdims=True)
    return ds


def start_sums(sums, dz, h_ref, x, agg, ds, dn):
    acc, bias_acc, spread_acc = sums
    acc[0, 1] = dot_tn(h_ref[0], dz)
    acc[1, 1] = dot_tn(h_ref[1], dz)
    acc[0, 0] = dot_tn(x, ds)
    acc[1, 0] = dot_tn(agg, dn)
    spread_acc[...] = jnp.zeros_like(spread_acc)
    bias_acc[...] = jnp.zeros_like(bias_acc)
    bias_acc[0:1] = jnp.sum(ds.astype(WIDE), axis=0, keepdims=True)
    bias_acc[1:2] = jnp.sum(dn.astype(WIDE), axis=0, keepdims=True)


def finish_sums(me, sums, table, own_ref, other_ref, bo_ref, bx_ref):
    acc, bias_acc, spread_acc = sums
    slots = table.shape[0]
    spread = spread_acc[:slots] + spread_acc[slots:]
    top, rest = split(spread)
    acc[1, 0] += dot_tn(table, top) + dot_tn(table, rest)
    own_ref[...] = acc[me].astype(NARROW)
    other_ref[...] = acc[1 - me].astype(NARROW)
    bo_ref[...] = jnp.broadcast_to(bias_acc[pl.ds(me, 1)], bo_ref.shape)
    bx_ref[...] = jnp.broadcast_to(bias_acc[pl.ds(1 - me, 1)], bx_ref.shape)
    return spread


def back_last_step(
    walk, sel, y_ref, m_ref, x_ref, d_ref, e_ref, h_ref,
    hl_ref, w_ref, hh_ref, xh_ref, gh_ref, dzh_ref, dsh_ref, dnh_ref,
    own_ref, other_ref, bo_ref, bx_ref, dx_ref, sp_ref, *sums,
):
    def step(i, first, last):
        @functools.partial(when, first)
        def _():
            start_sums(sums, dzh_ref[...], hh_ref, xh_ref[...], gh_ref[...], dsh_ref[...], dnh_ref[...])

        d_out = dot_tn(walk.along(d_ref, i)[...], hl_ref[...])
        dz = pull_rows(d_out, walk.down(y_ref, i)[...], walk.down(m_ref, i)[...])
        ds = add_sums(
            sums, dz, walk.under(h_ref, i), walk.down(x_ref, i)[...], walk.along(e_ref, i)[...], w_ref
        )
        walk.down(dx_ref, i)[...] = dot_nt(ds, w_ref[0, 0]).astype(NARROW)

        @functools.partial(when, last)
        def _():
            sp_ref[...] = finish_sums(sel[0], sums, xh_ref[...], own_ref, other_ref, bo_ref, bx_ref)

    return step


def back_first_step(
    walk, sel, y_ref, m_ref, x_ref, dx_ref, e_ref, h_ref,
    w_ref, hh_ref, xh_ref, gh_ref, up_ref, sp_ref, es_ref, ret_ref, dsh_ref, yh_ref, mh_ref,
    own_ref, other_ref, bo_ref, bx_ref, *sums,
):
    def step(i, first, last):
        @functools.partial(when, first)
        def _():
            slots = yh_ref.shape[0]
            back = dot(es_ref[...], ret_ref[...])
            top, rest = split(sp_ref[...] + back[:slots] + back[slots:])
            d_out = dot_nt(top, up_ref[1]) + dot_nt(rest, up_ref[1]) + dot_nt(dsh_ref[...], up_ref[0])
            dz = pull_rows(d_out, yh_ref[...], mh_ref[...])
            ds = dot_nt(dz, w_ref[0, 1]).astype(NARROW)
            dn = dot_nt(dz, w_ref[1, 1]).astype(NARROW)
            start_sums(sums, dz, hh_ref, xh_ref[...], gh_ref[...], ds, dn)

        dz = pull_rows(walk.down(dx_ref, i)[...].astype(WIDE), walk.down(y_ref, i)[...], walk.down(m_ref, i)[...])
        add_sums(sums, dz, walk.under(h_ref, i), walk.down(x_ref, i)[...], walk.along(e_ref, i)[...], w_ref)

        @functools.partial(when, last)
        def _():
            finish_sums(sel[0], sums, xh_ref[...], own_ref, other_ref, bo_ref, bx_ref)

    return step


def sums_scratch(kinds, slots, width):
    return [
        pltpu.VMEM((2, kinds, width, width), WIDE),
        pltpu.VMEM((8, width), WIDE),
        pltpu.VMEM((2 * slots, width), WIDE),
    ]


def last_steps(
    classes, walk, sel, x_ref, e_ref, s_ref, w_ref, b_ref, head_ref, hb_ref, label_ref, weight_ref, pair_ref, agg_ref,
    own_ref, other_ref, bo_ref, bx_ref, dx_ref, sp_ref, ds_ref, dn_ref, hr_ref,
    table, h_ref, y_ref, m_ref, dl_ref, st_ref, d_ref, hl_ref, hh_ref, dz_ref, slope, sums, extra, *acc,
):
    return [
        forward_step(
            walk, sel, x_ref, e_ref, s_ref, w_ref, b_ref, head_ref, hb_ref, label_ref, weight_ref,
            h_ref, y_ref, m_ref, dl_ref, st_ref, table,
        ),
        link_step(
            classes, walk, sel, s_ref, agg_ref, w_ref, b_ref, head_ref, st_ref, y_ref, dl_ref, weight_ref, pair_ref,
            d_ref, hl_ref, hh_ref, dz_ref, ds_ref, dn_ref, hr_ref, slope, sums, extra,
        ),
        back_last_step(
            walk, sel, y_ref, m_ref, x_ref, d_ref, e_ref, h_ref,
            hl_ref, w_ref, hh_ref, s_ref, agg_ref, dz_ref, ds_ref, dn_ref,
            own_ref, other_ref, bo_ref, bx_ref, dx_ref, sp_ref, *acc,
        ),
    ]


def last_layer(walk, sel, classes, x, edges, slot_rows, weights, bias, head, pair, agg):
    rows, width = x.shape
    slots = slot_rows.shape[0]
    if not isinstance(weights, list):
        kinds = weights.shape[1]
        hidden, y, m, d_logits, stats = forward(walk, sel, x, edges, slot_rows, weights, bias, head)
        drive, drive_rows, hidden_h, dz_h, ds_h, dn_h, head_rows = link(
            walk, sel, classes, slot_rows, agg, weights, bias, head[0], stats, y, d_logits, head[3], pair
        )
        grads = backward(
            back_last_step, walk, sel, [y, m, x], drive, edges, hidden,
            [drive_rows, weights, hidden_h, slot_rows, agg, dz_h, ds_h, dn_h], slots, True,
        )
        return list(grads) + [ds_h, dn_h, head_rows, weights]
    kinds = weights[0].shape[1]
    ins = [(x, DOWN), (edges, ALONG), (slot_rows, FULL), weights_in(weights), (bias, FULL), (head[0], FULL)]
    ins += [(head[1], FULL), (head[2], ALONG), (head[3], ALONG), (pair, ALONG), (agg, FULL)]
    outs = [((kinds, width, width), NARROW, FULL)] * 2 + [((8, width), WIDE, FULL)] * 2
    outs += [((rows, width), NARROW, DOWN), ((slots, width), WIDE, FULL)]
    outs += [((slots, width), NARROW, FULL)] * 2 + [((LANES, width), WIDE, FULL)] + weights_out(weights)
    scratch = [
        pltpu.VMEM((2 * slots, width), NARROW),
        pltpu.VMEM((2, rows, width), NARROW),
        pltpu.VMEM((rows, width), NARROW),
        pltpu.VMEM((rows, width), WIDE),
        pltpu.VMEM((LANES, rows), NARROW),
        pltpu.VMEM((8, LANES), WIDE),
        pltpu.VMEM((LANES + slots, rows), NARROW),
        pltpu.VMEM((LANES + slots, width), NARROW),
        pltpu.VMEM((2, slots, width), NARROW),
        pltpu.VMEM((slots, width), NARROW),
        pltpu.VMEM((slots, width), WIDE),
        pltpu.VMEM((LANES + slots, width), WIDE),
        pltpu.VMEM((8, LANES), WIDE),
    ] + sums_scratch(kinds, slots, width)
    return stage("last_layer", functools.partial(last_steps, classes), walk, sel, ins, outs, scratch, 22 * rows * width * width)


def backward(make, walk, sel, rowed, drive, edges, hidden, halo, slots, is_last):
    rows, width = rowed[0].shape
    kinds = hidden.shape[0]
    outs = [((kinds, width, width), NARROW, FULL)] * 2 + [((8, width), WIDE, FULL)] * 2
    if is_last:
        outs += [((rows, width), NARROW, DOWN), ((slots, width), WIDE, FULL)]
    ins = [(a, DOWN if a.ndim == 2 else PICK) for a in rowed]
    ins += [(drive, ALONG if is_last else DOWN), (edges, ALONG), (hidden, UNDER)]
    ins += [(a, FULL) if is_last or n != 4 else (a, LEAD) for n, a in enumerate(halo)]
    scratch = sums_scratch(kinds, slots, width)
    return stage("rows_backward", make, walk, sel, ins, outs, scratch, (13 if is_last else 11) * rows * width * width)


def extras(count):
    return up(2 * count + 2, 16)


def put_pairs(extra, pieces):
    extra[...] = jnp.zeros_like(extra)
    at = 0
    for piece in pieces:
        top = piece.astype(NARROW).astype(WIDE)
        count = piece.shape[0]
        extra[at : at + count] = top
        extra[at + count : at + 2 * count] = piece - top
        at += 2 * count


def pack_kernel(has_rows, apart, sel, own_ref, got_ref, bo_ref, bg_ref, *refs):
    rows_ref, refs = (refs[0], refs[1:]) if has_rows else (None, refs)
    extra, outs = refs[-1], refs[:-1]
    kinds, far, near, shard, _ = own_ref.shape
    for j in range(near):
        out_ref, place = (outs[j], lax.bitwise_xor(sel[2], j)) if apart else (outs[0].at[j], j)
        for f in range(far):
            for k in range(kinds):
                value = own_ref[k, f, place].astype(WIDE) + got_ref[k, f, place].astype(WIDE)
                at = (f * kinds + k) * shard
                out_ref[at : at + shard] = value.astype(NARROW)
        bias = bo_ref[0:1] + bg_ref[0:1]
        put_pairs(extra, [bias] if rows_ref is None else [rows_ref[place], bias])
        out_ref[far * kinds * shard :] = extra[...].astype(NARROW)


def pack(sel, far, near, own, got, bias_own, bias_got, head_rows=None, apart=True):
    kinds, width, _ = own.shape
    shard = width // (far * near)
    count = 0 if head_rows is None else head_rows.shape[1]
    body = far * kinds * shard
    shape = (kinds, far, near, shard, width)
    if shard % 16:
        total = (own.astype(WIDE) + got.astype(WIDE)).reshape(shape).transpose(2, 1, 0, 3, 4).reshape(near, body, width)
        bias = bias_own[0:1] + bias_got[0:1]
        pieces = [total.astype(NARROW)]
        if count:
            pieces += list(halves(head_rows))
        pieces += [jnp.broadcast_to(h[None], (near, 1, width)) for h in halves(bias)]
        out = pad_rows(jnp.concatenate(pieces, 1), 16)
        if apart:
            out = by_place(out, sel[2], 0)
        return [out[j] for j in range(near)] if apart else out
    ins = [own.reshape(shape), got.reshape(shape), bias_own, bias_got]
    if count:
        ins.append(head_rows)
    shape = (body + extras(count), width)
    outs = [shape] * near if apart else [(near,) + shape]
    out = run(
        "pack",
        functools.partial(pack_kernel, count > 0, apart),
        sel,
        ins,
        [full(a.shape) for a in ins],
        [shape_of(a) for a in outs],
        [full(a) for a in outs],
        [pltpu.VMEM((extras(count), width), WIDE)],
        limit=16,
    )
    return out if apart else out[0]


def middle_kernel(far, body, share, near, apart, sel, *refs):
    outs, (total, extra) = refs[near:-2], refs[-2:]
    given = refs[:near] if near > 1 else [refs[0].at[j] for j in range(refs[0].shape[0])]
    value = given[0][...].astype(WIDE)
    for ref in given[1:]:
        value = value + ref[...].astype(WIDE)
    total[...] = value
    count = far * share
    at = far * body
    bias = total[at + 2 * count : at + 2 * count + 1] + total[at + 2 * count + 1 : at + 2 * count + 2]
    for f in range(far):
        out_ref = outs[f] if apart else outs[0].at[f]
        place = lax.bitwise_xor(sel[1], f) if apart else f
        out_ref[:body] = total[pl.ds(pl.multiple_of(place * body, body), body)].astype(NARROW)
        pieces = [bias]
        if share:
            mine = jnp.zeros((share, total.shape[1]), WIDE)
            for g in range(far) if apart else [f]:
                low = at + g * share
                piece = total[low : low + share] + total[low + count : low + count + share]
                mine = jnp.where(place == g, piece, mine) if apart else piece
            pieces = [mine, bias]
        put_pairs(extra, pieces)
        out_ref[body:] = extra[...].astype(NARROW)


def middle(sel, far, share, got, apart=False):
    got = got if isinstance(got, list) else [got]
    rows, width = got[0].shape[-2:]
    near = len(got)
    count = far * share
    body = (rows - extras(count)) // far
    if body % 16:
        total = sum(g.astype(WIDE) for g in got) if near > 1 else jnp.sum(got[0].astype(WIDE), 0)
        at = far * body
        pieces = [total[:at].reshape(far, body, width).astype(NARROW)]
        if share:
            value = total[at : at + count] + total[at + count : at + 2 * count]
            pieces += list(halves(value.reshape(far, share, width)))
        bias = total[at + 2 * count : at + 2 * count + 1] + total[at + 2 * count + 1 : at + 2 * count + 2]
        pieces += [jnp.broadcast_to(h[None], (far, 1, width)) for h in halves(bias)]
        out = jnp.concatenate(pieces, 1)
        out = jnp.pad(out, ((0, 0), (0, body + extras(share) - out.shape[1]), (0, 0)))
        if apart:
            out = by_place(out, sel[1], 0)
        return [out[f] for f in range(far)] if apart else out
    shape = (body + extras(share), width)
    outs = [shape] * far if apart else [(far,) + shape]
    out = run(
        "middle",
        functools.partial(middle_kernel, far, body, share, near, apart),
        sel,
        got,
        [full(a.shape) for a in got],
        [shape_of(a) for a in outs],
        [full(a) for a in outs],
        [pltpu.VMEM((rows, width), WIDE), pltpu.VMEM((extras(share), width), WIDE)],
        limit=16,
    )
    return out if apart else out[0]


def adamw(old, first, second, grad, rate):
    first_new = BETA * first + (1.0 - BETA) * grad
    second_new = BETA * second + (1.0 - BETA) * grad * grad
    step = first_new / (1.0 - BETA**STEP) / (jnp.sqrt(second_new / (1.0 - BETA**STEP)) + EPSA)
    return (old - rate * (step + DECAY * old), first_new, second_new)


def round_kernel(sel, value_ref, out_ref):
    out_ref[...] = value_ref[...].astype(NARROW)


def rounded(sel, value):
    count, rows, width = value.shape
    spec = pl.BlockSpec((1, rows, width), lambda i, s: (i, 0, 0))
    return run(
        "rounded", round_kernel, sel, [value], [spec], shape_of(value.shape), spec, limit=58, grid=(count,)
    )


def square_kernel(body, share, near, sel, *refs):
    given, (sum_ref, bias_ref, out_ref) = refs[:-3], refs[-3:]
    first, second = given[: len(given) // 2], given[len(given) // 2 :]
    total = jnp.zeros((1, 1), WIDE)
    rows = []
    for layer, (given, at) in enumerate(((first, body), (second, body + 2 * share))):
        value = given[0][...].astype(WIDE)
        for ref in given[1:]:
            value = value + ref[...].astype(WIDE)
        sum_ref[layer] = value[:body]
        rows.append(value[at : at + 1] + value[at + 1 : at + 2])
        total = total + jnp.sum(value[:body] * value[:body], keepdims=True)
    width = sum_ref.shape[2]
    shard = bias_ref.shape[1]
    place = (sel[1] * near + sel[2]) * shard
    rows = jnp.concatenate(rows + [jnp.zeros((8 - len(rows), width), WIDE)], 0)
    own = pltpu.roll(rows, lax.rem(width - place, width), 1)[:2, :shard]
    bias_ref[...] = own
    total = total + jnp.sum(own * own, keepdims=True)
    out_ref[...] = jnp.broadcast_to(total[None], out_ref.shape)


def squares_of(sel, first, second, body, share, near, shard, devices):
    width = second[0].shape[1]
    ins = list(first) + list(second)
    outs = [shape_of((2, body, width), WIDE), shape_of((2, shard), WIDE), shape_of((devices, 8, LANES), WIDE)]
    return run(
        "squares",
        functools.partial(square_kernel, body, share, near),
        sel,
        ins,
        [full(a.shape) for a in ins],
        outs,
        [full(o.shape) for o in outs],
        limit=58,
    )


def stacked_halves(value):
    return jnp.concatenate(split(value), 0)


def turn_kernel(sel, value_ref, basis_ref, out_ref):
    for i in range(value_ref.shape[0]):
        both = dot(stacked_halves(value_ref[i]), basis_ref[i])
        out_ref[i] = both[: both.shape[0] // 2] + both[both.shape[0] // 2 :]


def turn(sel, value, basis):
    return run(
        "turn",
        turn_kernel,
        sel,
        [value, basis],
        [full(a.shape) for a in (value, basis)],
        shape_of(value.shape, WIDE),
        full(value.shape),
        limit=58,
    )


def update_kernel(
    sel, turned_ref, parts_ref, head_sq_ref, weight_ref, loss_ref, basis_ref, old_ref, first_ref, second_ref,
    bias_ref, b_old_ref, b_first_ref, b_second_ref, grad_ref, h_old_ref, h_first_ref, h_second_ref,
    norm_ref, pair_ref, new_ref, low_ref, m_ref, v_ref, bn_ref, bm_ref, bv_ref, hn_ref, hm_ref, hv_ref,
):
    squares = jnp.sum(parts_ref[...], axis=0)[0:1, 0:1] + head_sq_ref[...]
    norm = jnp.sqrt(squares) / weight_ref[...]
    norm_ref[...] = norm
    pair_ref[...] = jnp.where(lax.broadcasted_iota(jnp.int32, (1, 2), 1) == 0, loss_ref[...], weight_ref[...])
    factor = jnp.minimum(1.0, CLIP / norm) / weight_ref[...]
    bn_ref[...], bm_ref[...], bv_ref[...] = adamw(
        b_old_ref[...], b_first_ref[...], b_second_ref[...], bias_ref[...] * factor, LR_BIAS
    )
    hn_ref[...], hm_ref[...], hv_ref[...] = adamw(
        h_old_ref[...], h_first_ref[...], h_second_ref[...], grad_ref[...] * factor, LR_HEAD
    )
    for i in range(turned_ref.shape[0]):
        grad = turned_ref[i] * factor
        first = BETA * first_ref[i] + (1.0 - BETA) * grad
        second = BETA * second_ref[i] + (1.0 - BETA) * grad * grad
        m_ref[i] = first
        v_ref[i] = second
        step = first / (1.0 - BETA**STEP) / (jnp.sqrt(second / (1.0 - BETA**STEP)) + EPSA)
        both = dot_nt(stacked_halves(step), basis_ref[i])
        back = both[: both.shape[0] // 2] + both[both.shape[0] // 2 :]
        new = old_ref[i] - LR_MAT * (back + DECAY * old_ref[i])
        new_ref[i] = new
        low_ref[i] = new.astype(NARROW)


def update(sel, *ins):
    mats, bias, head = ins[6], ins[10], ins[14]
    outs = [shape_of((1, 1), WIDE), shape_of((1, 2), WIDE), shape_of(mats.shape, WIDE), shape_of(mats.shape)]
    outs += [shape_of(mats.shape, WIDE)] * 2 + [shape_of(bias.shape, WIDE)] * 3 + [shape_of(head.shape, WIDE)] * 3
    return run(
        "update", update_kernel, sel, ins, [full(a.shape) for a in ins], outs, [full(o.shape) for o in outs], limit=58
    )


def local(
    far,
    near,
    node_states,
    serve,
    neighbors,
    alpha,
    live,
    lam,
    labels,
    link_pair,
    mats,
    mats_m,
    mats_v,
    basis,
    bias,
    bias_m,
    bias_v,
    head,
    head_m,
    head_v,
):
    n = far * near
    branch = lax.axis_index("branch")
    both = ("far", "near")
    rows_dev, width = node_states.shape[1:]
    classes = head.shape[1]
    depth, kinds, _, shard, _ = mats.shape
    slots = serve.shape[1]
    cap = slots // n
    walk = Rows(rows_dev, slots)

    def pick(value):
        return lax.dynamic_index_in_dim(value, branch, 0, keepdims=False)

    def swap(value):
        return lax.ppermute(value, "branch", SWAP)

    def exchange(value, axes):
        return lax.all_to_all(value, axes, 0, 0, tiled=True)

    def hop(value, axis, size, k):
        return lax.ppermute(value, axis, [(i, i ^ k) for i in range(size)]) if k else value

    def spread(rows, count):
        return jnp.broadcast_to(rows[None], (count,) + rows.shape)

    places = (branch, lax.axis_index("far"), lax.axis_index("near"))
    sel = jnp.stack([p.astype(jnp.int32) for p in places])

    low = mats.astype(NARROW).reshape(depth, kinds, shard, width)

    def along_far(part):
        return jnp.stack([hop(part, "far", far, k) for k in range(far)])

    def along_near(pieces):
        return [hop(pieces, "near", near, k) for k in range(near)]

    def join(own):
        other = [swap(piece) for piece in own]
        return list(own) + other if walk.whole and shard % 16 == 0 else assemble(sel, own, other)

    far_0 = along_far(low[0])

    low_bias = jnp.pad(bias.reshape(1, depth * shard), ((0, 7), (0, width - depth * shard)))
    send = take_rows(sel, node_states, serve, low_bias, n)
    far_0, send = lax.optimization_barrier((far_0, send))
    got = exchange(send, both)
    near_0 = along_near(far_0)
    near_0[1], serve, branch, head = lax.optimization_barrier((near_0[1], serve, branch, head))
    edges, edges_s = make_edges(sel, neighbors.transpose(0, 2, 1), alpha.transpose(0, 2, 1), serve)
    slots_0 = got[:, :cap].reshape(slots, width)
    own_bias = got[:, cap, : depth * shard].reshape(n, depth, shard).transpose(1, 0, 2).reshape(depth, width)
    other_bias = swap(own_bias)
    first = branch == 0
    biases = jnp.stack([jnp.where(first, own_bias, other_bias), jnp.where(first, other_bias, own_bias)], 1)
    biases = biases.astype(WIDE)
    agg = lax.dot_general(edges_s, twice(slots_0), (((0,), (0,)), ((), ())), preferred_element_type=WIDE)
    agg_0 = exchange(agg.astype(NARROW), both)

    part, edges_s = lax.optimization_barrier((low[1], edges_s))
    far_1, near_0, agg_0 = lax.optimization_barrier((along_far(part), near_0, agg_0))
    weights = [join(near_0)]
    near_1 = along_near(far_1)

    share = -(-(classes + 1) // n)
    head_t = jnp.pad(head[:width].astype(NARROW).T, ((0, LANES - classes), (0, 0)))
    head_bias = jnp.pad(head[width][:, None], ((0, LANES - classes), (0, 0)), constant_values=-1e30)
    weight = jnp.where(jnp.arange(rows_dev, dtype=jnp.int32) < pick(live)[0], pick(lam), 0.0)[None]

    h_h0, slots_1, m_h0, agg, weights[0] = halo_forward(sel, slots_0, agg_0, weights[0], biases[0], edges_s)
    agg, edges = lax.optimization_barrier((agg, edges))
    agg_1 = exchange(agg, both)
    h_0, x_1, m_0 = forward(walk, sel, node_states, edges, slots_0, weights[0], biases[0])
    near_1, x_1, agg_1 = lax.optimization_barrier((near_1, x_1, agg_1))
    weights.append(join(near_1))
    own_1, other_1, bias_1, bias_x1, d_x, spread_1, ds_h1, dn_h1, head_rows, weights[1] = last_layer(
        walk, sel, classes, x_1, edges, slots_1, weights[1], biases[1],
        (head_t, head_bias, pick(labels)[None], weight), pick(link_pair)[None], agg_1,
    )
    returned = exchange(dn_h1, both)

    head_rows = head_rows[: n * share].reshape(near, far * share, width)
    packed = pack(sel, far, near, own_1, swap(other_1), bias_1, swap(bias_x1), head_rows)
    *packed, spread_1 = lax.optimization_barrier((*packed, spread_1))
    sums_1 = [hop(piece, "near", near, k) for k, piece in enumerate(packed)]
    own_0, other_0, bias_0, bias_x0 = backward(
        back_first_step, walk, sel, [x_1, m_0, node_states], d_x, edges, h_0,
        [weights[0], h_h0, slots_0, agg_0, weights[1], spread_1, edges_s, returned, ds_h1, slots_1, m_h0],
        slots, False,
    )
    own_0, other_0, bias_x0, sums_1 = lax.optimization_barrier((own_0, other_0, bias_x0, sums_1))
    packed = pack(sel, far, near, own_0, swap(other_0), bias_0, swap(bias_x0), apart=False)
    packed, sums_1 = lax.optimization_barrier((packed, sums_1))
    sums_0 = exchange(packed, "near")
    body = kinds * shard
    parts_1 = [hop(piece, "far", far, k) for k, piece in enumerate(middle(sel, far, share, sums_1, True))]
    mine = sum(piece[body : body + 2 * share].astype(WIDE) for piece in parts_1)
    send = pad_rows(jnp.concatenate(halves(mine[:share] + mine[share:]), 0), 8)
    send, sums_0 = lax.optimization_barrier((send, sums_0))
    low_basis = rounded(sel, basis.reshape(depth * kinds, width, width))
    low_basis, send = lax.optimization_barrier((low_basis, send))
    parts_0 = [hop(piece, "far", far, k) for k, piece in enumerate(middle(sel, far, 0, sums_0, True))]

    whole = exchange(spread(send, 2 * n), both + ("branch",)).astype(WIDE)
    head_sum = jnp.sum((whole[:, :share] + whole[:, share : 2 * share]).reshape(far, near, 2, share, width), 2)
    head_sum = head_sum.transpose(1, 0, 2, 3).reshape(n * share, width)
    stats = head_sum[classes : classes + 1]
    loss_sum = stats[:, classes : classes + 1]
    weight_sum = stats[:, classes + 1 : classes + 2]
    sum_head = jnp.concatenate([head_sum[:classes], stats[:, :classes].T], 1)
    head_squares = jnp.sum(sum_head * sum_head, keepdims=True)

    sums, sum_bias, squares = squares_of(sel, parts_0, parts_1, body, share, near, shard, 2 * n)
    squares = exchange(squares, both + ("branch",))
    flat = (depth * kinds, shard, width)
    sums, sum_head = lax.optimization_barrier((sums, sum_head))
    turned = turn(sel, sums.reshape(flat), low_basis)
    norm, loss_parts, mats_new, mats_low, first_new, second_new, *small = update(
        sel, turned, squares, head_squares, weight_sum, loss_sum, low_basis,
        *(a.reshape(flat) for a in (mats, mats_m, mats_v)),
        sum_bias, *(a.reshape(depth, shard) for a in (bias, bias_m, bias_v)),
        sum_head, *(a.T for a in (head, head_m, head_v)),
    )
    return (
        loss_parts[0],
        norm[0, 0],
        *(a.reshape(mats.shape) for a in (mats_new, mats_low, first_new, second_new)),
        *(a.reshape(bias.shape) for a in small[:3]),
        *(a.T for a in small[3:]),
    )


def solution(mesh):
    n = mesh.shape["rows"]
    near = 1 << (n.bit_length() // 2)
    far = n // near
    grid = Mesh(mesh.devices.reshape(far, near, 2), ("far", "near", "branch"))
    rows = ("far", "near")
    by_row = P(None, rows)
    by_row_last = P(None, rows, None)
    matrix = P(None, None, "branch", rows, None)
    vector = P(None, "branch", rows)
    return jax.shard_map(
        functools.partial(local, far, near),
        mesh=grid,
        in_specs=(by_row_last, by_row, by_row_last, by_row_last)
        + (by_row,) * 4
        + (matrix,) * 3
        + (P(None, None, "branch", None, None),)
        + (vector,) * 3
        + (P(),) * 3,
        out_specs=(P(), P()) + (matrix,) * 4 + (vector,) * 3 + (P(),) * 3,
        check_vma=False,
    )
```

```python
import functools

import jax
import jax.numpy as jnp
from jax import lax
from jax.experimental import pallas as pl
from jax.experimental.pallas import tpu as pltpu
from jax.sharding import Mesh
from jax.sharding import PartitionSpec as P

STEP = 5
LINK = 4.0
CLIP = 0.001
EPSN = 1e-06
BETA = 0.5
EPSA = 1e-08
LR_MAT = 0.02
LR_BIAS = 0.05
LR_HEAD = 0.02
DECAY = 0.01
HIGH = lax.Precision.HIGHEST
WIDE = jnp.float32
NARROW = jnp.bfloat16
GELU_A = 0.7978845608028654
GELU_B = 0.044715
LANES = 128
SWAP = [(0, 1), (1, 0)]


def halves(value):
    top = lax.reduce_precision(value, 8, 7)
    return top.astype(NARROW), (value - top).astype(NARROW)


def up(value, unit):
    return -(-value // unit) * unit


def pad_rows(rows, unit):
    extra = -rows.shape[-2] % unit
    return jnp.pad(rows, [(0, 0)] * (rows.ndim - 2) + [(0, extra), (0, 0)])


def split(value):
    top = value.astype(NARROW)
    return top, (value - top.astype(WIDE)).astype(NARROW)


def dot(left, right):
    return lax.dot_general(left, right, (((1,), (0,)), ((), ())), preferred_element_type=WIDE)


def dot_nt(left, right):
    return lax.dot_general(left, right, (((1,), (1,)), ((), ())), preferred_element_type=WIDE)


def dot_tn(left, right):
    return lax.dot_general(left, right, (((0,), (0,)), ((), ())), preferred_element_type=WIDE)


def unit_rows(pre):
    sq = pre * pre
    gate = 0.5 + 0.5 * jnp.tanh(pre * (GELU_A + GELU_A * GELU_B * sq))
    slope = gate * (1.0 + pre * (1.0 - gate) * (2.0 * GELU_A + 6.0 * GELU_A * GELU_B * sq))
    act = pre * gate
    inv = lax.rsqrt(jnp.sum(act * act, axis=1, keepdims=True) + EPSN)
    return (act * inv).astype(NARROW), slope * inv


def pull_rows(d_out, out, slope):
    wide = out.astype(WIDE)
    along = jnp.sum(wide * d_out, axis=1, keepdims=True)
    return (slope.astype(WIDE) * (d_out - wide * along)).astype(NARROW)


def full(shape):
    return pl.BlockSpec(shape, lambda *_: (0,) * len(shape))


def when(flag, body):
    if isinstance(flag, bool):
        if flag:
            body()
    else:
        pl.when(flag)(body)


class Rows:
    def __init__(self, rows, slots, tile=512):
        self.rows = rows
        self.whole = slots <= 256
        self.tile = min(rows, tile)
        self.count = rows // self.tile

    def at(self, i):
        return pl.ds(i * self.tile, self.tile)

    def down(self, ref, i):
        return ref.at[self.at(i)] if self.whole else ref

    def along(self, ref, i):
        return ref.at[:, self.at(i)] if self.whole else ref

    def under(self, ref, i):
        return ref.at[:, self.at(i)] if self.whole else ref

    def part(self, kind, ref, i):
        return ref if kind in ONCE else ref.at[self.at(i)] if kind in (DOWN, PICK) else ref.at[:, self.at(i)]

    def source(self, kind, ref, i, sel):
        return ref.at[:, 0] if kind in (LEAD, LATE_LEAD) else self.part(kind, ref.at[sel[0]] if kind == PICK else ref, i)

    def held(self, kind, shape):
        return shape[1:] if kind == PICK else shape[:1] + shape[2:] if kind in (LEAD, LATE_LEAD) else shape

    def spec(self, kind, shape):
        if kind in (FULL, LATE):
            return full(shape)
        if kind in (LEAD, LATE_LEAD):
            return pl.BlockSpec((shape[0], None) + shape[2:], lambda *_: (0,) * len(shape))
        if kind == PICK:
            return pl.BlockSpec((None, self.tile, shape[2]), lambda i, s: (s[0], i, 0))
        if kind == DOWN:
            return pl.BlockSpec((self.tile,) + shape[1:], lambda i, s: (i, 0))
        if kind == ALONG:
            return pl.BlockSpec((shape[0], self.tile), lambda i, s: (0, i))
        return pl.BlockSpec((shape[0], self.tile, shape[2]), lambda i, s: (0, i, 0))


FULL, DOWN, ALONG, UNDER, PICK, LEAD, PIECES, AGAIN, LATE, LATE_LEAD = range(10)
ONCE = (FULL, LEAD, PIECES, AGAIN, LATE, LATE_LEAD)


def grid_kernel(make, walk, n_in, n_out, sel, *refs):
    i = pl.program_id(0)
    make(walk, sel, *refs)(i, i == 0, i == walk.count - 1)


def piece_copies(sel, refs, out_ref):
    near = len(refs) // 2
    far, kinds, shard, _ = refs[0].shape
    pairs = []
    for half in range(2):
        slot = sel[0] if half == 0 else 1 - sel[0]
        for j in range(near):
            for f in range(far):
                place = lax.bitwise_xor(sel[1], f) * near + lax.bitwise_xor(sel[2], j)
                at = pl.ds(pl.multiple_of(place * shard, shard), shard)
                pairs += [(refs[half * near + j].at[f, k], out_ref.at[slot, k, at]) for k in range(kinds)]
    return pairs


def copy_kernel(make, walk, kinds, sizes, n_in, sel, *refs):
    count = len(kinds)
    far, at = [], 0
    for size in sizes:
        far.append(refs[at : at + size])
        at += size
    held = [k for k in range(count) if kinds[k] != AGAIN]
    near = dict(zip(held, refs[at : at + len(held)]))
    steps = make(walk, sel, *near.values(), *refs[at + len(held) : -1])
    steps = steps if isinstance(steps, list) else [steps]
    sems = refs[-1]
    used = [0]

    def copies(k, i):
        kind = kinds[k]
        if kind == PIECES:
            pairs = piece_copies(sel, far[k], near[k])
        elif kind == AGAIN:
            pairs = [(near[kinds.index(PIECES)], far[k][0])]
        else:
            pair = (walk.source(kind, far[k][0], i, sel), walk.part(kind, near[k], i))
            pairs = [pair if k < n_in else pair[::-1]]
        used[0] += len(pairs)
        return [
            pltpu.make_async_copy(*pair, sems.at[used[0] - len(pairs) + n]) for n, pair in enumerate(pairs)
        ]

    def wanted(i, given):
        chosen = []
        for k in given:
            late = k >= n_in or kinds[k] in (LATE, LATE_LEAD)
            if kinds[k] not in ONCE or i == (walk.count - 1 if late else 0):
                chosen += copies(k, i)
        return chosen

    loads = [wanted(i, range(n_in)) for i in range(walk.count)]
    ahead = 2
    for group in loads[:ahead]:
        for item in group:
            item.start()
    stores = []
    results = [k for k in range(n_in, count) if kinds[k] != AGAIN]
    for n, step in enumerate(steps):
        for i in range(walk.count):
            for item in loads[i] if n == 0 else []:
                item.wait()
            for item in loads[i + ahead] if n == 0 and i + ahead < walk.count else []:
                item.start()
            if n == 0 and i == 0:
                stores = [item for k in range(n_in, count) if kinds[k] == AGAIN for item in copies(k, i)]
                for item in stores:
                    item.start()
            step(i, i == 0, i == walk.count - 1)
            for item in wanted(i, results) if n == len(steps) - 1 else []:
                item.start()
                stores.append(item)
    for item in stores:
        item.wait()


def run(name, kernel, sel, ins, in_specs, outs, out_specs, scratch=(), flops=0, limit=20, grid=(), size=None):
    if size is None:
        size = sum(a.size * a.dtype.itemsize for a in ins)
        size += sum(o.size * o.dtype.itemsize for o in (outs if isinstance(outs, list) else [outs]))
    return pl.pallas_call(
        kernel,
        out_shape=outs,
        grid_spec=pltpu.PrefetchScalarGridSpec(
            num_scalar_prefetch=1,
            grid=grid,
            in_specs=in_specs,
            out_specs=out_specs,
            scratch_shapes=list(scratch),
        ),
        compiler_params=pltpu.CompilerParams(
            dimension_semantics=("arbitrary",) * len(grid), vmem_limit_bytes=limit << 20
        ),
        name=name,
        cost_estimate=pl.CostEstimate(flops=flops, bytes_accessed=size, transcendentals=0),
    )(sel, *ins)


def stage(name, make, walk, sel, ins, outs, scratch=(), flops=0):
    kinds = [k for _, k in ins] + [k for *_, k in outs]
    groups = [a if isinstance(a, list) else [a] for a, _ in ins]
    arrays = [a for group in groups for a in group]
    shapes = [shape_of(shape, dtype) for shape, dtype, _ in outs]
    n_in = len(ins)
    if not walk.whole:
        specs = [walk.spec(k, a.shape) for k, a in zip(kinds, arrays + shapes)]
        return run(
            name, functools.partial(grid_kernel, make, walk, n_in, len(outs)),
            sel, arrays, specs[:n_in], shapes, specs[n_in:], scratch, flops, 58, (walk.count,),
        )
    held, copies = [], 0
    for kind, group in zip(kinds, groups + [[a] for a in shapes]):
        shape = group[0].shape
        if kind == PIECES:
            far, parts, shard, width = shape
            shape = (2, parts, width, width)
            copies += len(group) * far * parts
        else:
            copies += 1 if kind in ONCE else walk.count
        if kind != AGAIN:
            held.append(pltpu.VMEM(walk.held(kind, shape), group[0].dtype))
    hbm = pl.BlockSpec(memory_space=pltpu.HBM)
    free = pl.BlockSpec(memory_space=pl.ANY)
    specs = [free if kind == PIECES else hbm for kind, group in zip(kinds, groups) for _ in group]
    return run(
        name, functools.partial(copy_kernel, make, walk, kinds, [len(g) for g in groups] + [1] * len(outs), n_in),
        sel, arrays, specs, shapes, [hbm] * len(outs),
        held + list(scratch) + [pltpu.SemaphoreType.DMA((copies,))], flops, 58,
    )


def shape_of(shape, dtype=NARROW):
    return jax.ShapeDtypeStruct(shape, dtype)


def serve_kernel(sel, states_ref, serve_ref, bias_ref, out_ref, held, sems):
    me = sel[0]
    part = held.shape[1]
    copies = []
    for i in range(held.shape[0]):
        copies.append(pltpu.make_async_copy(states_ref.at[me, pl.ds(i * part, part)], held.at[i], sems.at[i]))
        copies[-1].start()
    serve = serve_ref[pl.ds(me, 1)]
    row = lax.broadcasted_iota(jnp.int32, (part, serve.shape[1]), 0)
    total = None
    for i, copy in enumerate(copies):
        copy.wait()
        one = jnp.where(row == serve - i * part, 1.0, 0.0).astype(NARROW)
        value = dot_tn(one, held[i])
        total = value if total is None else total + value
    cap = serve.shape[1] // out_ref.shape[0]
    depth, _, shard = bias_ref.shape
    bias = jnp.zeros((8, out_ref.shape[2]), WIDE)
    for layer in range(depth):
        spot = lax.broadcasted_iota(jnp.int32, (shard, out_ref.shape[2]), 1)
        here = spot == lax.broadcasted_iota(jnp.int32, spot.shape, 0) + layer * shard
        row = jnp.broadcast_to(bias_ref[layer].astype(NARROW), (8, shard))
        bias = bias + dot(row, jnp.where(here, 1.0, 0.0).astype(NARROW))
    for d in range(out_ref.shape[0]):
        out_ref[d] = jnp.concatenate([total[d * cap : (d + 1) * cap], bias], 0).astype(NARROW)


def take_rows(sel, node_states, serve, bias, n):
    _, rows, width = node_states.shape
    shape = (n, serve.shape[1] // n + 8, width)
    return run(
        "serve",
        serve_kernel,
        sel,
        (node_states, serve, bias),
        [pl.BlockSpec(memory_space=pltpu.HBM), full(serve.shape), full(bias.shape)],
        shape_of(shape),
        full(shape),
        [pltpu.VMEM((4, rows // 4, width), NARROW), pltpu.SemaphoreType.DMA((4,))],
        limit=58,
    )


def edge_kernel(sel, nbr_ref, alpha_ref, serve_ref, out_ref, served_ref, total):
    me = sel[0]
    slots = served_ref.shape[1]
    rows = nbr_ref.shape[2]
    tile = min(rows, 512)
    total[...] = jnp.zeros_like(total)
    lane = lax.broadcasted_iota(jnp.int32, (slots, tile), 0)
    row = lax.broadcasted_iota(jnp.int32, (tile, slots), 0)

    def step(i, carry):
        at = pl.ds(pl.multiple_of(i * tile, tile), tile)
        nbr, alpha = nbr_ref[me, :, at], alpha_ref[me, :, at]
        value = jnp.zeros((slots, tile), WIDE)
        for k in range(nbr.shape[0]):
            value = value + jnp.where(nbr[k : k + 1] == lane, alpha[k : k + 1], 0.0)
        top, rest = split(value)
        out_ref[:slots, at] = top
        out_ref[slots:, at] = rest
        one = jnp.where(row == serve_ref[pl.ds(me, 1)] - i * tile, 1.0, 0.0).astype(NARROW)
        total[...] += dot(out_ref[:, at], one)
        return carry

    lax.fori_loop(0, rows // tile, step, 0)
    served_ref[...] = total[...].astype(NARROW)


def make_edges(sel, neighbors, alpha, serve):
    _, deg, rows = neighbors.shape
    slots = serve.shape[1]
    shapes = [(2 * slots, rows), (2 * slots, slots)]
    return run(
        "edges",
        edge_kernel,
        sel,
        (neighbors, alpha, serve),
        [full(neighbors.shape), full(alpha.shape), full(serve.shape)],
        [shape_of(a) for a in shapes],
        [full(a) for a in shapes],
        [pltpu.VMEM((2 * slots, slots), WIDE)],
        flops=5 * 10**9,
        limit=16 if slots <= 256 else 56,
    )


def by_place(value, me, axis):
    count = value.shape[axis]
    return jnp.concatenate(
        [lax.dynamic_slice_in_dim(value, lax.bitwise_xor(me, i), 1, axis) for i in range(count)], axis
    )


def twice(rows):
    return jnp.concatenate([rows, rows], 0)


def assemble(sel, own, other):
    near = len(own)
    far, kinds, shard, width = own[0].shape
    own, other = (by_place(by_place(jnp.stack(w), sel[2], 0), sel[1], 1).transpose(2, 1, 0, 3, 4) for w in (own, other))
    first = sel[0] == 0
    both = jnp.stack([jnp.where(first, own, other), jnp.where(first, other, own)])
    return both.reshape(2, kinds, far * near * shard, width)


def layer_rows(x, sums, w_ref, b_ref, h_ref):
    hs = (dot(x, w_ref[0, 0]) + b_ref[0:1]).astype(NARROW)
    hn = (sums + b_ref[1:2]).astype(NARROW)
    h_ref[0] = hs
    h_ref[1] = hn
    return unit_rows(dot(hs, w_ref[0, 1]) + dot(hn, w_ref[1, 1]))


def halo_step(walk, sel, x_ref, agg_ref, w_ref, b_ref, e_ref, h_ref, y_ref, m_ref, next_ref):
    def step(i, first, last):
        y, m = layer_rows(x_ref[...], dot(agg_ref[...], w_ref[1, 0]), w_ref, b_ref, h_ref)
        y_ref[...] = y
        m_ref[...] = m
        next_ref[...] = dot_tn(e_ref[...], twice(y)).astype(NARROW)

    return step


def weights_in(weights):
    return (weights, PIECES if isinstance(weights, list) else FULL)


def weights_out(weights):
    if not isinstance(weights, list):
        return []
    _, kinds, _, width = weights[0].shape
    return [((2, kinds, width, width), NARROW, AGAIN)]


def halo_forward(sel, x, agg, weights, bias, edges_s):
    slots, width = x.shape
    walk = Rows(slots, slots)
    walk.tile, walk.count = slots, 1
    ins = [(x, FULL), (agg, FULL), weights_in(weights), (bias, FULL), (edges_s, FULL)]
    outs = [((2, slots, width), NARROW, FULL), ((slots, width), NARROW, FULL), ((slots, width), WIDE, FULL)]
    outs += [((slots, width), NARROW, FULL)] + weights_out(weights)
    out = stage("halo", halo_step, walk, sel, ins, outs, flops=10 * slots * width * width)
    return (*out[:4], out[4] if isinstance(weights, list) else weights)


def own_row(walk, sel, ref, i):
    return ref[pl.ds(sel[0], 1), pl.ds(i * walk.tile if walk.whole else pl.multiple_of(i * walk.tile, LANES), walk.tile)]


def node_weights(walk, sel, lam_ref, i):
    node = lax.broadcasted_iota(jnp.int32, (1, walk.tile), 1) + i * walk.tile
    return jnp.where(node < sel[3], own_row(walk, sel, lam_ref, i), 0.0)


def forward_step(walk, sel, x_ref, e_ref, s_ref, w_ref, b_ref, *refs):
    has_head = len(refs) > 4
    if has_head:
        head_ref, label_ref, lam_ref, h_ref, y_ref, m_ref, dl_ref, st_ref, table, class_ref, hb_ref = refs
        classes, width = head_ref.shape[0], head_ref.shape[1] - 1
    else:
        h_ref, y_ref, m_ref, table = refs

    def step(i, first, last):
        @functools.partial(when, first)
        def _():
            table[...] = twice(dot(s_ref[...], w_ref[1, 0]).astype(NARROW))
            if has_head:
                st_ref[...] = jnp.zeros_like(st_ref)
                class_ref[...] = jnp.zeros_like(class_ref)
                class_ref[:classes] = head_ref[:, :width].astype(NARROW)
                hb_ref[...] = jnp.full_like(hb_ref, -1e30)
                hb_ref[:classes] = head_ref[:, width:]

        sums = dot_tn(walk.along(e_ref, i)[...], table[...])
        y, m = layer_rows(walk.down(x_ref, i)[...], sums, w_ref, b_ref, walk.under(h_ref, i))
        walk.down(y_ref, i)[...] = y
        walk.down(m_ref, i)[...] = m.astype(m_ref.dtype)
        if has_head:
            logits = dot_nt(class_ref[...], y) + hb_ref[...]
            label, weight = own_row(walk, sel, label_ref, i), node_weights(walk, sel, lam_ref, i)
            hit = lax.broadcasted_iota(jnp.int32, logits.shape, 0) == label
            top = jnp.max(logits, axis=0, keepdims=True)
            power = jnp.exp(logits - top)
            total = jnp.sum(power, axis=0, keepdims=True)
            picked = jnp.sum(jnp.where(hit, logits, 0.0), axis=0, keepdims=True)
            cross = top + jnp.log(total) - picked
            dl = (power * (weight / total) - jnp.where(hit, weight, 0.0)).astype(NARROW)
            walk.along(dl_ref, i)[...] = dl
            ones = jnp.ones((8, walk.tile), NARROW)
            st_ref[0:1] += jnp.broadcast_to(jnp.sum(weight * cross, axis=1, keepdims=True), (1, LANES))
            st_ref[1:2] += dot_nt(ones, dl)[0:1]
            st_ref[2:3] += jnp.broadcast_to(jnp.sum(weight, axis=1, keepdims=True), (1, LANES))

    return step


def head_scratch(width):
    return [pltpu.VMEM((LANES, width), NARROW), pltpu.VMEM((LANES, 1), WIDE)]


def forward(walk, sel, x, edges, slot_rows, weights, bias, head=None):
    rows, width = x.shape[-2:]
    slots = slot_rows.shape[0]
    ins = [(x, DOWN if x.ndim == 2 else PICK), (edges, ALONG), (slot_rows, FULL), (weights, FULL), (bias, FULL)]
    outs = [((2, rows, width), NARROW, UNDER)] + [((rows, width), NARROW, DOWN)] * 2
    if head is not None:
        ins += [(a, FULL) for a in head]
        outs += [((LANES, rows), NARROW, ALONG), ((8, LANES), WIDE, FULL)]
    scratch = [pltpu.VMEM((2 * slots, width), NARROW)] + (head_scratch(width) if head is not None else [])
    return stage("rows_forward", forward_step, walk, sel, ins, outs, scratch, 7 * rows * width * width)


def link_step(
    walk, sel, x_ref, agg_ref, w_ref, b_ref, head_ref, st_ref, lam_ref, pair_ref, y_ref, dl_ref,
    d_ref, hl_ref, h_ref, dz_ref, ds_ref, dn_ref, hr_ref, slope, sums, extra,
):
    classes, width = head_ref.shape[0], head_ref.shape[1] - 1

    def step(i, first, last):
        @functools.partial(when, first)
        def _():
            y, m = layer_rows(x_ref[...], dot(agg_ref[...], w_ref[1, 0]), w_ref, b_ref, h_ref)
            hl_ref[:LANES] = jnp.zeros((LANES, width), NARROW)
            hl_ref[:classes] = head_ref[:, :width].astype(NARROW)
            hl_ref[LANES:] = y
            slope[...] = m
            sums[...] = jnp.zeros_like(sums)
            extra[...] = jnp.zeros_like(extra)

        y = walk.down(y_ref, i)[...]
        near = dot_nt(hl_ref[LANES:], y)
        weight, pair = node_weights(walk, sel, lam_ref, i), own_row(walk, sel, pair_ref, i)
        hit = lax.broadcasted_iota(jnp.int32, near.shape, 0) == pair
        arg = -LINK * jnp.sum(jnp.where(hit, near, 0.0), axis=0, keepdims=True)
        small = jnp.exp(-jnp.abs(arg))
        soft = jnp.maximum(arg, 0.0) + jnp.log(1.0 + small)
        sigmoid = jnp.where(arg >= 0.0, 1.0, small) / (1.0 + small)
        extra[0:1] += jnp.broadcast_to(jnp.sum(weight * soft, axis=1, keepdims=True), (1, LANES))
        d_score = -LINK * weight * sigmoid
        d_at = walk.along(d_ref, i)
        d_at[:LANES] = walk.along(dl_ref, i)[...]
        d_at[LANES:] = jnp.where(hit, d_score, 0.0).astype(NARROW)
        sums[...] += dot(d_at[...], y)

        @functools.partial(when, last)
        def _():
            dz = pull_rows(sums[LANES:], hl_ref[LANES:], slope[...])
            dz_ref[...] = dz
            ds_ref[...] = dot_nt(dz, w_ref[0, 1]).astype(NARROW)
            dn_ref[...] = dot_nt(dz, w_ref[1, 1]).astype(NARROW)
            lane = lax.broadcasted_iota(jnp.int32, (1, LANES), 1)
            row = jnp.where(lane < classes, st_ref[1:2], 0.0)
            row = jnp.where(lane == classes, st_ref[0:1] + extra[0:1], row)
            row = jnp.where(lane == classes + 1, st_ref[2:3], row)
            sums[classes : classes + 1, :LANES] = row
            for j in range(hr_ref.shape[0]):
                hr_ref[j] = sums[j * hr_ref.shape[1] : (j + 1) * hr_ref.shape[1]]

    return step


def link(walk, sel, head_shape, x, agg, weights, bias, head_t, stats, lam, pair, y, d_logits):
    slots, width = x.shape
    rows = y.shape[0]
    ins = [(a, FULL) for a in (x, agg, weights, bias, head_t, stats, lam, pair)]
    ins += [(y, DOWN), (d_logits, ALONG)]
    outs = [((LANES + slots, rows), NARROW, ALONG), ((LANES + slots, width), NARROW, FULL)]
    outs += [((2, slots, width), NARROW, FULL)] + [((slots, width), NARROW, FULL)] * 3
    outs += [(head_shape + (width,), WIDE, FULL)]
    scratch = [
        pltpu.VMEM((slots, width), WIDE),
        pltpu.VMEM((LANES + slots, width), WIDE),
        pltpu.VMEM((8, LANES), WIDE),
    ]
    flops = 6 * rows * slots * width + 12 * slots * width * width
    return stage("link", link_step, walk, sel, ins, outs, scratch, flops)


def add_sums(sums, dz, h, x, edges, w_ref):
    acc, bias_acc, spread_acc = sums
    acc[0, 1] += dot_tn(h[0], dz)
    acc[1, 1] += dot_tn(h[1], dz)
    ds = dot_nt(dz, w_ref[0, 1]).astype(NARROW)
    dn = dot_nt(dz, w_ref[1, 1]).astype(NARROW)
    acc[0, 0] += dot_tn(x, ds)
    spread_acc[...] += dot(edges, dn)
    bias_acc[0:1] += jnp.sum(ds.astype(WIDE), axis=0, keepdims=True)
    bias_acc[1:2] += jnp.sum(dn.astype(WIDE), axis=0, keepdims=True)
    return ds


def more_sums(sums, dz, h_ref, x, agg, ds, dn):
    acc, bias_acc, _ = sums
    acc[0, 1] += dot_tn(h_ref[0], dz)
    acc[1, 1] += dot_tn(h_ref[1], dz)
    acc[0, 0] += dot_tn(x, ds)
    acc[1, 0] += dot_tn(agg, dn)
    bias_acc[0:1] += jnp.sum(ds.astype(WIDE), axis=0, keepdims=True)
    bias_acc[1:2] += jnp.sum(dn.astype(WIDE), axis=0, keepdims=True)


def finish_sums(me, sums, table, own_ref, other_ref, bo_ref, bx_ref):
    acc, bias_acc, spread_acc = sums
    slots = table.shape[0]
    spread = spread_acc[:slots] + spread_acc[slots:]
    top, rest = split(spread)
    acc[1, 0] += dot_tn(table, top) + dot_tn(table, rest)
    own_ref[...] = acc[me].astype(NARROW)
    other_ref[...] = acc[1 - me].astype(NARROW)
    bo_ref[...] = jnp.broadcast_to(bias_acc[pl.ds(me, 1)], bo_ref.shape)
    bx_ref[...] = jnp.broadcast_to(bias_acc[pl.ds(1 - me, 1)], bx_ref.shape)
    return spread


def back_last_step(
    walk, sel, y_ref, m_ref, x_ref, d_ref, e_ref, h_ref,
    hl_ref, w_ref, hh_ref, xh_ref, gh_ref, dzh_ref, dsh_ref, dnh_ref,
    own_ref, other_ref, bo_ref, bx_ref, dx_ref, sp_ref, *sums,
):
    def step(i, first, last):
        @functools.partial(when, first)
        def _():
            for ref in sums:
                ref[...] = jnp.zeros_like(ref)
            more_sums(sums, dzh_ref[...], hh_ref, xh_ref[...], gh_ref[...], dsh_ref[...], dnh_ref[...])

        d_out = dot_tn(walk.along(d_ref, i)[...], hl_ref[...])
        dz = pull_rows(d_out, walk.down(y_ref, i)[...], walk.down(m_ref, i)[...])
        ds = add_sums(
            sums, dz, walk.under(h_ref, i), walk.down(x_ref, i)[...], walk.along(e_ref, i)[...], w_ref
        )
        walk.down(dx_ref, i)[...] = dot_nt(ds, w_ref[0, 0]).astype(NARROW)

        @functools.partial(when, last)
        def _():
            sp_ref[...] = finish_sums(sel[0], sums, xh_ref[...], own_ref, other_ref, bo_ref, bx_ref)

    return step


def back_first_step(
    walk, sel, y_ref, m_ref, x_ref, dx_ref, e_ref, h_ref,
    w_ref, hh_ref, xh_ref, gh_ref, up_ref, sp_ref, es_ref, ret_ref, dsh_ref, yh_ref, mh_ref,
    own_ref, other_ref, bo_ref, bx_ref, *sums,
):
    def step(i, first, last):
        @functools.partial(when, first)
        def _():
            for ref in sums:
                ref[...] = jnp.zeros_like(ref)

        dz = pull_rows(walk.down(dx_ref, i)[...].astype(WIDE), walk.down(y_ref, i)[...], walk.down(m_ref, i)[...])
        add_sums(sums, dz, walk.under(h_ref, i), walk.down(x_ref, i)[...], walk.along(e_ref, i)[...], w_ref)

        @functools.partial(when, last)
        def _():
            slots = yh_ref.shape[0]
            back = dot(es_ref[...], ret_ref[...])
            top, rest = split(sp_ref[...] + back[:slots] + back[slots:])
            d_out = dot_nt(top, up_ref[1]) + dot_nt(rest, up_ref[1]) + dot_nt(dsh_ref[...], up_ref[0])
            dz = pull_rows(d_out, yh_ref[...], mh_ref[...])
            ds = dot_nt(dz, w_ref[0, 1]).astype(NARROW)
            dn = dot_nt(dz, w_ref[1, 1]).astype(NARROW)
            more_sums(sums, dz, hh_ref, xh_ref[...], gh_ref[...], ds, dn)
            finish_sums(sel[0], sums, xh_ref[...], own_ref, other_ref, bo_ref, bx_ref)

    return step


def sums_scratch(kinds, slots, width):
    return [
        pltpu.VMEM((2, kinds, width, width), WIDE),
        pltpu.VMEM((8, width), WIDE),
        pltpu.VMEM((2 * slots, width), WIDE),
    ]


def last_steps(
    walk, sel, x_ref, e_ref, s_ref, w_ref, b_ref, head_ref, label_ref, lam_ref, pair_ref, agg_ref,
    own_ref, other_ref, bo_ref, bx_ref, dx_ref, sp_ref, ds_ref, dn_ref, hr_ref,
    table, class_ref, hb_ref, h_ref, y_ref, m_ref, dl_ref, st_ref, d_ref, hl_ref, hh_ref, dz_ref, slope, sums, extra,
    *acc,
):
    return [
        forward_step(
            walk, sel, x_ref, e_ref, s_ref, w_ref, b_ref, head_ref, label_ref, lam_ref,
            h_ref, y_ref, m_ref, dl_ref, st_ref, table, class_ref, hb_ref,
        ),
        link_step(
            walk, sel, s_ref, agg_ref, w_ref, b_ref, head_ref, st_ref, lam_ref, pair_ref, y_ref, dl_ref,
            d_ref, hl_ref, hh_ref, dz_ref, ds_ref, dn_ref, hr_ref, slope, sums, extra,
        ),
        back_last_step(
            walk, sel, y_ref, m_ref, x_ref, d_ref, e_ref, h_ref,
            hl_ref, w_ref, hh_ref, s_ref, agg_ref, dz_ref, ds_ref, dn_ref,
            own_ref, other_ref, bo_ref, bx_ref, dx_ref, sp_ref, *acc,
        ),
    ]


def last_layer(walk, sel, head_shape, x, edges, slot_rows, weights, bias, head, pair, agg):
    rows, width = x.shape
    slots = slot_rows.shape[0]
    if not isinstance(weights, list):
        hidden, y, m, d_logits, stats = forward(walk, sel, x, edges, slot_rows, weights, bias, head)
        drive, drive_rows, hidden_h, dz_h, ds_h, dn_h, head_rows = link(
            walk, sel, head_shape, slot_rows, agg, weights, bias, head[0], stats, head[2], pair, y, d_logits
        )
        grads = backward(
            back_last_step, walk, sel, [y, m, x], drive, edges, hidden,
            [drive_rows, weights, hidden_h, slot_rows, agg, dz_h, ds_h, dn_h], slots, True,
        )
        return list(grads) + [ds_h, dn_h, head_rows, weights]
    kinds = weights[0].shape[1]
    ins = [(x, DOWN), (edges, ALONG), (slot_rows, FULL), weights_in(weights), (bias, FULL)]
    ins += [(a, FULL) for a in (*head, pair, agg)]
    outs = [((kinds, width, width), NARROW, FULL)] * 2 + [((8, width), WIDE, FULL)] * 2
    outs += [((rows, width), NARROW, DOWN), ((slots, width), WIDE, FULL)]
    outs += [((slots, width), NARROW, FULL)] * 2 + [(head_shape + (width,), WIDE, FULL)] + weights_out(weights)
    scratch = [pltpu.VMEM((2 * slots, width), NARROW)] + head_scratch(width) + [
        pltpu.VMEM((2, rows, width), NARROW),
        pltpu.VMEM((rows, width), NARROW),
        pltpu.VMEM((rows, width), WIDE),
        pltpu.VMEM((LANES, rows), NARROW),
        pltpu.VMEM((8, LANES), WIDE),
        pltpu.VMEM((LANES + slots, rows), NARROW),
        pltpu.VMEM((LANES + slots, width), NARROW),
        pltpu.VMEM((2, slots, width), NARROW),
        pltpu.VMEM((slots, width), NARROW),
        pltpu.VMEM((slots, width), WIDE),
        pltpu.VMEM((LANES + slots, width), WIDE),
        pltpu.VMEM((8, LANES), WIDE),
    ]
    scratch += sums_scratch(kinds, slots, width)
    walk = Rows(rows, slots, 1024)
    return stage("last_layer", last_steps, walk, sel, ins, outs, scratch, 22 * rows * width * width)


def backward(make, walk, sel, rowed, drive, edges, hidden, halo, slots, is_last):
    rows, width = rowed[0].shape
    kinds = hidden.shape[0]
    outs = [((kinds, width, width), NARROW, FULL)] * 2 + [((8, width), WIDE, FULL)] * 2
    if is_last:
        outs += [((rows, width), NARROW, DOWN), ((slots, width), WIDE, FULL)]
    ins = [(a, DOWN if a.ndim == 2 else PICK) for a in rowed]
    ins += [(drive, ALONG if is_last else DOWN), (edges, ALONG), (hidden, UNDER)]
    if is_last:
        ins += [(a, FULL) for a in halo]
    else:
        ins += [(a, FULL if n == 0 else LATE_LEAD if n == 4 else LATE) for n, a in enumerate(halo)]
    scratch = sums_scratch(kinds, slots, width)
    return stage("rows_backward", make, walk, sel, ins, outs, scratch, (13 if is_last else 11) * rows * width * width)


def extras(count):
    return up(2 * count + 2, 16)


def put_pairs(extra, pieces):
    extra[...] = jnp.zeros_like(extra)
    at = 0
    for piece in pieces:
        top = piece.astype(NARROW).astype(WIDE)
        count = piece.shape[0]
        extra[at : at + count] = top
        extra[at + count : at + 2 * count] = piece - top
        at += 2 * count


def pack_kernel(has_rows, apart, sel, own_ref, got_ref, bo_ref, bg_ref, *refs):
    rows_ref, refs = (refs[0], refs[1:]) if has_rows else (None, refs)
    extra, outs = refs[-1], refs[:-1]
    kinds, far, near, shard, _ = own_ref.shape
    for j in range(near):
        out_ref, place = (outs[j], lax.bitwise_xor(sel[2], j)) if apart else (outs[0].at[j], j)
        for f in range(far):
            for k in range(kinds):
                value = own_ref[k, f, place].astype(WIDE) + got_ref[k, f, place].astype(WIDE)
                at = (f * kinds + k) * shard
                out_ref[at : at + shard] = value.astype(NARROW)
        bias = bo_ref[0:1] + bg_ref[0:1]
        put_pairs(extra, [bias] if rows_ref is None else [rows_ref[place], bias])
        out_ref[far * kinds * shard :] = extra[...].astype(NARROW)


def pack(sel, far, near, own, got, bias_own, bias_got, head_rows=None, apart=True):
    kinds, width, _ = own.shape
    shard = width // (far * near)
    count = 0 if head_rows is None else head_rows.shape[1]
    body = far * kinds * shard
    shape = (kinds, far, near, shard, width)
    if shard % 16:
        total = (own.astype(WIDE) + got.astype(WIDE)).reshape(shape).transpose(2, 1, 0, 3, 4).reshape(near, body, width)
        bias = bias_own[0:1] + bias_got[0:1]
        pieces = [total.astype(NARROW)]
        if count:
            pieces += list(halves(head_rows))
        pieces += [jnp.broadcast_to(h[None], (near, 1, width)) for h in halves(bias)]
        out = pad_rows(jnp.concatenate(pieces, 1), 16)
        if apart:
            out = by_place(out, sel[2], 0)
        return [out[j] for j in range(near)] if apart else out
    ins = [own.reshape(shape), got.reshape(shape), bias_own, bias_got] + ([head_rows] if count else [])
    shape = (body + extras(count), width)
    outs = [shape] * near if apart else [(near,) + shape]
    out = run(
        "pack",
        functools.partial(pack_kernel, count > 0, apart),
        sel,
        ins,
        [full(a.shape) for a in ins],
        [shape_of(a) for a in outs],
        [full(a) for a in outs],
        [pltpu.VMEM((extras(count), width), WIDE)],
        limit=16,
    )
    return out if apart else out[0]


def middle_kernel(far, body, share, near, apart, sel, *refs):
    outs, (total, extra) = refs[near:-2], refs[-2:]
    given = refs[:near] if near > 1 else [refs[0].at[j] for j in range(refs[0].shape[0])]
    value = given[0][...].astype(WIDE)
    for ref in given[1:]:
        value = value + ref[...].astype(WIDE)
    total[...] = value
    count = far * share
    at = far * body
    bias = total[at + 2 * count : at + 2 * count + 1] + total[at + 2 * count + 1 : at + 2 * count + 2]
    for f in range(far):
        out_ref = outs[f] if apart else outs[0].at[f]
        place = lax.bitwise_xor(sel[1], f) if apart else f
        out_ref[:body] = total[pl.ds(pl.multiple_of(place * body, body), body)].astype(NARROW)
        pieces = [bias]
        if share:
            mine = jnp.zeros((share, total.shape[1]), WIDE)
            for g in range(far) if apart else [f]:
                low = at + g * share
                piece = total[low : low + share] + total[low + count : low + count + share]
                mine = jnp.where(place == g, piece, mine) if apart else piece
            pieces = [mine, bias]
        put_pairs(extra, pieces)
        out_ref[body:] = extra[...].astype(NARROW)


def middle(sel, far, share, got, apart=False):
    got = got if isinstance(got, list) else [got]
    rows, width = got[0].shape[-2:]
    near = len(got)
    count = far * share
    body = (rows - extras(count)) // far
    if body % 16:
        total = sum(g.astype(WIDE) for g in got) if near > 1 else jnp.sum(got[0].astype(WIDE), 0)
        at = far * body
        pieces = [total[:at].reshape(far, body, width).astype(NARROW)]
        if share:
            value = total[at : at + count] + total[at + count : at + 2 * count]
            pieces += list(halves(value.reshape(far, share, width)))
        bias = total[at + 2 * count : at + 2 * count + 1] + total[at + 2 * count + 1 : at + 2 * count + 2]
        pieces += [jnp.broadcast_to(h[None], (far, 1, width)) for h in halves(bias)]
        out = jnp.concatenate(pieces, 1)
        out = jnp.pad(out, ((0, 0), (0, body + extras(share) - out.shape[1]), (0, 0)))
        if apart:
            out = by_place(out, sel[1], 0)
        return [out[f] for f in range(far)] if apart else out
    shape = (body + extras(share), width)
    outs = [shape] * far if apart else [(far,) + shape]
    out = run(
        "middle",
        functools.partial(middle_kernel, far, body, share, near, apart),
        sel,
        got,
        [full(a.shape) for a in got],
        [shape_of(a) for a in outs],
        [full(a) for a in outs],
        [pltpu.VMEM((rows, width), WIDE), pltpu.VMEM((extras(share), width), WIDE)],
        limit=16,
    )
    return out if apart else out[0]


def adamw(old, first, second, grad, rate):
    first_new = BETA * first + (1.0 - BETA) * grad
    second_new = BETA * second + (1.0 - BETA) * grad * grad
    step = first_new / (1.0 - BETA**STEP) / (jnp.sqrt(second_new / (1.0 - BETA**STEP)) + EPSA)
    return (old - rate * (step + DECAY * old), first_new, second_new)


def round_kernel(sel, value_ref, out_ref):
    out_ref[...] = value_ref[...].astype(NARROW)


def rounded(sel, value):
    count, rows, width = value.shape
    spec = pl.BlockSpec((1, rows, width), lambda i, s: (i, 0, 0))
    return run(
        "rounded", round_kernel, sel, [value], [spec], shape_of(value.shape), spec, limit=58, grid=(count,)
    )


def square_kernel(body, share, near, sel, *refs):
    given, (sum_ref, bias_ref, out_ref) = refs[:-3], refs[-3:]
    first, second = given[: len(given) // 2], given[len(given) // 2 :]
    total = jnp.zeros((1, 1), WIDE)
    rows = []
    for layer, (given, at) in enumerate(((first, body), (second, body + 2 * share))):
        value = given[0][...].astype(WIDE)
        for ref in given[1:]:
            value = value + ref[...].astype(WIDE)
        sum_ref[layer] = value[:body]
        rows.append(value[at : at + 1] + value[at + 1 : at + 2])
        total = total + jnp.sum(value[:body] * value[:body], keepdims=True)
    width = sum_ref.shape[2]
    shard = bias_ref.shape[1]
    place = (sel[1] * near + sel[2]) * shard
    rows = jnp.concatenate(rows + [jnp.zeros((8 - len(rows), width), WIDE)], 0)
    own = pltpu.roll(rows, lax.rem(width - place, width), 1)[:2, :shard]
    bias_ref[...] = own
    total = total + jnp.sum(own * own, keepdims=True)
    out_ref[...] = jnp.broadcast_to(total[None], out_ref.shape)


def squares_of(sel, first, second, body, share, near, shard, devices):
    width = second[0].shape[1]
    ins = list(first) + list(second)
    outs = [shape_of((2, body, width), WIDE), shape_of((2, shard), WIDE), shape_of((devices, 8, LANES), WIDE)]
    return run(
        "squares",
        functools.partial(square_kernel, body, share, near),
        sel,
        ins,
        [full(a.shape) for a in ins],
        outs,
        [full(o.shape) for o in outs],
        flops=2 * 10**10,
        limit=58,
    )


def stacked_halves(value):
    return jnp.concatenate(split(value), 0)


def turn_kernel(sel, value_ref, basis_ref, out_ref):
    for i in range(value_ref.shape[0]):
        both = dot(stacked_halves(value_ref[i]), basis_ref[i])
        out_ref[i] = both[: both.shape[0] // 2] + both[both.shape[0] // 2 :]


def turn(sel, value, basis):
    return run(
        "turn",
        turn_kernel,
        sel,
        [value, basis],
        [full(a.shape) for a in (value, basis)],
        shape_of(value.shape, WIDE),
        full(value.shape),
        limit=58,
    )


def update_kernel(
    sel, turned_ref, parts_ref, head_sq_ref, weight_ref, loss_ref, basis_ref, old_ref, first_ref, second_ref,
    bias_ref, b_old_ref, b_first_ref, b_second_ref, grad_ref, h_old_ref, h_first_ref, h_second_ref,
    norm_ref, pair_ref, new_ref, low_ref, m_ref, v_ref, bn_ref, bm_ref, bv_ref, hn_ref, hm_ref, hv_ref,
):
    squares = jnp.sum(parts_ref[...], axis=0)[0:1, 0:1] + head_sq_ref[...]
    norm = jnp.sqrt(squares) / weight_ref[...]
    norm_ref[...] = norm
    pair_ref[...] = jnp.where(lax.broadcasted_iota(jnp.int32, (1, 2), 1) == 0, loss_ref[...], weight_ref[...])
    factor = jnp.minimum(1.0, CLIP / norm) / weight_ref[...]
    bn_ref[...], bm_ref[...], bv_ref[...] = adamw(
        b_old_ref[...], b_first_ref[...], b_second_ref[...], bias_ref[...] * factor, LR_BIAS
    )
    hn_ref[...], hm_ref[...], hv_ref[...] = adamw(
        h_old_ref[...], h_first_ref[...], h_second_ref[...], grad_ref[...] * factor, LR_HEAD
    )
    for i in range(turned_ref.shape[0]):
        grad = turned_ref[i] * factor
        first = BETA * first_ref[i] + (1.0 - BETA) * grad
        second = BETA * second_ref[i] + (1.0 - BETA) * grad * grad
        m_ref[i] = first
        v_ref[i] = second
        step = first / (1.0 - BETA**STEP) / (jnp.sqrt(second / (1.0 - BETA**STEP)) + EPSA)
        both = dot_nt(stacked_halves(step), basis_ref[i])
        back = both[: both.shape[0] // 2] + both[both.shape[0] // 2 :]
        new = old_ref[i] - LR_MAT * (back + DECAY * old_ref[i])
        new_ref[i] = new
        low_ref[i] = new.astype(NARROW)


def update(sel, *ins):
    mats, bias, head = ins[6], ins[10], ins[14]
    outs = [shape_of((1, 1), WIDE), shape_of((1, 2), WIDE), shape_of(mats.shape, WIDE), shape_of(mats.shape)]
    outs += [shape_of(mats.shape, WIDE)] * 2 + [shape_of(bias.shape, WIDE)] * 3 + [shape_of(head.shape, WIDE)] * 3
    return run(
        "update", update_kernel, sel, ins, [full(a.shape) for a in ins], outs, [full(o.shape) for o in outs], limit=58
    )


def local(
    far,
    near,
    node_states,
    serve,
    neighbors,
    alpha,
    live,
    lam,
    labels,
    link_pair,
    mats,
    mats_m,
    mats_v,
    basis,
    bias,
    bias_m,
    bias_v,
    head,
    head_m,
    head_v,
):
    n = far * near
    branch = lax.axis_index("branch")
    both = ("far", "near")
    rows_dev, width = node_states.shape[1:]
    classes = head.shape[1]
    depth, kinds, _, shard, _ = mats.shape
    slots = serve.shape[1]
    cap = slots // n
    walk = Rows(rows_dev, slots)

    def pick(value):
        return lax.dynamic_index_in_dim(value, branch, 0, keepdims=False)

    def swap(value):
        return lax.ppermute(value, "branch", SWAP)

    def exchange(value, axes):
        return lax.all_to_all(value, axes, 0, 0, tiled=True)

    def hop(value, axis, size, k):
        return lax.ppermute(value, axis, [(i, i ^ k) for i in range(size)]) if k else value

    def spread(rows, count):
        return jnp.broadcast_to(rows[None], (count,) + rows.shape)

    places = (branch, lax.axis_index("far"), lax.axis_index("near"))
    sel = jnp.stack([p.astype(jnp.int32) for p in places])

    low = mats.astype(NARROW).reshape(depth, kinds, shard, width)

    def along_far():
        parts = [hop(low, "far", far, k) for k in range(far)]
        return [jnp.stack([part[layer] for part in parts]) for layer in range(depth)]

    def along_near(pieces):
        return [hop(pieces, "near", near, k) for k in range(near)]

    def join(own):
        other = [swap(piece) for piece in own]
        return list(own) + other if walk.whole and shard % 16 == 0 else assemble(sel, own, other)

    far_0, far_1 = along_far()

    send = take_rows(sel, node_states, serve, bias, n)
    far_0, send = lax.optimization_barrier((far_0, send))
    got = exchange(send, both)
    near_0 = along_near(far_0)
    near_0[1], serve, branch, head = lax.optimization_barrier((near_0[1], serve, branch, head))
    edges, edges_s = make_edges(sel, neighbors.transpose(0, 2, 1), alpha.transpose(0, 2, 1), serve)
    slots_0 = got[:, :cap].reshape(slots, width)
    own_bias = got[:, cap, : depth * shard].reshape(n, depth, shard).transpose(1, 0, 2).reshape(depth, width)
    other_bias = swap(own_bias)
    first = branch == 0
    biases = jnp.stack([jnp.where(first, own_bias, other_bias), jnp.where(first, other_bias, own_bias)], 1)
    biases = biases.astype(WIDE)
    agg = lax.dot_general(edges_s, twice(slots_0), (((0,), (0,)), ((), ())), preferred_element_type=WIDE)
    agg, near_0 = lax.optimization_barrier((agg, near_0))
    agg_0 = exchange(agg.astype(NARROW), both)
    weights = [join(near_0)]
    weights[0], far_1 = lax.optimization_barrier((weights[0], far_1))
    near_1 = along_near(far_1)
    share = -(-(classes + 1) // n)
    sel = jnp.concatenate([sel, pick(live)])

    h_h0, slots_1, m_h0, agg, weights[0] = halo_forward(sel, slots_0, agg_0, weights[0], biases[0], edges_s)
    agg, edges = lax.optimization_barrier((agg, edges))
    agg_1 = exchange(agg, both)
    h_0, x_1, m_0 = forward(walk, sel, node_states, edges, slots_0, weights[0], biases[0])
    near_1, x_1, agg_1 = lax.optimization_barrier((near_1, x_1, agg_1))
    weights.append(join(near_1))
    own_1, other_1, bias_1, bias_x1, d_x, spread_1, ds_h1, dn_h1, head_rows, weights[1] = last_layer(
        walk, sel, (near, far * share), x_1, edges, slots_1, weights[1], biases[1], (head.T, labels, lam), link_pair,
        agg_1,
    )
    returned = exchange(dn_h1, both)

    packed = pack(sel, far, near, own_1, swap(other_1), bias_1, swap(bias_x1), head_rows)
    *packed, spread_1 = lax.optimization_barrier((*packed, spread_1))
    sums_1 = [hop(piece, "near", near, k) for k, piece in enumerate(packed)]
    own_0, other_0, bias_0, bias_x0 = backward(
        back_first_step, walk, sel, [x_1, m_0, node_states], d_x, edges, h_0,
        [weights[0], h_h0, slots_0, agg_0, weights[1], spread_1, edges_s, returned, ds_h1, slots_1, m_h0],
        slots, False,
    )
    own_0, other_0, bias_x0, sums_1 = lax.optimization_barrier((own_0, other_0, bias_x0, sums_1))
    packed = pack(sel, far, near, own_0, swap(other_0), bias_0, swap(bias_x0), apart=False)
    packed, sums_1 = lax.optimization_barrier((packed, sums_1))
    sums_0 = exchange(packed, "near")
    body = kinds * shard
    parts_1 = [hop(piece, "far", far, k) for k, piece in enumerate(middle(sel, far, share, sums_1, True))]
    mine = sum(piece[body : body + 2 * share].astype(WIDE) for piece in parts_1)
    mine = mine[:share] + mine[share:]
    low_basis = rounded(sel, basis.reshape(depth * kinds, width, width))
    mine, sums_0, low_basis = lax.optimization_barrier((mine, sums_0, low_basis))
    send = pad_rows(jnp.concatenate(halves(mine + swap(mine)), 0), 8)
    parts_0 = [hop(piece, "far", far, k) for k, piece in enumerate(middle(sel, far, 0, sums_0, True))]

    whole = exchange(spread(send, n), both).astype(WIDE)
    head_sum = (whole[:, :share] + whole[:, share : 2 * share]).reshape(far, near, share, width)
    head_sum = head_sum.transpose(1, 0, 2, 3).reshape(n * share, width)
    stats = head_sum[classes : classes + 1]
    loss_sum = stats[:, classes : classes + 1]
    weight_sum = stats[:, classes + 1 : classes + 2]
    sum_head = jnp.concatenate([head_sum[:classes], stats[:, :classes].T], 1)
    head_squares = jnp.sum(sum_head * sum_head, keepdims=True)

    sums, sum_bias, squares = squares_of(sel, parts_0, parts_1, body, share, near, shard, 2 * n)
    squares = exchange(squares, both + ("branch",))
    flat = (depth * kinds, shard, width)
    sums, sum_head = lax.optimization_barrier((sums, sum_head))
    turned = turn(sel, sums.reshape(flat), low_basis)
    norm, loss_parts, mats_new, mats_low, first_new, second_new, *small = update(
        sel, turned, squares, head_squares, weight_sum, loss_sum, low_basis,
        *(a.reshape(flat) for a in (mats, mats_m, mats_v)),
        sum_bias, *(a.reshape(depth, shard) for a in (bias, bias_m, bias_v)),
        sum_head, *(a.T for a in (head, head_m, head_v)),
    )
    return (
        loss_parts[0],
        norm[0, 0],
        *(a.reshape(mats.shape) for a in (mats_new, mats_low, first_new, second_new)),
        *(a.reshape(bias.shape) for a in small[:3]),
        *(a.T for a in small[3:]),
    )


def solution(mesh):
    n = mesh.shape["rows"]
    near = 1 << (n.bit_length() // 2)
    far = n // near
    grid = Mesh(mesh.devices.reshape(far, near, 2), ("far", "near", "branch"))
    rows = ("far", "near")
    by_row = P(None, rows)
    by_row_last = P(None, rows, None)
    matrix = P(None, None, "branch", rows, None)
    vector = P(None, "branch", rows)
    return jax.shard_map(
        functools.partial(local, far, near),
        mesh=grid,
        in_specs=(by_row_last, by_row, by_row_last, by_row_last)
        + (by_row,) * 4
        + (matrix,) * 3
        + (P(None, None, "branch", None, None),)
        + (vector,) * 3
        + (P(),) * 3,
        out_specs=(P(), P()) + (matrix,) * 4 + (vector,) * 3 + (P(),) * 3,
        check_vma=False,
    )
```

```python
import functools

import jax
import jax.numpy as jnp
from jax import lax
from jax.experimental import pallas as pl
from jax.experimental.pallas import tpu as pltpu
from jax.sharding import Mesh
from jax.sharding import PartitionSpec as P

STEP = 5
LINK = 4.0
CLIP = 0.001
EPSN = 1e-06
BETA = 0.5
EPSA = 1e-08
LR_MAT = 0.02
LR_BIAS = 0.05
LR_HEAD = 0.02
DECAY = 0.01
HIGH = lax.Precision.HIGHEST
WIDE = jnp.float32
NARROW = jnp.bfloat16
GELU_A = 0.7978845608028654
GELU_B = 0.044715
LANES = 128
SWAP = [(0, 1), (1, 0)]


def halves(value):
    top = lax.reduce_precision(value, 8, 7)
    return top.astype(NARROW), (value - top).astype(NARROW)


def up(value, unit):
    return -(-value // unit) * unit


def pad_rows(rows, unit):
    extra = -rows.shape[-2] % unit
    return jnp.pad(rows, [(0, 0)] * (rows.ndim - 2) + [(0, extra), (0, 0)])


def split(value):
    top = value.astype(NARROW)
    return top, (value - top.astype(WIDE)).astype(NARROW)


def dot(left, right):
    return lax.dot_general(left, right, (((1,), (0,)), ((), ())), preferred_element_type=WIDE)


def dot_nt(left, right):
    return lax.dot_general(left, right, (((1,), (1,)), ((), ())), preferred_element_type=WIDE)


def dot_tn(left, right):
    return lax.dot_general(left, right, (((0,), (0,)), ((), ())), preferred_element_type=WIDE)


def unit_rows(pre):
    sq = pre * pre
    gate = 0.5 + 0.5 * jnp.tanh(pre * (GELU_A + GELU_A * GELU_B * sq))
    slope = gate * (1.0 + pre * (1.0 - gate) * (2.0 * GELU_A + 6.0 * GELU_A * GELU_B * sq))
    act = pre * gate
    inv = lax.rsqrt(jnp.sum(act * act, axis=1, keepdims=True) + EPSN)
    return (act * inv).astype(NARROW), slope * inv


def pull_rows(d_out, out, slope):
    wide = out.astype(WIDE)
    along = jnp.sum(wide * d_out, axis=1, keepdims=True)
    return (slope.astype(WIDE) * (d_out - wide * along)).astype(NARROW)


def full(shape):
    return pl.BlockSpec(shape, lambda *_: (0,) * len(shape))


def when(flag, body):
    if isinstance(flag, bool):
        if flag:
            body()
    else:
        pl.when(flag)(body)


class Rows:
    def __init__(self, rows, slots, tile=512):
        self.rows = rows
        self.whole = slots <= 256
        self.tile = min(rows, tile)
        self.count = rows // self.tile

    def at(self, i):
        return pl.ds(i * self.tile, self.tile)

    def down(self, ref, i):
        return ref.at[self.at(i)] if self.whole else ref

    def along(self, ref, i):
        return ref.at[:, self.at(i)] if self.whole else ref

    def under(self, ref, i):
        return ref.at[:, self.at(i)] if self.whole else ref

    def part(self, kind, ref, i):
        return ref if kind in ONCE else ref.at[self.at(i)] if kind in (DOWN, PICK) else ref.at[:, self.at(i)]

    def source(self, kind, ref, i, sel):
        return ref.at[:, 0] if kind in (LEAD, LATE_LEAD) else self.part(kind, ref.at[sel[0]] if kind == PICK else ref, i)

    def held(self, kind, shape):
        return shape[1:] if kind == PICK else shape[:1] + shape[2:] if kind in (LEAD, LATE_LEAD) else shape

    def spec(self, kind, shape):
        if kind in (FULL, LATE):
            return full(shape)
        if kind in (LEAD, LATE_LEAD):
            return pl.BlockSpec((shape[0], None) + shape[2:], lambda *_: (0,) * len(shape))
        if kind == PICK:
            return pl.BlockSpec((None, self.tile, shape[2]), lambda i, s: (s[0], i, 0))
        if kind == DOWN:
            return pl.BlockSpec((self.tile,) + shape[1:], lambda i, s: (i, 0))
        if kind == ALONG:
            return pl.BlockSpec((shape[0], self.tile), lambda i, s: (0, i))
        return pl.BlockSpec((shape[0], self.tile, shape[2]), lambda i, s: (0, i, 0))


FULL, DOWN, ALONG, UNDER, PICK, LEAD, PIECES, AGAIN, LATE, LATE_LEAD = range(10)
ONCE = (FULL, LEAD, PIECES, AGAIN, LATE, LATE_LEAD)


def grid_kernel(make, walk, n_in, n_out, sel, *refs):
    i = pl.program_id(0)
    make(walk, sel, *refs)(i, i == 0, i == walk.count - 1)


def piece_copies(sel, refs, out_ref):
    near = len(refs) // 2
    far, kinds, shard, _ = refs[0].shape
    pairs = []
    for half in range(2):
        slot = sel[0] if half == 0 else 1 - sel[0]
        for j in range(near):
            for f in range(far):
                place = lax.bitwise_xor(sel[1], f) * near + lax.bitwise_xor(sel[2], j)
                at = pl.ds(pl.multiple_of(place * shard, shard), shard)
                pairs += [(refs[half * near + j].at[f, k], out_ref.at[slot, k, at]) for k in range(kinds)]
    return pairs


def copy_kernel(make, walk, kinds, sizes, n_in, sel, *refs):
    count = len(kinds)
    far, at = [], 0
    for size in sizes:
        far.append(refs[at : at + size])
        at += size
    held = [k for k in range(count) if kinds[k] != AGAIN]
    near = dict(zip(held, refs[at : at + len(held)]))
    steps = make(walk, sel, *near.values(), *refs[at + len(held) : -1])
    steps = steps if isinstance(steps, list) else [steps]
    sems = refs[-1]
    used = [0]

    def copies(k, i):
        kind = kinds[k]
        if kind == PIECES:
            pairs = piece_copies(sel, far[k], near[k])
        elif kind == AGAIN:
            pairs = [(near[kinds.index(PIECES)], far[k][0])]
        else:
            pair = (walk.source(kind, far[k][0], i, sel), walk.part(kind, near[k], i))
            pairs = [pair if k < n_in else pair[::-1]]
        used[0] += len(pairs)
        return [
            pltpu.make_async_copy(*pair, sems.at[used[0] - len(pairs) + n]) for n, pair in enumerate(pairs)
        ]

    def wanted(i, given):
        chosen = []
        for k in given:
            late = k >= n_in or kinds[k] in (LATE, LATE_LEAD)
            if kinds[k] not in ONCE or i == (walk.count - 1 if late else 0):
                chosen += copies(k, i)
        return chosen

    loads = [wanted(i, range(n_in)) for i in range(walk.count)]
    ahead = 2
    for group in loads[:ahead]:
        for item in group:
            item.start()
    stores = []
    results = [k for k in range(n_in, count) if kinds[k] != AGAIN]
    for n, step in enumerate(steps):
        for i in range(walk.count):
            for item in loads[i] if n == 0 else []:
                item.wait()
            for item in loads[i + ahead] if n == 0 and i + ahead < walk.count else []:
                item.start()
            if n == 0 and i == 0:
                stores = [item for k in range(n_in, count) if kinds[k] == AGAIN for item in copies(k, i)]
                for item in stores:
                    item.start()
            step(i, i == 0, i == walk.count - 1)
            for item in wanted(i, results) if n == len(steps) - 1 else []:
                item.start()
                stores.append(item)
    for item in stores:
        item.wait()


def run(name, kernel, sel, ins, in_specs, outs, out_specs, scratch=(), flops=0, limit=20, grid=(), size=None):
    if size is None:
        size = sum(a.size * a.dtype.itemsize for a in ins)
        size += sum(o.size * o.dtype.itemsize for o in (outs if isinstance(outs, list) else [outs]))
    return pl.pallas_call(
        kernel,
        out_shape=outs,
        grid_spec=pltpu.PrefetchScalarGridSpec(
            num_scalar_prefetch=1,
            grid=grid,
            in_specs=in_specs,
            out_specs=out_specs,
            scratch_shapes=list(scratch),
        ),
        compiler_params=pltpu.CompilerParams(
            dimension_semantics=("arbitrary",) * len(grid), vmem_limit_bytes=limit << 20
        ),
        name=name,
        cost_estimate=pl.CostEstimate(flops=flops, bytes_accessed=size, transcendentals=0),
    )(sel, *ins)


def stage(name, make, walk, sel, ins, outs, scratch=(), flops=0):
    kinds = [k for _, k in ins] + [k for *_, k in outs]
    groups = [a if isinstance(a, list) else [a] for a, _ in ins]
    arrays = [a for group in groups for a in group]
    shapes = [shape_of(shape, dtype) for shape, dtype, _ in outs]
    n_in = len(ins)
    if not walk.whole:
        specs = [walk.spec(k, a.shape) for k, a in zip(kinds, arrays + shapes)]
        return run(
            name, functools.partial(grid_kernel, make, walk, n_in, len(outs)),
            sel, arrays, specs[:n_in], shapes, specs[n_in:], scratch, flops, 58, (walk.count,),
        )
    held, copies = [], 0
    for kind, group in zip(kinds, groups + [[a] for a in shapes]):
        shape = group[0].shape
        if kind == PIECES:
            far, parts, shard, width = shape
            shape = (2, parts, width, width)
            copies += len(group) * far * parts
        else:
            copies += 1 if kind in ONCE else walk.count
        if kind != AGAIN:
            held.append(pltpu.VMEM(walk.held(kind, shape), group[0].dtype))
    hbm = pl.BlockSpec(memory_space=pltpu.HBM)
    free = pl.BlockSpec(memory_space=pl.ANY)
    small = 300_000
    specs = [
        free if kind == PIECES or (kind in (FULL, LATE) and a.size * a.dtype.itemsize < small) else hbm
        for kind, group in zip(kinds, groups)
        for a in group
    ]
    return run(
        name, functools.partial(copy_kernel, make, walk, kinds, [len(g) for g in groups] + [1] * len(outs), n_in),
        sel, arrays, specs, shapes, [hbm] * len(outs),
        held + list(scratch) + [pltpu.SemaphoreType.DMA((copies,))], flops, 58,
    )


def shape_of(shape, dtype=NARROW):
    return jax.ShapeDtypeStruct(shape, dtype)


def serve_kernel(sel, states_ref, serve_ref, bias_ref, out_ref, held, sems):
    me = sel[0]
    part = held.shape[1]
    copies = []
    for i in range(held.shape[0]):
        copies.append(pltpu.make_async_copy(states_ref.at[me, pl.ds(i * part, part)], held.at[i], sems.at[i]))
        copies[-1].start()
    serve = serve_ref[pl.ds(me, 1)]
    row = lax.broadcasted_iota(jnp.int32, (part, serve.shape[1]), 0)
    total = None
    for i, copy in enumerate(copies):
        copy.wait()
        one = jnp.where(row == serve - i * part, 1.0, 0.0).astype(NARROW)
        value = dot_tn(one, held[i])
        total = value if total is None else total + value
    cap = serve.shape[1] // out_ref.shape[0]
    depth, _, shard = bias_ref.shape
    bias = jnp.zeros((8, out_ref.shape[2]), WIDE)
    for layer in range(depth):
        spot = lax.broadcasted_iota(jnp.int32, (shard, out_ref.shape[2]), 1)
        here = spot == lax.broadcasted_iota(jnp.int32, spot.shape, 0) + layer * shard
        row = jnp.broadcast_to(bias_ref[layer].astype(NARROW), (8, shard))
        bias = bias + dot(row, jnp.where(here, 1.0, 0.0).astype(NARROW))
    for d in range(out_ref.shape[0]):
        out_ref[d] = jnp.concatenate([total[d * cap : (d + 1) * cap], bias], 0).astype(NARROW)


def take_rows(sel, node_states, serve, bias, n):
    _, rows, width = node_states.shape
    shape = (n, serve.shape[1] // n + 8, width)
    return run(
        "serve",
        serve_kernel,
        sel,
        (node_states, serve, bias),
        [pl.BlockSpec(memory_space=pltpu.HBM), full(serve.shape), full(bias.shape)],
        shape_of(shape),
        full(shape),
        [pltpu.VMEM((4, rows // 4, width), NARROW), pltpu.SemaphoreType.DMA((4,))],
        limit=58,
    )


def edge_kernel(sel, nbr_ref, alpha_ref, serve_ref, out_ref, served_ref, total):
    me = sel[0]
    slots = served_ref.shape[1]
    rows = nbr_ref.shape[2]
    tile = min(rows, 512)
    total[...] = jnp.zeros_like(total)
    lane = lax.broadcasted_iota(jnp.int32, (slots, tile), 0)
    row = lax.broadcasted_iota(jnp.int32, (tile, slots), 0)

    def step(i, carry):
        at = pl.ds(pl.multiple_of(i * tile, tile), tile)
        nbr, alpha = nbr_ref[me, :, at], alpha_ref[me, :, at]
        value = jnp.zeros((slots, tile), WIDE)
        for k in range(nbr.shape[0]):
            value = value + jnp.where(nbr[k : k + 1] == lane, alpha[k : k + 1], 0.0)
        top, rest = split(value)
        out_ref[:slots, at] = top
        out_ref[slots:, at] = rest
        one = jnp.where(row == serve_ref[pl.ds(me, 1)] - i * tile, 1.0, 0.0).astype(NARROW)
        total[...] += dot(out_ref[:, at], one)
        return carry

    lax.fori_loop(0, rows // tile, step, 0)
    served_ref[...] = total[...].astype(NARROW)


def make_edges(sel, neighbors, alpha, serve):
    _, deg, rows = neighbors.shape
    slots = serve.shape[1]
    shapes = [(2 * slots, rows), (2 * slots, slots)]
    return run(
        "edges",
        edge_kernel,
        sel,
        (neighbors, alpha, serve),
        [full(neighbors.shape), full(alpha.shape), full(serve.shape)],
        [shape_of(a) for a in shapes],
        [full(a) for a in shapes],
        [pltpu.VMEM((2 * slots, slots), WIDE)],
        flops=5 * 10**9,
        limit=16 if slots <= 256 else 56,
    )


def by_place(value, me, axis):
    count = value.shape[axis]
    return jnp.concatenate(
        [lax.dynamic_slice_in_dim(value, lax.bitwise_xor(me, i), 1, axis) for i in range(count)], axis
    )


def twice(rows):
    return jnp.concatenate([rows, rows], 0)


def assemble(sel, own, other):
    near = len(own)
    far, kinds, shard, width = own[0].shape
    own, other = (by_place(by_place(jnp.stack(w), sel[2], 0), sel[1], 1).transpose(2, 1, 0, 3, 4) for w in (own, other))
    first = sel[0] == 0
    both = jnp.stack([jnp.where(first, own, other), jnp.where(first, other, own)])
    return both.reshape(2, kinds, far * near * shard, width)


def layer_rows(x, sums, w_ref, b_ref, h_ref):
    hs = (dot(x, w_ref[0, 0]) + b_ref[0:1]).astype(NARROW)
    hn = (sums + b_ref[1:2]).astype(NARROW)
    h_ref[0] = hs
    h_ref[1] = hn
    return unit_rows(dot(hs, w_ref[0, 1]) + dot(hn, w_ref[1, 1]))


def halo_step(walk, sel, x_ref, agg_ref, w_ref, b_ref, e_ref, h_ref, y_ref, m_ref, next_ref):
    def step(i, first, last):
        y, m = layer_rows(x_ref[...], dot(agg_ref[...], w_ref[1, 0]), w_ref, b_ref, h_ref)
        y_ref[...] = y
        m_ref[...] = m
        next_ref[...] = dot_tn(e_ref[...], twice(y)).astype(NARROW)

    return step


def weights_in(weights):
    return (weights, PIECES if isinstance(weights, list) else FULL)


def weights_out(weights):
    if not isinstance(weights, list):
        return []
    _, kinds, _, width = weights[0].shape
    return [((2, kinds, width, width), NARROW, AGAIN)]


def halo_forward(sel, x, agg, weights, bias, edges_s):
    slots, width = x.shape
    walk = Rows(slots, slots)
    walk.tile, walk.count = slots, 1
    ins = [(x, FULL), (agg, FULL), weights_in(weights), (bias, FULL), (edges_s, FULL)]
    outs = [((2, slots, width), NARROW, FULL), ((slots, width), NARROW, FULL), ((slots, width), WIDE, FULL)]
    outs += [((slots, width), NARROW, FULL)] + weights_out(weights)
    out = stage("halo", halo_step, walk, sel, ins, outs, flops=10 * slots * width * width)
    return (*out[:4], out[4] if isinstance(weights, list) else weights)


def own_row(walk, sel, ref, i):
    return ref[pl.ds(sel[0], 1), pl.ds(i * walk.tile if walk.whole else pl.multiple_of(i * walk.tile, LANES), walk.tile)]


def node_weights(walk, sel, lam_ref, i):
    node = lax.broadcasted_iota(jnp.int32, (1, walk.tile), 1) + i * walk.tile
    return jnp.where(node < sel[3], own_row(walk, sel, lam_ref, i), 0.0)


def forward_step(walk, sel, x_ref, e_ref, s_ref, w_ref, b_ref, *refs):
    has_head = len(refs) > 4
    if has_head:
        head_ref, label_ref, lam_ref, h_ref, y_ref, m_ref, dl_ref, st_ref, table, class_ref, hb_ref = refs
        classes, width = head_ref.shape[0], head_ref.shape[1] - 1
    else:
        h_ref, y_ref, m_ref, table = refs

    def step(i, first, last):
        @functools.partial(when, first)
        def _():
            table[...] = twice(dot(s_ref[...], w_ref[1, 0]).astype(NARROW))
            if has_head:
                st_ref[...] = jnp.zeros_like(st_ref)
                class_ref[...] = jnp.zeros_like(class_ref)
                class_ref[:classes] = head_ref[:, :width].astype(NARROW)
                hb_ref[...] = jnp.full_like(hb_ref, -1e30)
                hb_ref[:classes] = head_ref[:, width:]

        sums = dot_tn(walk.along(e_ref, i)[...], table[...])
        y, m = layer_rows(walk.down(x_ref, i)[...], sums, w_ref, b_ref, walk.under(h_ref, i))
        walk.down(y_ref, i)[...] = y
        walk.down(m_ref, i)[...] = m.astype(m_ref.dtype)
        if has_head:
            logits = dot_nt(class_ref[...], y) + hb_ref[...]
            label, weight = own_row(walk, sel, label_ref, i), node_weights(walk, sel, lam_ref, i)
            hit = lax.broadcasted_iota(jnp.int32, logits.shape, 0) == label
            top = jnp.max(logits, axis=0, keepdims=True)
            power = jnp.exp(logits - top)
            total = jnp.sum(power, axis=0, keepdims=True)
            picked = jnp.sum(jnp.where(hit, logits, 0.0), axis=0, keepdims=True)
            cross = top + jnp.log(total) - picked
            dl = (power * (weight / total) - jnp.where(hit, weight, 0.0)).astype(NARROW)
            walk.along(dl_ref, i)[...] = dl
            ones = jnp.ones((8, walk.tile), NARROW)
            st_ref[0:1] += jnp.broadcast_to(jnp.sum(weight * cross, axis=1, keepdims=True), (1, LANES))
            st_ref[1:2] += dot_nt(ones, dl)[0:1]
            st_ref[2:3] += jnp.broadcast_to(jnp.sum(weight, axis=1, keepdims=True), (1, LANES))

    return step


def head_scratch(width):
    return [pltpu.VMEM((LANES, width), NARROW), pltpu.VMEM((LANES, 1), WIDE)]


def forward(walk, sel, x, edges, slot_rows, weights, bias, head=None):
    rows, width = x.shape[-2:]
    slots = slot_rows.shape[0]
    ins = [(x, DOWN if x.ndim == 2 else PICK), (edges, ALONG), (slot_rows, FULL), (weights, FULL), (bias, FULL)]
    outs = [((2, rows, width), NARROW, UNDER)] + [((rows, width), NARROW, DOWN)] * 2
    if head is not None:
        ins += [(a, FULL) for a in head]
        outs += [((LANES, rows), NARROW, ALONG), ((8, LANES), WIDE, FULL)]
    scratch = [pltpu.VMEM((2 * slots, width), NARROW)] + (head_scratch(width) if head is not None else [])
    return stage("rows_forward", forward_step, walk, sel, ins, outs, scratch, 7 * rows * width * width)


def link_step(
    walk, sel, x_ref, agg_ref, w_ref, b_ref, head_ref, st_ref, lam_ref, pair_ref, y_ref, dl_ref,
    d_ref, hl_ref, h_ref, dz_ref, ds_ref, dn_ref, hr_ref, slope, sums, extra,
):
    classes, width = head_ref.shape[0], head_ref.shape[1] - 1

    def step(i, first, last):
        @functools.partial(when, first)
        def _():
            y, m = layer_rows(x_ref[...], dot(agg_ref[...], w_ref[1, 0]), w_ref, b_ref, h_ref)
            hl_ref[:LANES] = jnp.zeros((LANES, width), NARROW)
            hl_ref[:classes] = head_ref[:, :width].astype(NARROW)
            hl_ref[LANES:] = y
            slope[...] = m
            sums[...] = jnp.zeros_like(sums)
            extra[...] = jnp.zeros_like(extra)

        y = walk.down(y_ref, i)[...]
        near = dot_nt(hl_ref[LANES:], y)
        weight, pair = node_weights(walk, sel, lam_ref, i), own_row(walk, sel, pair_ref, i)
        hit = lax.broadcasted_iota(jnp.int32, near.shape, 0) == pair
        arg = -LINK * jnp.sum(jnp.where(hit, near, 0.0), axis=0, keepdims=True)
        small = jnp.exp(-jnp.abs(arg))
        soft = jnp.maximum(arg, 0.0) + jnp.log(1.0 + small)
        sigmoid = jnp.where(arg >= 0.0, 1.0, small) / (1.0 + small)
        extra[0:1] += jnp.broadcast_to(jnp.sum(weight * soft, axis=1, keepdims=True), (1, LANES))
        d_score = -LINK * weight * sigmoid
        d_at = walk.along(d_ref, i)
        d_at[:LANES] = walk.along(dl_ref, i)[...]
        d_at[LANES:] = jnp.where(hit, d_score, 0.0).astype(NARROW)
        sums[...] += dot(d_at[...], y)

        @functools.partial(when, last)
        def _():
            dz = pull_rows(sums[LANES:], hl_ref[LANES:], slope[...])
            dz_ref[...] = dz
            ds_ref[...] = dot_nt(dz, w_ref[0, 1]).astype(NARROW)
            dn_ref[...] = dot_nt(dz, w_ref[1, 1]).astype(NARROW)
            lane = lax.broadcasted_iota(jnp.int32, (1, LANES), 1)
            row = jnp.where(lane < classes, st_ref[1:2], 0.0)
            row = jnp.where(lane == classes, st_ref[0:1] + extra[0:1], row)
            row = jnp.where(lane == classes + 1, st_ref[2:3], row)
            sums[classes : classes + 1, :LANES] = row
            for j in range(hr_ref.shape[0]):
                hr_ref[j] = sums[j * hr_ref.shape[1] : (j + 1) * hr_ref.shape[1]]

    return step


def link(walk, sel, head_shape, x, agg, weights, bias, head_t, stats, lam, pair, y, d_logits):
    slots, width = x.shape
    rows = y.shape[0]
    ins = [(a, FULL) for a in (x, agg, weights, bias, head_t, stats, lam, pair)]
    ins += [(y, DOWN), (d_logits, ALONG)]
    outs = [((LANES + slots, rows), NARROW, ALONG), ((LANES + slots, width), NARROW, FULL)]
    outs += [((2, slots, width), NARROW, FULL)] + [((slots, width), NARROW, FULL)] * 3
    outs += [(head_shape + (width,), WIDE, FULL)]
    scratch = [
        pltpu.VMEM((slots, width), WIDE),
        pltpu.VMEM((LANES + slots, width), WIDE),
        pltpu.VMEM((8, LANES), WIDE),
    ]
    flops = 6 * rows * slots * width + 12 * slots * width * width
    return stage("link", link_step, walk, sel, ins, outs, scratch, flops)


def add_sums(sums, dz, h, x, edges, w_ref):
    acc, bias_acc, spread_acc = sums
    acc[0, 1] += dot_tn(h[0], dz)
    acc[1, 1] += dot_tn(h[1], dz)
    ds = dot_nt(dz, w_ref[0, 1]).astype(NARROW)
    dn = dot_nt(dz, w_ref[1, 1]).astype(NARROW)
    acc[0, 0] += dot_tn(x, ds)
    spread_acc[...] += dot(edges, dn)
    bias_acc[0:1] += jnp.sum(ds.astype(WIDE), axis=0, keepdims=True)
    bias_acc[1:2] += jnp.sum(dn.astype(WIDE), axis=0, keepdims=True)
    return ds


def more_sums(sums, dz, h_ref, x, agg, ds, dn):
    acc, bias_acc, _ = sums
    acc[0, 1] += dot_tn(h_ref[0], dz)
    acc[1, 1] += dot_tn(h_ref[1], dz)
    acc[0, 0] += dot_tn(x, ds)
    acc[1, 0] += dot_tn(agg, dn)
    bias_acc[0:1] += jnp.sum(ds.astype(WIDE), axis=0, keepdims=True)
    bias_acc[1:2] += jnp.sum(dn.astype(WIDE), axis=0, keepdims=True)


def finish_sums(me, sums, table, own_ref, other_ref, bo_ref, bx_ref):
    acc, bias_acc, spread_acc = sums
    slots = table.shape[0]
    spread = spread_acc[:slots] + spread_acc[slots:]
    top, rest = split(spread)
    acc[1, 0] += dot_tn(table, top) + dot_tn(table, rest)
    own_ref[...] = acc[me].astype(NARROW)
    other_ref[...] = acc[1 - me].astype(NARROW)
    bo_ref[...] = jnp.broadcast_to(bias_acc[pl.ds(me, 1)], bo_ref.shape)
    bx_ref[...] = jnp.broadcast_to(bias_acc[pl.ds(1 - me, 1)], bx_ref.shape)
    return spread


def back_last_step(
    walk, sel, y_ref, m_ref, x_ref, d_ref, e_ref, h_ref,
    hl_ref, w_ref, hh_ref, xh_ref, gh_ref, dzh_ref, dsh_ref, dnh_ref,
    own_ref, other_ref, bo_ref, bx_ref, dx_ref, sp_ref, *sums,
):
    def step(i, first, last):
        @functools.partial(when, first)
        def _():
            for ref in sums:
                ref[...] = jnp.zeros_like(ref)
            more_sums(sums, dzh_ref[...], hh_ref, xh_ref[...], gh_ref[...], dsh_ref[...], dnh_ref[...])

        d_out = dot_tn(walk.along(d_ref, i)[...], hl_ref[...])
        dz = pull_rows(d_out, walk.down(y_ref, i)[...], walk.down(m_ref, i)[...])
        ds = add_sums(
            sums, dz, walk.under(h_ref, i), walk.down(x_ref, i)[...], walk.along(e_ref, i)[...], w_ref
        )
        walk.down(dx_ref, i)[...] = dot_nt(ds, w_ref[0, 0]).astype(NARROW)

        @functools.partial(when, last)
        def _():
            sp_ref[...] = finish_sums(sel[0], sums, xh_ref[...], own_ref, other_ref, bo_ref, bx_ref)

    return step


def back_first_step(
    walk, sel, y_ref, m_ref, x_ref, dx_ref, e_ref, h_ref,
    w_ref, hh_ref, xh_ref, gh_ref, up_ref, sp_ref, es_ref, ret_ref, dsh_ref, yh_ref, mh_ref,
    own_ref, other_ref, bo_ref, bx_ref, *sums,
):
    def step(i, first, last):
        @functools.partial(when, first)
        def _():
            for ref in sums:
                ref[...] = jnp.zeros_like(ref)

        dz = pull_rows(walk.down(dx_ref, i)[...].astype(WIDE), walk.down(y_ref, i)[...], walk.down(m_ref, i)[...])
        add_sums(sums, dz, walk.under(h_ref, i), walk.down(x_ref, i)[...], walk.along(e_ref, i)[...], w_ref)

        @functools.partial(when, last)
        def _():
            slots = yh_ref.shape[0]
            back = dot(es_ref[...], ret_ref[...])
            top, rest = split(sp_ref[...] + back[:slots] + back[slots:])
            d_out = dot_nt(top, up_ref[1]) + dot_nt(rest, up_ref[1]) + dot_nt(dsh_ref[...], up_ref[0])
            dz = pull_rows(d_out, yh_ref[...], mh_ref[...])
            ds = dot_nt(dz, w_ref[0, 1]).astype(NARROW)
            dn = dot_nt(dz, w_ref[1, 1]).astype(NARROW)
            more_sums(sums, dz, hh_ref, xh_ref[...], gh_ref[...], ds, dn)
            finish_sums(sel[0], sums, xh_ref[...], own_ref, other_ref, bo_ref, bx_ref)

    return step


def sums_scratch(kinds, slots, width):
    return [
        pltpu.VMEM((2, kinds, width, width), WIDE),
        pltpu.VMEM((8, width), WIDE),
        pltpu.VMEM((2 * slots, width), WIDE),
    ]


def last_steps(
    walk, sel, x_ref, e_ref, s_ref, w_ref, b_ref, head_ref, label_ref, lam_ref, pair_ref, agg_ref,
    own_ref, other_ref, bo_ref, bx_ref, dx_ref, sp_ref, ds_ref, dn_ref, hr_ref,
    table, class_ref, hb_ref, h_ref, y_ref, m_ref, dl_ref, st_ref, d_ref, hl_ref, hh_ref, dz_ref, slope, sums, extra,
    *acc,
):
    return [
        forward_step(
            walk, sel, x_ref, e_ref, s_ref, w_ref, b_ref, head_ref, label_ref, lam_ref,
            h_ref, y_ref, m_ref, dl_ref, st_ref, table, class_ref, hb_ref,
        ),
        link_step(
            walk, sel, s_ref, agg_ref, w_ref, b_ref, head_ref, st_ref, lam_ref, pair_ref, y_ref, dl_ref,
            d_ref, hl_ref, hh_ref, dz_ref, ds_ref, dn_ref, hr_ref, slope, sums, extra,
        ),
        back_last_step(
            walk, sel, y_ref, m_ref, x_ref, d_ref, e_ref, h_ref,
            hl_ref, w_ref, hh_ref, s_ref, agg_ref, dz_ref, ds_ref, dn_ref,
            own_ref, other_ref, bo_ref, bx_ref, dx_ref, sp_ref, *acc,
        ),
    ]


def last_layer(walk, sel, head_shape, x, edges, slot_rows, weights, bias, head, pair, agg):
    rows, width = x.shape
    slots = slot_rows.shape[0]
    if not isinstance(weights, list):
        hidden, y, m, d_logits, stats = forward(walk, sel, x, edges, slot_rows, weights, bias, head)
        drive, drive_rows, hidden_h, dz_h, ds_h, dn_h, head_rows = link(
            walk, sel, head_shape, slot_rows, agg, weights, bias, head[0], stats, head[2], pair, y, d_logits
        )
        grads = backward(
            back_last_step, walk, sel, [y, m, x], drive, edges, hidden,
            [drive_rows, weights, hidden_h, slot_rows, agg, dz_h, ds_h, dn_h], slots, True,
        )
        return list(grads) + [ds_h, dn_h, head_rows, weights]
    kinds = weights[0].shape[1]
    ins = [(x, DOWN), (edges, ALONG), (slot_rows, FULL), weights_in(weights), (bias, FULL)]
    ins += [(a, FULL) for a in (*head, pair, agg)]
    outs = [((kinds, width, width), NARROW, FULL)] * 2 + [((8, width), WIDE, FULL)] * 2
    outs += [((rows, width), NARROW, DOWN), ((slots, width), WIDE, FULL)]
    outs += [((slots, width), NARROW, FULL)] * 2 + [(head_shape + (width,), WIDE, FULL)] + weights_out(weights)
    scratch = [pltpu.VMEM((2 * slots, width), NARROW)] + head_scratch(width) + [
        pltpu.VMEM((2, rows, width), NARROW),
        pltpu.VMEM((rows, width), NARROW),
        pltpu.VMEM((rows, width), WIDE),
        pltpu.VMEM((LANES, rows), NARROW),
        pltpu.VMEM((8, LANES), WIDE),
        pltpu.VMEM((LANES + slots, rows), NARROW),
        pltpu.VMEM((LANES + slots, width), NARROW),
        pltpu.VMEM((2, slots, width), NARROW),
        pltpu.VMEM((slots, width), NARROW),
        pltpu.VMEM((slots, width), WIDE),
        pltpu.VMEM((LANES + slots, width), WIDE),
        pltpu.VMEM((8, LANES), WIDE),
    ]
    scratch += sums_scratch(kinds, slots, width)
    walk = Rows(rows, slots, 1024)
    return stage("last_layer", last_steps, walk, sel, ins, outs, scratch, 22 * rows * width * width)


def backward(make, walk, sel, rowed, drive, edges, hidden, halo, slots, is_last):
    rows, width = rowed[0].shape
    kinds = hidden.shape[0]
    outs = [((kinds, width, width), NARROW, FULL)] * 2 + [((8, width), WIDE, FULL)] * 2
    if is_last:
        outs += [((rows, width), NARROW, DOWN), ((slots, width), WIDE, FULL)]
    ins = [(a, DOWN if a.ndim == 2 else PICK) for a in rowed]
    ins += [(drive, ALONG if is_last else DOWN), (edges, ALONG), (hidden, UNDER)]
    if is_last:
        ins += [(a, FULL) for a in halo]
    else:
        ins += [(a, FULL if n == 0 else LATE_LEAD if n == 4 else LATE) for n, a in enumerate(halo)]
    scratch = sums_scratch(kinds, slots, width)
    return stage("rows_backward", make, walk, sel, ins, outs, scratch, (13 if is_last else 11) * rows * width * width)


def extras(count):
    return up(2 * count + 2, 16)


def put_pairs(extra, pieces):
    extra[...] = jnp.zeros_like(extra)
    at = 0
    for piece in pieces:
        top = piece.astype(NARROW).astype(WIDE)
        count = piece.shape[0]
        extra[at : at + count] = top
        extra[at + count : at + 2 * count] = piece - top
        at += 2 * count


def pack_kernel(has_rows, apart, sel, own_ref, got_ref, bo_ref, bg_ref, *refs):
    rows_ref, refs = (refs[0], refs[1:]) if has_rows else (None, refs)
    extra, outs = refs[-1], refs[:-1]
    kinds, far, near, shard, _ = own_ref.shape
    for j in range(near):
        out_ref, place = (outs[j], lax.bitwise_xor(sel[2], j)) if apart else (outs[0].at[j], j)
        for f in range(far):
            for k in range(kinds):
                value = own_ref[k, f, place].astype(WIDE) + got_ref[k, f, place].astype(WIDE)
                at = (f * kinds + k) * shard
                out_ref[at : at + shard] = value.astype(NARROW)
        bias = bo_ref[0:1] + bg_ref[0:1]
        put_pairs(extra, [bias] if rows_ref is None else [rows_ref[place], bias])
        out_ref[far * kinds * shard :] = extra[...].astype(NARROW)


def pack(sel, far, near, own, got, bias_own, bias_got, head_rows=None, apart=True):
    kinds, width, _ = own.shape
    shard = width // (far * near)
    count = 0 if head_rows is None else head_rows.shape[1]
    body = far * kinds * shard
    shape = (kinds, far, near, shard, width)
    if shard % 16:
        total = (own.astype(WIDE) + got.astype(WIDE)).reshape(shape).transpose(2, 1, 0, 3, 4).reshape(near, body, width)
        bias = bias_own[0:1] + bias_got[0:1]
        pieces = [total.astype(NARROW)]
        if count:
            pieces += list(halves(head_rows))
        pieces += [jnp.broadcast_to(h[None], (near, 1, width)) for h in halves(bias)]
        out = pad_rows(jnp.concatenate(pieces, 1), 16)
        if apart:
            out = by_place(out, sel[2], 0)
        return [out[j] for j in range(near)] if apart else out
    ins = [own.reshape(shape), got.reshape(shape), bias_own, bias_got] + ([head_rows] if count else [])
    shape = (body + extras(count), width)
    outs = [shape] * near if apart else [(near,) + shape]
    out = run(
        "pack",
        functools.partial(pack_kernel, count > 0, apart),
        sel,
        ins,
        [full(a.shape) for a in ins],
        [shape_of(a) for a in outs],
        [full(a) for a in outs],
        [pltpu.VMEM((extras(count), width), WIDE)],
        limit=16,
    )
    return out if apart else out[0]


def middle_kernel(far, body, share, near, apart, sel, *refs):
    outs, (total, extra) = refs[near:-2], refs[-2:]
    given = refs[:near] if near > 1 else [refs[0].at[j] for j in range(refs[0].shape[0])]
    value = given[0][...].astype(WIDE)
    for ref in given[1:]:
        value = value + ref[...].astype(WIDE)
    total[...] = value
    count = far * share
    at = far * body
    bias = total[at + 2 * count : at + 2 * count + 1] + total[at + 2 * count + 1 : at + 2 * count + 2]
    for f in range(far):
        out_ref = outs[f] if apart else outs[0].at[f]
        place = lax.bitwise_xor(sel[1], f) if apart else f
        out_ref[:body] = total[pl.ds(pl.multiple_of(place * body, body), body)].astype(NARROW)
        pieces = [bias]
        if share:
            mine = jnp.zeros((share, total.shape[1]), WIDE)
            for g in range(far) if apart else [f]:
                low = at + g * share
                piece = total[low : low + share] + total[low + count : low + count + share]
                mine = jnp.where(place == g, piece, mine) if apart else piece
            pieces = [mine, bias]
        put_pairs(extra, pieces)
        out_ref[body:] = extra[...].astype(NARROW)


def middle(sel, far, share, got, apart=False):
    got = got if isinstance(got, list) else [got]
    rows, width = got[0].shape[-2:]
    near = len(got)
    count = far * share
    body = (rows - extras(count)) // far
    if body % 16:
        total = sum(g.astype(WIDE) for g in got) if near > 1 else jnp.sum(got[0].astype(WIDE), 0)
        at = far * body
        pieces = [total[:at].reshape(far, body, width).astype(NARROW)]
        if share:
            value = total[at : at + count] + total[at + count : at + 2 * count]
            pieces += list(halves(value.reshape(far, share, width)))
        bias = total[at + 2 * count : at + 2 * count + 1] + total[at + 2 * count + 1 : at + 2 * count + 2]
        pieces += [jnp.broadcast_to(h[None], (far, 1, width)) for h in halves(bias)]
        out = jnp.concatenate(pieces, 1)
        out = jnp.pad(out, ((0, 0), (0, body + extras(share) - out.shape[1]), (0, 0)))
        if apart:
            out = by_place(out, sel[1], 0)
        return [out[f] for f in range(far)] if apart else out
    shape = (body + extras(share), width)
    outs = [shape] * far if apart else [(far,) + shape]
    out = run(
        "middle",
        functools.partial(middle_kernel, far, body, share, near, apart),
        sel,
        got,
        [full(a.shape) for a in got],
        [shape_of(a) for a in outs],
        [full(a) for a in outs],
        [pltpu.VMEM((rows, width), WIDE), pltpu.VMEM((extras(share), width), WIDE)],
        limit=16,
    )
    return out if apart else out[0]


def adamw(old, first, second, grad, rate):
    first_new = BETA * first + (1.0 - BETA) * grad
    second_new = BETA * second + (1.0 - BETA) * grad * grad
    step = first_new / (1.0 - BETA**STEP) / (jnp.sqrt(second_new / (1.0 - BETA**STEP)) + EPSA)
    return (old - rate * (step + DECAY * old), first_new, second_new)


def round_kernel(sel, value_ref, out_ref):
    out_ref[...] = value_ref[...].astype(NARROW)


def rounded(sel, value):
    count, rows, width = value.shape
    spec = pl.BlockSpec((1, rows, width), lambda i, s: (i, 0, 0))
    return run(
        "rounded", round_kernel, sel, [value], [spec], shape_of(value.shape), spec, limit=58, grid=(count,)
    )


def square_kernel(body, share, near, sel, *refs):
    given, (sum_ref, bias_ref, out_ref) = refs[:-3], refs[-3:]
    first, second = given[: len(given) // 2], given[len(given) // 2 :]
    total = jnp.zeros((1, 1), WIDE)
    rows = []
    for layer, (given, at) in enumerate(((first, body), (second, body + 2 * share))):
        value = given[0][...].astype(WIDE)
        for ref in given[1:]:
            value = value + ref[...].astype(WIDE)
        sum_ref[layer] = value[:body]
        rows.append(value[at : at + 1] + value[at + 1 : at + 2])
        total = total + jnp.sum(value[:body] * value[:body], keepdims=True)
    mine = value[body : body + share] + value[body + share : body + 2 * share]
    width = sum_ref.shape[2]
    shard = bias_ref.shape[1]
    place = (sel[1] * near + sel[2]) * shard
    rows = jnp.concatenate(rows + [jnp.zeros((8 - len(rows), width), WIDE)], 0)
    own = pltpu.roll(rows, lax.rem(width - place, width), 1)[:2, :shard]
    bias_ref[...] = own
    total = total + jnp.sum(own * own, keepdims=True)
    lane = lax.broadcasted_iota(jnp.int32, (1, width), 1)
    line = jnp.zeros((1, width), WIDE)
    for k in range(3):
        part = total.astype(NARROW).astype(WIDE)
        line = jnp.where(lane == k, part, line)
        total = total - part
    top = mine.astype(NARROW).astype(WIDE)
    pieces = [top, mine - top, line]
    spare = out_ref.shape[1] - 2 * share - 1
    pieces += [jnp.zeros((spare, width), WIDE)] if spare else []
    payload = jnp.concatenate(pieces, 0).astype(NARROW)
    for d in range(out_ref.shape[0]):
        out_ref[d] = payload


def squares_of(sel, first, second, body, share, near, shard, devices):
    width = second[0].shape[1]
    ins = list(first) + list(second)
    rows = up(2 * share + 1, 8)
    outs = [shape_of((2, body, width), WIDE), shape_of((2, shard), WIDE), shape_of((devices, rows, width))]
    return run(
        "squares",
        functools.partial(square_kernel, body, share, near),
        sel,
        ins,
        [full(a.shape) for a in ins],
        outs,
        [full(o.shape) for o in outs],
        limit=24,
    )


def stacked_halves(value):
    return jnp.concatenate(split(value), 0)


def turn_kernel(sel, value_ref, basis_ref, out_ref):
    for i in range(value_ref.shape[0]):
        both = dot(stacked_halves(value_ref[i]), basis_ref[i])
        out_ref[i] = both[: both.shape[0] // 2] + both[both.shape[0] // 2 :]


def turn(sel, value, basis):
    return run(
        "turn",
        turn_kernel,
        sel,
        [value, basis],
        [full(a.shape) for a in (value, basis)],
        shape_of(value.shape, WIDE),
        full(value.shape),
        limit=24,
    )


def update_kernel(
    share, near, sel, turned_ref, parts_ref, basis_ref, old_ref, first_ref, second_ref,
    bias_ref, b_old_ref, b_first_ref, b_second_ref, h_old_ref, h_first_ref, h_second_ref,
    norm_ref, pair_ref, new_ref, low_ref, m_ref, v_ref, bn_ref, bm_ref, bv_ref, hn_ref, hm_ref, hv_ref, heads,
):
    classes, width = h_old_ref.shape[0], h_old_ref.shape[1] - 1
    far = parts_ref.shape[0] // (2 * near)
    squares = jnp.zeros((1, 1), WIDE)
    for f in range(far):
        for j in range(near):
            at = (f * near + j) * 2
            both = parts_ref[at].astype(WIDE), parts_ref[at + 1].astype(WIDE)
            spot = (j * far + f) * share
            one, two = (part[:share] + part[share : 2 * share] for part in both)
            heads[spot : spot + share] = one + two
            for part in both:
                squares = squares + jnp.sum(part[2 * share : 2 * share + 1, :LANES], keepdims=True)
    grad = heads[:classes]
    last = heads[classes : classes + 1, :LANES]
    lane = lax.broadcasted_iota(jnp.int32, (classes, LANES), 1)
    here = lane == lax.broadcasted_iota(jnp.int32, (classes, LANES), 0)
    grad_last = jnp.sum(jnp.where(here, last, 0.0), axis=1, keepdims=True)
    squares = squares + jnp.sum(grad * grad, keepdims=True) + jnp.sum(grad_last * grad_last, keepdims=True)
    loss, weight = last[:, classes : classes + 1], last[:, classes + 1 : classes + 2]
    norm = jnp.sqrt(squares) / weight
    norm_ref[...] = norm
    pair_ref[...] = jnp.where(lax.broadcasted_iota(jnp.int32, (1, 2), 1) == 0, loss, weight)
    factor = jnp.minimum(1.0, CLIP / norm) / weight
    bn_ref[...], bm_ref[...], bv_ref[...] = adamw(
        b_old_ref[...], b_first_ref[...], b_second_ref[...], bias_ref[...] * factor, LR_BIAS
    )
    for at, value in ((slice(0, width), grad), (slice(width, width + 1), grad_last)):
        hn_ref[:, at], hm_ref[:, at], hv_ref[:, at] = adamw(
            h_old_ref[:, at], h_first_ref[:, at], h_second_ref[:, at], value * factor, LR_HEAD
        )
    for i in range(turned_ref.shape[0]):
        grad = turned_ref[i] * factor
        first = BETA * first_ref[i] + (1.0 - BETA) * grad
        second = BETA * second_ref[i] + (1.0 - BETA) * grad * grad
        m_ref[i] = first
        v_ref[i] = second
        step = first / (1.0 - BETA**STEP) / (jnp.sqrt(second / (1.0 - BETA**STEP)) + EPSA)
        both = dot_nt(stacked_halves(step), basis_ref[i])
        back = both[: both.shape[0] // 2] + both[both.shape[0] // 2 :]
        new = old_ref[i] - LR_MAT * (back + DECAY * old_ref[i])
        new_ref[i] = new
        low_ref[i] = new.astype(NARROW)


def update(sel, share, near, *ins):
    mats, bias, head = ins[3], ins[7], ins[10]
    outs = [shape_of((1, 1), WIDE), shape_of((1, 2), WIDE), shape_of(mats.shape, WIDE), shape_of(mats.shape)]
    outs += [shape_of(mats.shape, WIDE)] * 2 + [shape_of(bias.shape, WIDE)] * 3 + [shape_of(head.shape, WIDE)] * 3
    rows = ins[1].shape[0] // 2 * share
    return run(
        "update",
        functools.partial(update_kernel, share, near),
        sel,
        ins,
        [full(a.shape) for a in ins],
        outs,
        [full(o.shape) for o in outs],
        [pltpu.VMEM((rows, head.shape[1] - 1), WIDE)],
        limit=24,
    )


def local(
    far,
    near,
    node_states,
    serve,
    neighbors,
    alpha,
    live,
    lam,
    labels,
    link_pair,
    mats,
    mats_m,
    mats_v,
    basis,
    bias,
    bias_m,
    bias_v,
    head,
    head_m,
    head_v,
):
    n = far * near
    branch = lax.axis_index("branch")
    both = ("far", "near")
    rows_dev, width = node_states.shape[1:]
    classes = head.shape[1]
    depth, kinds, _, shard, _ = mats.shape
    slots = serve.shape[1]
    cap = slots // n
    walk = Rows(rows_dev, slots)

    def pick(value):
        return lax.dynamic_index_in_dim(value, branch, 0, keepdims=False)

    def swap(value):
        return lax.ppermute(value, "branch", SWAP)

    def exchange(value, axes):
        return lax.all_to_all(value, axes, 0, 0, tiled=True)

    def hop(value, axis, size, k):
        return lax.ppermute(value, axis, [(i, i ^ k) for i in range(size)]) if k else value

    def spread(rows, count):
        return jnp.broadcast_to(rows[None], (count,) + rows.shape)

    places = (branch, lax.axis_index("far"), lax.axis_index("near"))
    sel = jnp.stack([p.astype(jnp.int32) for p in places])

    low = mats.astype(NARROW).reshape(depth, kinds, shard, width)

    def along_far():
        parts = [hop(low, "far", far, k) for k in range(far)]
        return [jnp.stack([part[layer] for part in parts]) for layer in range(depth)]

    def along_near(pieces):
        return [hop(pieces, "near", near, k) for k in range(near)]

    def join(own):
        other = [swap(piece) for piece in own]
        return list(own) + other if walk.whole and shard % 16 == 0 else assemble(sel, own, other)

    far_0, far_1 = along_far()

    send = take_rows(sel, node_states, serve, bias, n)
    far_0, send = lax.optimization_barrier((far_0, send))
    got = exchange(send, both)
    near_0 = along_near(far_0)
    near_0[1], serve, branch, head = lax.optimization_barrier((near_0[1], serve, branch, head))
    edges, edges_s = make_edges(sel, neighbors.transpose(0, 2, 1), alpha.transpose(0, 2, 1), serve)
    slots_0 = got[:, :cap].reshape(slots, width)
    own_bias = got[:, cap, : depth * shard].reshape(n, depth, shard).transpose(1, 0, 2).reshape(depth, width)
    other_bias = swap(own_bias)
    first = branch == 0
    biases = jnp.stack([jnp.where(first, own_bias, other_bias), jnp.where(first, other_bias, own_bias)], 1)
    biases = biases.astype(WIDE)
    agg = lax.dot_general(edges_s, twice(slots_0), (((0,), (0,)), ((), ())), preferred_element_type=WIDE)
    agg, near_0 = lax.optimization_barrier((agg, near_0))
    agg_0 = exchange(agg.astype(NARROW), both)
    weights = [join(near_0)]
    weights[0], far_1 = lax.optimization_barrier((weights[0], far_1))
    near_1 = along_near(far_1)
    share = -(-(classes + 1) // n)
    sel = jnp.concatenate([sel, pick(live)])

    h_h0, slots_1, m_h0, agg, weights[0] = halo_forward(sel, slots_0, agg_0, weights[0], biases[0], edges_s)
    agg, edges = lax.optimization_barrier((agg, edges))
    agg_1 = exchange(agg, both)
    h_0, x_1, m_0 = forward(walk, sel, node_states, edges, slots_0, weights[0], biases[0])
    near_1, x_1, agg_1 = lax.optimization_barrier((near_1, x_1, agg_1))
    weights.append(join(near_1))
    own_1, other_1, bias_1, bias_x1, d_x, spread_1, ds_h1, dn_h1, head_rows, weights[1] = last_layer(
        walk, sel, (near, far * share), x_1, edges, slots_1, weights[1], biases[1], (head.T, labels, lam), link_pair,
        agg_1,
    )
    returned = exchange(dn_h1, both)

    packed = pack(sel, far, near, own_1, swap(other_1), bias_1, swap(bias_x1), head_rows)
    *packed, spread_1 = lax.optimization_barrier((*packed, spread_1))
    sums_1 = [hop(piece, "near", near, k) for k, piece in enumerate(packed)]
    own_0, other_0, bias_0, bias_x0 = backward(
        back_first_step, walk, sel, [x_1, m_0, node_states], d_x, edges, h_0,
        [weights[0], h_h0, slots_0, agg_0, weights[1], spread_1, edges_s, returned, ds_h1, slots_1, m_h0],
        slots, False,
    )
    own_0, other_0, bias_x0, sums_1 = lax.optimization_barrier((own_0, other_0, bias_x0, sums_1))
    packed = pack(sel, far, near, own_0, swap(other_0), bias_0, swap(bias_x0), apart=False)
    packed, sums_1 = lax.optimization_barrier((packed, sums_1))
    sums_0 = exchange(packed, "near")
    body = kinds * shard
    parts_1 = [hop(piece, "far", far, k) for k, piece in enumerate(middle(sel, far, share, sums_1, True))]
    low_basis = rounded(sel, basis.reshape(depth * kinds, width, width))
    sums_0, low_basis = lax.optimization_barrier((sums_0, low_basis))
    parts_0 = [hop(piece, "far", far, k) for k, piece in enumerate(middle(sel, far, 0, sums_0, True))]

    sums, sum_bias, parts = squares_of(sel, parts_0, parts_1, body, share, near, shard, 2 * n)
    parts = exchange(parts, both + ("branch",))
    flat = (depth * kinds, shard, width)
    turned = turn(sel, sums.reshape(flat), low_basis)
    norm, loss_parts, mats_new, mats_low, first_new, second_new, *small = update(
        sel, share, near, turned, parts, low_basis,
        *(a.reshape(flat) for a in (mats, mats_m, mats_v)),
        sum_bias, *(a.reshape(depth, shard) for a in (bias, bias_m, bias_v)),
        *(a.T for a in (head, head_m, head_v)),
    )
    return (
        loss_parts[0],
        norm[0, 0],
        *(a.reshape(mats.shape) for a in (mats_new, mats_low, first_new, second_new)),
        *(a.reshape(bias.shape) for a in small[:3]),
        *(a.T for a in small[3:]),
    )


def solution(mesh):
    n = mesh.shape["rows"]
    near = 1 << (n.bit_length() // 2)
    far = n // near
    grid = Mesh(mesh.devices.reshape(far, near, 2), ("far", "near", "branch"))
    rows = ("far", "near")
    by_row = P(None, rows)
    by_row_last = P(None, rows, None)
    matrix = P(None, None, "branch", rows, None)
    vector = P(None, "branch", rows)
    return jax.shard_map(
        functools.partial(local, far, near),
        mesh=grid,
        in_specs=(by_row_last, by_row, by_row_last, by_row_last)
        + (by_row,) * 4
        + (matrix,) * 3
        + (P(None, None, "branch", None, None),)
        + (vector,) * 3
        + (P(),) * 3,
        out_specs=(P(), P()) + (matrix,) * 4 + (vector,) * 3 + (P(),) * 3,
        check_vma=False,
    )
```

```python
import functools

import jax
import jax.numpy as jnp
from jax import lax
from jax.experimental import pallas as pl
from jax.experimental.pallas import tpu as pltpu
from jax.sharding import Mesh
from jax.sharding import PartitionSpec as P

STEP = 5
LINK = 4.0
CLIP = 0.001
EPSN = 1e-06
BETA = 0.5
EPSA = 1e-08
LR_MAT = 0.02
LR_BIAS = 0.05
LR_HEAD = 0.02
DECAY = 0.01
HIGH = lax.Precision.HIGHEST
WIDE = jnp.float32
NARROW = jnp.bfloat16
GELU_A = 0.7978845608028654
GELU_B = 0.044715
LANES = 128
SWAP = [(0, 1), (1, 0)]


def halves(value):
    top = lax.reduce_precision(value, 8, 7)
    return top.astype(NARROW), (value - top).astype(NARROW)


def up(value, unit):
    return -(-value // unit) * unit


def pad_rows(rows, unit):
    extra = -rows.shape[-2] % unit
    return jnp.pad(rows, [(0, 0)] * (rows.ndim - 2) + [(0, extra), (0, 0)])


def split(value):
    top = value.astype(NARROW)
    return top, (value - top.astype(WIDE)).astype(NARROW)


def dot(left, right):
    return lax.dot_general(left, right, (((1,), (0,)), ((), ())), preferred_element_type=WIDE)


def dot_nt(left, right):
    return lax.dot_general(left, right, (((1,), (1,)), ((), ())), preferred_element_type=WIDE)


def dot_tn(left, right):
    return lax.dot_general(left, right, (((0,), (0,)), ((), ())), preferred_element_type=WIDE)


def unit_rows(pre):
    sq = pre * pre
    gate = 0.5 + 0.5 * jnp.tanh(pre * (GELU_A + GELU_A * GELU_B * sq))
    slope = gate * (1.0 + pre * (1.0 - gate) * (2.0 * GELU_A + 6.0 * GELU_A * GELU_B * sq))
    act = pre * gate
    inv = lax.rsqrt(jnp.sum(act * act, axis=1, keepdims=True) + EPSN)
    return (act * inv).astype(NARROW), slope * inv


def pull_rows(d_out, out, slope):
    wide = out.astype(WIDE)
    along = jnp.sum(wide * d_out, axis=1, keepdims=True)
    return (slope.astype(WIDE) * (d_out - wide * along)).astype(NARROW)


def full(shape):
    return pl.BlockSpec(shape, lambda *_: (0,) * len(shape))


def when(flag, body):
    if isinstance(flag, bool):
        if flag:
            body()
    else:
        pl.when(flag)(body)


class Rows:
    def __init__(self, rows, slots, tile=512):
        self.rows = rows
        self.whole = slots <= 256
        self.tile = min(rows, tile)
        self.count = rows // self.tile

    def at(self, i):
        return pl.ds(i * self.tile, self.tile)

    def down(self, ref, i):
        return ref.at[self.at(i)] if self.whole else ref

    def along(self, ref, i):
        return ref.at[:, self.at(i)] if self.whole else ref

    def under(self, ref, i):
        return ref.at[:, self.at(i)] if self.whole else ref

    def part(self, kind, ref, i):
        return ref if kind in ONCE else ref.at[self.at(i)] if kind in (DOWN, PICK) else ref.at[:, self.at(i)]

    def source(self, kind, ref, i, sel):
        return ref.at[:, 0] if kind in (LEAD, LATE_LEAD) else self.part(kind, ref.at[sel[0]] if kind == PICK else ref, i)

    def held(self, kind, shape):
        return shape[1:] if kind == PICK else shape[:1] + shape[2:] if kind in (LEAD, LATE_LEAD) else shape

    def spec(self, kind, shape):
        if kind in (FULL, LATE):
            return full(shape)
        if kind in (LEAD, LATE_LEAD):
            return pl.BlockSpec((shape[0], None) + shape[2:], lambda *_: (0,) * len(shape))
        if kind == PICK:
            return pl.BlockSpec((None, self.tile, shape[2]), lambda i, s: (s[0], i, 0))
        if kind == DOWN:
            return pl.BlockSpec((self.tile,) + shape[1:], lambda i, s: (i, 0))
        if kind == ALONG:
            return pl.BlockSpec((shape[0], self.tile), lambda i, s: (0, i))
        return pl.BlockSpec((shape[0], self.tile, shape[2]), lambda i, s: (0, i, 0))


FULL, DOWN, ALONG, UNDER, PICK, LEAD, PIECES, AGAIN, LATE, LATE_LEAD = range(10)
ONCE = (FULL, LEAD, PIECES, AGAIN, LATE, LATE_LEAD)


def grid_kernel(make, walk, n_in, n_out, sel, *refs):
    i = pl.program_id(0)
    make(walk, sel, *refs)(i, i == 0, i == walk.count - 1)


def piece_copies(sel, refs, out_ref):
    near = len(refs) // 2
    far, kinds, shard, _ = refs[0].shape
    pairs = []
    for half in range(2):
        slot = sel[0] if half == 0 else 1 - sel[0]
        for j in range(near):
            for f in range(far):
                place = lax.bitwise_xor(sel[1], f) * near + lax.bitwise_xor(sel[2], j)
                at = pl.ds(pl.multiple_of(place * shard, shard), shard)
                pairs += [(refs[half * near + j].at[f, k], out_ref.at[slot, k, at]) for k in range(kinds)]
    return pairs


def copy_kernel(make, walk, kinds, sizes, n_in, sel, *refs):
    count = len(kinds)
    far, at = [], 0
    for size in sizes:
        far.append(refs[at : at + size])
        at += size
    held = [k for k in range(count) if kinds[k] != AGAIN]
    near = dict(zip(held, refs[at : at + len(held)]))
    steps = make(walk, sel, *near.values(), *refs[at + len(held) : -1])
    steps = steps if isinstance(steps, list) else [steps]
    sems = refs[-1]
    used = [0]

    def copies(k, i):
        kind = kinds[k]
        if kind == PIECES:
            pairs = piece_copies(sel, far[k], near[k])
        elif kind == AGAIN:
            pairs = [(near[kinds.index(PIECES)], far[k][0])]
        else:
            pair = (walk.source(kind, far[k][0], i, sel), walk.part(kind, near[k], i))
            pairs = [pair if k < n_in else pair[::-1]]
        used[0] += len(pairs)
        return [
            pltpu.make_async_copy(*pair, sems.at[used[0] - len(pairs) + n]) for n, pair in enumerate(pairs)
        ]

    def wanted(i, given):
        chosen = []
        for k in given:
            late = k >= n_in or kinds[k] in (LATE, LATE_LEAD)
            if kinds[k] not in ONCE or i == (walk.count - 1 if late else 0):
                chosen += copies(k, i)
        return chosen

    loads = [wanted(i, range(n_in)) for i in range(walk.count)]
    ahead = 2
    for group in loads[:ahead]:
        for item in group:
            item.start()
    stores = []
    results = [k for k in range(n_in, count) if kinds[k] != AGAIN]
    for n, step in enumerate(steps):
        for i in range(walk.count):
            for item in loads[i] if n == 0 else []:
                item.wait()
            for item in loads[i + ahead] if n == 0 and i + ahead < walk.count else []:
                item.start()
            if n == 0 and i == 0:
                stores = [item for k in range(n_in, count) if kinds[k] == AGAIN for item in copies(k, i)]
                for item in stores:
                    item.start()
            step(i, i == 0, i == walk.count - 1)
            for item in wanted(i, results) if n == len(steps) - 1 else []:
                item.start()
                stores.append(item)
    for item in stores:
        item.wait()


def run(name, kernel, sel, ins, in_specs, outs, out_specs, scratch=(), flops=0, limit=20, grid=(), size=None):
    if size is None:
        size = sum(a.size * a.dtype.itemsize for a in ins)
        size += sum(o.size * o.dtype.itemsize for o in (outs if isinstance(outs, list) else [outs]))
    return pl.pallas_call(
        kernel,
        out_shape=outs,
        grid_spec=pltpu.PrefetchScalarGridSpec(
            num_scalar_prefetch=1,
            grid=grid,
            in_specs=in_specs,
            out_specs=out_specs,
            scratch_shapes=list(scratch),
        ),
        compiler_params=pltpu.CompilerParams(
            dimension_semantics=("arbitrary",) * len(grid), vmem_limit_bytes=limit << 20
        ),
        name=name,
        cost_estimate=pl.CostEstimate(flops=flops, bytes_accessed=size, transcendentals=0),
    )(sel, *ins)


def stage(name, make, walk, sel, ins, outs, scratch=(), flops=0):
    kinds = [k for _, k in ins] + [k for *_, k in outs]
    groups = [a if isinstance(a, list) else [a] for a, _ in ins]
    arrays = [a for group in groups for a in group]
    shapes = [shape_of(shape, dtype) for shape, dtype, _ in outs]
    n_in = len(ins)
    if not walk.whole:
        specs = [walk.spec(k, a.shape) for k, a in zip(kinds, arrays + shapes)]
        return run(
            name, functools.partial(grid_kernel, make, walk, n_in, len(outs)),
            sel, arrays, specs[:n_in], shapes, specs[n_in:], scratch, flops, 58, (walk.count,),
        )
    held, copies = [], 0
    for kind, group in zip(kinds, groups + [[a] for a in shapes]):
        shape = group[0].shape
        if kind == PIECES:
            far, parts, shard, width = shape
            shape = (2, parts, width, width)
            copies += len(group) * far * parts
        else:
            copies += 1 if kind in ONCE else walk.count
        if kind != AGAIN:
            held.append(pltpu.VMEM(walk.held(kind, shape), group[0].dtype))
    hbm = pl.BlockSpec(memory_space=pltpu.HBM)
    free = pl.BlockSpec(memory_space=pl.ANY)
    small = 300_000
    specs = [
        free if kind == PIECES or (kind in (FULL, LATE) and a.size * a.dtype.itemsize < small) else hbm
        for kind, group in zip(kinds, groups)
        for a in group
    ]
    return run(
        name, functools.partial(copy_kernel, make, walk, kinds, [len(g) for g in groups] + [1] * len(outs), n_in),
        sel, arrays, specs, shapes, [hbm] * len(outs),
        held + list(scratch) + [pltpu.SemaphoreType.DMA((copies,))], flops, 58,
    )


def shape_of(shape, dtype=NARROW):
    return jax.ShapeDtypeStruct(shape, dtype)


def serve_kernel(sel, states_ref, serve_ref, bias_ref, out_ref, held, sems):
    me = sel[0]
    part = held.shape[1]
    copies = []
    for i in range(held.shape[0]):
        copies.append(pltpu.make_async_copy(states_ref.at[me, pl.ds(i * part, part)], held.at[i], sems.at[i]))
        copies[-1].start()
    serve = serve_ref[pl.ds(me, 1)]
    row = lax.broadcasted_iota(jnp.int32, (part, serve.shape[1]), 0)
    total = None
    for i, copy in enumerate(copies):
        copy.wait()
        one = jnp.where(row == serve - i * part, 1.0, 0.0).astype(NARROW)
        value = dot_tn(one, held[i])
        total = value if total is None else total + value
    cap = serve.shape[1] // out_ref.shape[0]
    depth, _, shard = bias_ref.shape
    bias = jnp.zeros((8, out_ref.shape[2]), WIDE)
    for layer in range(depth):
        spot = lax.broadcasted_iota(jnp.int32, (shard, out_ref.shape[2]), 1)
        here = spot == lax.broadcasted_iota(jnp.int32, spot.shape, 0) + layer * shard
        row = jnp.broadcast_to(bias_ref[layer].astype(NARROW), (8, shard))
        bias = bias + dot(row, jnp.where(here, 1.0, 0.0).astype(NARROW))
    for d in range(out_ref.shape[0]):
        out_ref[d] = jnp.concatenate([total[d * cap : (d + 1) * cap], bias], 0).astype(NARROW)


def take_rows(sel, node_states, serve, bias, n):
    _, rows, width = node_states.shape
    shape = (n, serve.shape[1] // n + 8, width)
    return run(
        "serve",
        serve_kernel,
        sel,
        (node_states, serve, bias),
        [pl.BlockSpec(memory_space=pltpu.HBM), full(serve.shape), full(bias.shape)],
        shape_of(shape),
        full(shape),
        [pltpu.VMEM((4, rows // 4, width), NARROW), pltpu.SemaphoreType.DMA((4,))],
        limit=58,
    )


def edge_kernel(sel, nbr_ref, alpha_ref, serve_ref, out_ref, served_ref, total):
    me = sel[0]
    slots = served_ref.shape[1]
    rows = nbr_ref.shape[2]
    tile = min(rows, 512)
    total[...] = jnp.zeros_like(total)
    lane = lax.broadcasted_iota(jnp.int32, (slots, tile), 0)
    row = lax.broadcasted_iota(jnp.int32, (tile, slots), 0)

    def step(i, carry):
        at = pl.ds(pl.multiple_of(i * tile, tile), tile)
        nbr, alpha = nbr_ref[me, :, at], alpha_ref[me, :, at]
        value = jnp.zeros((slots, tile), WIDE)
        for k in range(nbr.shape[0]):
            value = value + jnp.where(nbr[k : k + 1] == lane, alpha[k : k + 1], 0.0)
        top, rest = split(value)
        out_ref[:slots, at] = top
        out_ref[slots:, at] = rest
        one = jnp.where(row == serve_ref[pl.ds(me, 1)] - i * tile, 1.0, 0.0).astype(NARROW)
        total[...] += dot(out_ref[:, at], one)
        return carry

    lax.fori_loop(0, rows // tile, step, 0)
    served_ref[...] = total[...].astype(NARROW)


def make_edges(sel, neighbors, alpha, serve):
    _, deg, rows = neighbors.shape
    slots = serve.shape[1]
    shapes = [(2 * slots, rows), (2 * slots, slots)]
    return run(
        "edges",
        edge_kernel,
        sel,
        (neighbors, alpha, serve),
        [full(neighbors.shape), full(alpha.shape), full(serve.shape)],
        [shape_of(a) for a in shapes],
        [full(a) for a in shapes],
        [pltpu.VMEM((2 * slots, slots), WIDE)],
        flops=5 * 10**9,
        limit=16 if slots <= 256 else 56,
    )


def by_place(value, me, axis):
    count = value.shape[axis]
    return jnp.concatenate(
        [lax.dynamic_slice_in_dim(value, lax.bitwise_xor(me, i), 1, axis) for i in range(count)], axis
    )


def twice(rows):
    return jnp.concatenate([rows, rows], 0)


def assemble(sel, own, other):
    near = len(own)
    far, kinds, shard, width = own[0].shape
    own, other = (by_place(by_place(jnp.stack(w), sel[2], 0), sel[1], 1).transpose(2, 1, 0, 3, 4) for w in (own, other))
    first = sel[0] == 0
    both = jnp.stack([jnp.where(first, own, other), jnp.where(first, other, own)])
    return both.reshape(2, kinds, far * near * shard, width)


def layer_rows(x, sums, w_ref, b_ref, h_ref):
    hs = (dot(x, w_ref[0, 0]) + b_ref[0:1]).astype(NARROW)
    hn = (sums + b_ref[1:2]).astype(NARROW)
    h_ref[0] = hs
    h_ref[1] = hn
    return unit_rows(dot(hs, w_ref[0, 1]) + dot(hn, w_ref[1, 1]))


def halo_step(walk, sel, x_ref, agg_ref, w_ref, b_ref, e_ref, h_ref, y_ref, m_ref, next_ref):
    def step(i, first, last):
        y, m = layer_rows(x_ref[...], dot(agg_ref[...], w_ref[1, 0]), w_ref, b_ref, h_ref)
        y_ref[...] = y
        m_ref[...] = m
        next_ref[...] = dot_tn(e_ref[...], twice(y)).astype(NARROW)

    return step


def weights_in(weights):
    return (weights, PIECES if isinstance(weights, list) else FULL)


def weights_out(weights):
    if not isinstance(weights, list):
        return []
    _, kinds, _, width = weights[0].shape
    return [((2, kinds, width, width), NARROW, AGAIN)]


def halo_forward(sel, x, agg, weights, bias, edges_s):
    slots, width = x.shape
    walk = Rows(slots, slots)
    walk.tile, walk.count = slots, 1
    ins = [(x, FULL), (agg, FULL), weights_in(weights), (bias, FULL), (edges_s, FULL)]
    outs = [((2, slots, width), NARROW, FULL), ((slots, width), NARROW, FULL), ((slots, width), WIDE, FULL)]
    outs += [((slots, width), NARROW, FULL)] + weights_out(weights)
    out = stage("halo", halo_step, walk, sel, ins, outs, flops=10 * slots * width * width)
    return (*out[:4], out[4] if isinstance(weights, list) else weights)


def own_row(walk, sel, ref, i):
    return ref[pl.ds(sel[0], 1), pl.ds(i * walk.tile if walk.whole else pl.multiple_of(i * walk.tile, LANES), walk.tile)]


def node_weights(walk, sel, lam_ref, i):
    node = lax.broadcasted_iota(jnp.int32, (1, walk.tile), 1) + i * walk.tile
    return jnp.where(node < sel[3], own_row(walk, sel, lam_ref, i), 0.0)


def forward_step(walk, sel, x_ref, e_ref, s_ref, w_ref, b_ref, *refs):
    has_head = len(refs) > 4
    if has_head:
        head_ref, label_ref, lam_ref, h_ref, y_ref, m_ref, dl_ref, st_ref, table, class_ref, hb_ref = refs
        classes, width = head_ref.shape[0], head_ref.shape[1] - 1
    else:
        h_ref, y_ref, m_ref, table = refs

    def step(i, first, last):
        @functools.partial(when, first)
        def _():
            table[...] = twice(dot(s_ref[...], w_ref[1, 0]).astype(NARROW))
            if has_head:
                st_ref[...] = jnp.zeros_like(st_ref)
                class_ref[...] = jnp.zeros_like(class_ref)
                class_ref[:classes] = head_ref[:, :width].astype(NARROW)
                hb_ref[...] = jnp.full_like(hb_ref, -1e30)
                hb_ref[:classes] = head_ref[:, width:]

        sums = dot_tn(walk.along(e_ref, i)[...], table[...])
        y, m = layer_rows(walk.down(x_ref, i)[...], sums, w_ref, b_ref, walk.under(h_ref, i))
        walk.down(y_ref, i)[...] = y
        walk.down(m_ref, i)[...] = m.astype(m_ref.dtype)
        if has_head:
            logits = dot_nt(class_ref[...], y) + hb_ref[...]
            label, weight = own_row(walk, sel, label_ref, i), node_weights(walk, sel, lam_ref, i)
            hit = lax.broadcasted_iota(jnp.int32, logits.shape, 0) == label
            top = jnp.max(logits, axis=0, keepdims=True)
            power = jnp.exp(logits - top)
            total = jnp.sum(power, axis=0, keepdims=True)
            picked = jnp.sum(jnp.where(hit, logits, 0.0), axis=0, keepdims=True)
            cross = top + jnp.log(total) - picked
            dl = (power * (weight / total) - jnp.where(hit, weight, 0.0)).astype(NARROW)
            walk.along(dl_ref, i)[...] = dl
            ones = jnp.ones((8, walk.tile), NARROW)
            st_ref[0:1] += jnp.broadcast_to(jnp.sum(weight * cross, axis=1, keepdims=True), (1, LANES))
            st_ref[1:2] += dot_nt(ones, dl)[0:1]
            st_ref[2:3] += jnp.broadcast_to(jnp.sum(weight, axis=1, keepdims=True), (1, LANES))

    return step


def head_scratch(width):
    return [pltpu.VMEM((LANES, width), NARROW), pltpu.VMEM((LANES, 1), WIDE)]


def forward(walk, sel, x, edges, slot_rows, weights, bias, head=None):
    rows, width = x.shape[-2:]
    slots = slot_rows.shape[0]
    ins = [(x, DOWN if x.ndim == 2 else PICK), (edges, ALONG), (slot_rows, FULL), (weights, FULL), (bias, FULL)]
    outs = [((2, rows, width), NARROW, UNDER)] + [((rows, width), NARROW, DOWN)] * 2
    if head is not None:
        ins += [(a, FULL) for a in head]
        outs += [((LANES, rows), NARROW, ALONG), ((8, LANES), WIDE, FULL)]
    scratch = [pltpu.VMEM((2 * slots, width), NARROW)] + (head_scratch(width) if head is not None else [])
    return stage("rows_forward", forward_step, walk, sel, ins, outs, scratch, 7 * rows * width * width)


def link_step(
    walk, sel, x_ref, agg_ref, w_ref, b_ref, head_ref, st_ref, lam_ref, pair_ref, y_ref, dl_ref,
    d_ref, hl_ref, h_ref, dz_ref, ds_ref, dn_ref, hr_ref, slope, sums, extra,
):
    classes, width = head_ref.shape[0], head_ref.shape[1] - 1

    def step(i, first, last):
        @functools.partial(when, first)
        def _():
            y, m = layer_rows(x_ref[...], dot(agg_ref[...], w_ref[1, 0]), w_ref, b_ref, h_ref)
            hl_ref[:LANES] = jnp.zeros((LANES, width), NARROW)
            hl_ref[:classes] = head_ref[:, :width].astype(NARROW)
            hl_ref[LANES:] = y
            slope[...] = m
            sums[...] = jnp.zeros_like(sums)
            extra[...] = jnp.zeros_like(extra)

        y = walk.down(y_ref, i)[...]
        near = dot_nt(hl_ref[LANES:], y)
        weight, pair = node_weights(walk, sel, lam_ref, i), own_row(walk, sel, pair_ref, i)
        hit = lax.broadcasted_iota(jnp.int32, near.shape, 0) == pair
        arg = -LINK * jnp.sum(jnp.where(hit, near, 0.0), axis=0, keepdims=True)
        small = jnp.exp(-jnp.abs(arg))
        soft = jnp.maximum(arg, 0.0) + jnp.log(1.0 + small)
        sigmoid = jnp.where(arg >= 0.0, 1.0, small) / (1.0 + small)
        extra[0:1] += jnp.broadcast_to(jnp.sum(weight * soft, axis=1, keepdims=True), (1, LANES))
        d_score = -LINK * weight * sigmoid
        d_at = walk.along(d_ref, i)
        d_at[:LANES] = walk.along(dl_ref, i)[...]
        d_at[LANES:] = jnp.where(hit, d_score, 0.0).astype(NARROW)
        sums[...] += dot(d_at[...], y)

        @functools.partial(when, last)
        def _():
            dz = pull_rows(sums[LANES:], hl_ref[LANES:], slope[...])
            dz_ref[...] = dz
            ds_ref[...] = dot_nt(dz, w_ref[0, 1]).astype(NARROW)
            dn_ref[...] = dot_nt(dz, w_ref[1, 1]).astype(NARROW)
            lane = lax.broadcasted_iota(jnp.int32, (1, LANES), 1)
            row = jnp.where(lane < classes, st_ref[1:2], 0.0)
            row = jnp.where(lane == classes, st_ref[0:1] + extra[0:1], row)
            row = jnp.where(lane == classes + 1, st_ref[2:3], row)
            sums[classes : classes + 1, :LANES] = row
            for j in range(hr_ref.shape[0]):
                hr_ref[j] = sums[j * hr_ref.shape[1] : (j + 1) * hr_ref.shape[1]]

    return step


def link(walk, sel, head_shape, x, agg, weights, bias, head_t, stats, lam, pair, y, d_logits):
    slots, width = x.shape
    rows = y.shape[0]
    ins = [(a, FULL) for a in (x, agg, weights, bias, head_t, stats, lam, pair)]
    ins += [(y, DOWN), (d_logits, ALONG)]
    outs = [((LANES + slots, rows), NARROW, ALONG), ((LANES + slots, width), NARROW, FULL)]
    outs += [((2, slots, width), NARROW, FULL)] + [((slots, width), NARROW, FULL)] * 3
    outs += [(head_shape + (width,), WIDE, FULL)]
    scratch = [
        pltpu.VMEM((slots, width), WIDE),
        pltpu.VMEM((LANES + slots, width), WIDE),
        pltpu.VMEM((8, LANES), WIDE),
    ]
    flops = 6 * rows * slots * width + 12 * slots * width * width
    return stage("link", link_step, walk, sel, ins, outs, scratch, flops)


def add_sums(sums, dz, h, x, edges, w_ref):
    acc, bias_acc, spread_acc = sums
    acc[0, 1] += dot_tn(h[0], dz)
    acc[1, 1] += dot_tn(h[1], dz)
    ds = dot_nt(dz, w_ref[0, 1]).astype(NARROW)
    dn = dot_nt(dz, w_ref[1, 1]).astype(NARROW)
    acc[0, 0] += dot_tn(x, ds)
    spread_acc[...] += dot(edges, dn)
    bias_acc[0:1] += jnp.sum(ds.astype(WIDE), axis=0, keepdims=True)
    bias_acc[1:2] += jnp.sum(dn.astype(WIDE), axis=0, keepdims=True)
    return ds


def more_sums(sums, dz, h_ref, x, agg, ds, dn):
    acc, bias_acc, _ = sums
    acc[0, 1] += dot_tn(h_ref[0], dz)
    acc[1, 1] += dot_tn(h_ref[1], dz)
    acc[0, 0] += dot_tn(x, ds)
    acc[1, 0] += dot_tn(agg, dn)
    bias_acc[0:1] += jnp.sum(ds.astype(WIDE), axis=0, keepdims=True)
    bias_acc[1:2] += jnp.sum(dn.astype(WIDE), axis=0, keepdims=True)


def finish_sums(me, sums, table, own_ref, other_ref, bo_ref, bx_ref):
    acc, bias_acc, spread_acc = sums
    slots = table.shape[0]
    spread = spread_acc[:slots] + spread_acc[slots:]
    top, rest = split(spread)
    acc[1, 0] += dot_tn(table, top) + dot_tn(table, rest)
    own_ref[...] = acc[me].astype(NARROW)
    other_ref[...] = acc[1 - me].astype(NARROW)
    bo_ref[...] = jnp.broadcast_to(bias_acc[pl.ds(me, 1)], bo_ref.shape)
    bx_ref[...] = jnp.broadcast_to(bias_acc[pl.ds(1 - me, 1)], bx_ref.shape)
    return spread


def back_last_step(
    walk, sel, y_ref, m_ref, x_ref, d_ref, e_ref, h_ref,
    hl_ref, w_ref, hh_ref, xh_ref, gh_ref, dzh_ref, dsh_ref, dnh_ref,
    own_ref, other_ref, bo_ref, bx_ref, dx_ref, sp_ref, *sums,
):
    def step(i, first, last):
        @functools.partial(when, first)
        def _():
            for ref in sums:
                ref[...] = jnp.zeros_like(ref)
            more_sums(sums, dzh_ref[...], hh_ref, xh_ref[...], gh_ref[...], dsh_ref[...], dnh_ref[...])

        d_out = dot_tn(walk.along(d_ref, i)[...], hl_ref[...])
        dz = pull_rows(d_out, walk.down(y_ref, i)[...], walk.down(m_ref, i)[...])
        ds = add_sums(
            sums, dz, walk.under(h_ref, i), walk.down(x_ref, i)[...], walk.along(e_ref, i)[...], w_ref
        )
        walk.down(dx_ref, i)[...] = dot_nt(ds, w_ref[0, 0]).astype(NARROW)

        @functools.partial(when, last)
        def _():
            sp_ref[...] = finish_sums(sel[0], sums, xh_ref[...], own_ref, other_ref, bo_ref, bx_ref)

    return step


def back_first_step(
    walk, sel, y_ref, m_ref, x_ref, dx_ref, e_ref, h_ref,
    w_ref, hh_ref, xh_ref, gh_ref, up_ref, sp_ref, es_ref, ret_ref, dsh_ref, yh_ref, mh_ref,
    own_ref, other_ref, bo_ref, bx_ref, *sums,
):
    def step(i, first, last):
        @functools.partial(when, first)
        def _():
            for ref in sums:
                ref[...] = jnp.zeros_like(ref)

        dz = pull_rows(walk.down(dx_ref, i)[...].astype(WIDE), walk.down(y_ref, i)[...], walk.down(m_ref, i)[...])
        add_sums(sums, dz, walk.under(h_ref, i), walk.down(x_ref, i)[...], walk.along(e_ref, i)[...], w_ref)

        @functools.partial(when, last)
        def _():
            slots = yh_ref.shape[0]
            back = dot(es_ref[...], ret_ref[...])
            top, rest = split(sp_ref[...] + back[:slots] + back[slots:])
            d_out = dot_nt(top, up_ref[1]) + dot_nt(rest, up_ref[1]) + dot_nt(dsh_ref[...], up_ref[0])
            dz = pull_rows(d_out, yh_ref[...], mh_ref[...])
            ds = dot_nt(dz, w_ref[0, 1]).astype(NARROW)
            dn = dot_nt(dz, w_ref[1, 1]).astype(NARROW)
            more_sums(sums, dz, hh_ref, xh_ref[...], gh_ref[...], ds, dn)
            finish_sums(sel[0], sums, xh_ref[...], own_ref, other_ref, bo_ref, bx_ref)

    return step


def sums_scratch(kinds, slots, width):
    return [
        pltpu.VMEM((2, kinds, width, width), WIDE),
        pltpu.VMEM((8, width), WIDE),
        pltpu.VMEM((2 * slots, width), WIDE),
    ]


def last_steps(
    walk, sel, x_ref, e_ref, s_ref, w_ref, b_ref, head_ref, label_ref, lam_ref, pair_ref, agg_ref,
    own_ref, other_ref, bo_ref, bx_ref, dx_ref, sp_ref, ds_ref, dn_ref, hr_ref,
    table, class_ref, hb_ref, h_ref, y_ref, m_ref, dl_ref, st_ref, d_ref, hl_ref, hh_ref, dz_ref, slope, sums, extra,
    *acc,
):
    return [
        forward_step(
            walk, sel, x_ref, e_ref, s_ref, w_ref, b_ref, head_ref, label_ref, lam_ref,
            h_ref, y_ref, m_ref, dl_ref, st_ref, table, class_ref, hb_ref,
        ),
        link_step(
            walk, sel, s_ref, agg_ref, w_ref, b_ref, head_ref, st_ref, lam_ref, pair_ref, y_ref, dl_ref,
            d_ref, hl_ref, hh_ref, dz_ref, ds_ref, dn_ref, hr_ref, slope, sums, extra,
        ),
        back_last_step(
            walk, sel, y_ref, m_ref, x_ref, d_ref, e_ref, h_ref,
            hl_ref, w_ref, hh_ref, s_ref, agg_ref, dz_ref, ds_ref, dn_ref,
            own_ref, other_ref, bo_ref, bx_ref, dx_ref, sp_ref, *acc,
        ),
    ]


def last_layer(walk, sel, head_shape, x, edges, slot_rows, weights, bias, head, pair, agg):
    rows, width = x.shape
    slots = slot_rows.shape[0]
    if not isinstance(weights, list):
        hidden, y, m, d_logits, stats = forward(walk, sel, x, edges, slot_rows, weights, bias, head)
        drive, drive_rows, hidden_h, dz_h, ds_h, dn_h, head_rows = link(
            walk, sel, head_shape, slot_rows, agg, weights, bias, head[0], stats, head[2], pair, y, d_logits
        )
        grads = backward(
            back_last_step, walk, sel, [y, m, x], drive, edges, hidden,
            [drive_rows, weights, hidden_h, slot_rows, agg, dz_h, ds_h, dn_h], slots, True,
        )
        return list(grads) + [ds_h, dn_h, head_rows, weights]
    kinds = weights[0].shape[1]
    ins = [(x, DOWN), (edges, ALONG), (slot_rows, FULL), weights_in(weights), (bias, FULL)]
    ins += [(a, FULL) for a in (*head, pair, agg)]
    outs = [((kinds, width, width), NARROW, FULL)] * 2 + [((8, width), WIDE, FULL)] * 2
    outs += [((rows, width), NARROW, DOWN), ((slots, width), WIDE, FULL)]
    outs += [((slots, width), NARROW, FULL)] * 2 + [(head_shape + (width,), WIDE, FULL)] + weights_out(weights)
    scratch = [pltpu.VMEM((2 * slots, width), NARROW)] + head_scratch(width) + [
        pltpu.VMEM((2, rows, width), NARROW),
        pltpu.VMEM((rows, width), NARROW),
        pltpu.VMEM((rows, width), WIDE),
        pltpu.VMEM((LANES, rows), NARROW),
        pltpu.VMEM((8, LANES), WIDE),
        pltpu.VMEM((LANES + slots, rows), NARROW),
        pltpu.VMEM((LANES + slots, width), NARROW),
        pltpu.VMEM((2, slots, width), NARROW),
        pltpu.VMEM((slots, width), NARROW),
        pltpu.VMEM((slots, width), WIDE),
        pltpu.VMEM((LANES + slots, width), WIDE),
        pltpu.VMEM((8, LANES), WIDE),
    ]
    scratch += sums_scratch(kinds, slots, width)
    walk = Rows(rows, slots, 1024)
    return stage("last_layer", last_steps, walk, sel, ins, outs, scratch, 22 * rows * width * width)


def backward(make, walk, sel, rowed, drive, edges, hidden, halo, slots, is_last):
    rows, width = rowed[0].shape
    kinds = hidden.shape[0]
    outs = [((kinds, width, width), NARROW, FULL)] * 2 + [((8, width), WIDE, FULL)] * 2
    if is_last:
        outs += [((rows, width), NARROW, DOWN), ((slots, width), WIDE, FULL)]
    ins = [(a, DOWN if a.ndim == 2 else PICK) for a in rowed]
    ins += [(drive, ALONG if is_last else DOWN), (edges, ALONG), (hidden, UNDER)]
    if is_last:
        ins += [(a, FULL) for a in halo]
    else:
        ins += [(a, FULL if n == 0 else LATE_LEAD if n == 4 else LATE) for n, a in enumerate(halo)]
    scratch = sums_scratch(kinds, slots, width)
    return stage("rows_backward", make, walk, sel, ins, outs, scratch, (13 if is_last else 11) * rows * width * width)


def extras(count):
    return up(2 * count + 2, 16)


def put_pairs(extra, pieces):
    extra[...] = jnp.zeros_like(extra)
    at = 0
    for piece in pieces:
        top = piece.astype(NARROW).astype(WIDE)
        count = piece.shape[0]
        extra[at : at + count] = top
        extra[at + count : at + 2 * count] = piece - top
        at += 2 * count


def pack_kernel(has_rows, apart, sel, own_ref, got_ref, bo_ref, bg_ref, *refs):
    rows_ref, refs = (refs[0], refs[1:]) if has_rows else (None, refs)
    extra, outs = refs[-1], refs[:-1]
    kinds, far, near, shard, _ = own_ref.shape
    for j in range(near):
        out_ref, place = (outs[j], lax.bitwise_xor(sel[2], j)) if apart else (outs[0].at[j], j)
        for f in range(far):
            for k in range(kinds):
                value = own_ref[k, f, place].astype(WIDE) + got_ref[k, f, place].astype(WIDE)
                at = (f * kinds + k) * shard
                out_ref[at : at + shard] = value.astype(NARROW)
        bias = bo_ref[0:1] + bg_ref[0:1]
        put_pairs(extra, [bias] if rows_ref is None else [rows_ref[place], bias])
        out_ref[far * kinds * shard :] = extra[...].astype(NARROW)


def pack(sel, far, near, own, got, bias_own, bias_got, head_rows=None, apart=True):
    kinds, width, _ = own.shape
    shard = width // (far * near)
    count = 0 if head_rows is None else head_rows.shape[1]
    body = far * kinds * shard
    shape = (kinds, far, near, shard, width)
    if shard % 16:
        total = (own.astype(WIDE) + got.astype(WIDE)).reshape(shape).transpose(2, 1, 0, 3, 4).reshape(near, body, width)
        bias = bias_own[0:1] + bias_got[0:1]
        pieces = [total.astype(NARROW)]
        if count:
            pieces += list(halves(head_rows))
        pieces += [jnp.broadcast_to(h[None], (near, 1, width)) for h in halves(bias)]
        out = pad_rows(jnp.concatenate(pieces, 1), 16)
        if apart:
            out = by_place(out, sel[2], 0)
        return [out[j] for j in range(near)] if apart else out
    ins = [own.reshape(shape), got.reshape(shape), bias_own, bias_got] + ([head_rows] if count else [])
    shape = (body + extras(count), width)
    outs = [shape] * near if apart else [(near,) + shape]
    out = run(
        "pack",
        functools.partial(pack_kernel, count > 0, apart),
        sel,
        ins,
        [full(a.shape) for a in ins],
        [shape_of(a) for a in outs],
        [full(a) for a in outs],
        [pltpu.VMEM((extras(count), width), WIDE)],
        limit=16,
    )
    return out if apart else out[0]


def middle_kernel(far, body, share, near, apart, sel, *refs):
    outs, (total, extra) = refs[near:-2], refs[-2:]
    given = refs[:near] if near > 1 else [refs[0].at[j] for j in range(refs[0].shape[0])]
    value = given[0][...].astype(WIDE)
    for ref in given[1:]:
        value = value + ref[...].astype(WIDE)
    total[...] = value
    count = far * share
    at = far * body
    bias = total[at + 2 * count : at + 2 * count + 1] + total[at + 2 * count + 1 : at + 2 * count + 2]
    for f in range(far):
        out_ref = outs[f] if apart else outs[0].at[f]
        place = lax.bitwise_xor(sel[1], f) if apart else f
        out_ref[:body] = total[pl.ds(pl.multiple_of(place * body, body), body)].astype(NARROW)
        pieces = [bias]
        if share:
            mine = jnp.zeros((share, total.shape[1]), WIDE)
            for g in range(far) if apart else [f]:
                low = at + g * share
                piece = total[low : low + share] + total[low + count : low + count + share]
                mine = jnp.where(place == g, piece, mine) if apart else piece
            pieces = [mine, bias]
        put_pairs(extra, pieces)
        out_ref[body:] = extra[...].astype(NARROW)


def middle(sel, far, share, got, apart=False):
    got = got if isinstance(got, list) else [got]
    rows, width = got[0].shape[-2:]
    near = len(got)
    count = far * share
    body = (rows - extras(count)) // far
    if body % 16:
        total = sum(g.astype(WIDE) for g in got) if near > 1 else jnp.sum(got[0].astype(WIDE), 0)
        at = far * body
        pieces = [total[:at].reshape(far, body, width).astype(NARROW)]
        if share:
            value = total[at : at + count] + total[at + count : at + 2 * count]
            pieces += list(halves(value.reshape(far, share, width)))
        bias = total[at + 2 * count : at + 2 * count + 1] + total[at + 2 * count + 1 : at + 2 * count + 2]
        pieces += [jnp.broadcast_to(h[None], (far, 1, width)) for h in halves(bias)]
        out = jnp.concatenate(pieces, 1)
        out = jnp.pad(out, ((0, 0), (0, body + extras(share) - out.shape[1]), (0, 0)))
        if apart:
            out = by_place(out, sel[1], 0)
        return [out[f] for f in range(far)] if apart else out
    shape = (body + extras(share), width)
    outs = [shape] * far if apart else [(far,) + shape]
    out = run(
        "middle",
        functools.partial(middle_kernel, far, body, share, near, apart),
        sel,
        got,
        [full(a.shape) for a in got],
        [shape_of(a) for a in outs],
        [full(a) for a in outs],
        [pltpu.VMEM((rows, width), WIDE), pltpu.VMEM((extras(share), width), WIDE)],
        limit=16,
    )
    return out if apart else out[0]


def adamw(old, first, second, grad, rate):
    first_new = BETA * first + (1.0 - BETA) * grad
    second_new = BETA * second + (1.0 - BETA) * grad * grad
    step = first_new / (1.0 - BETA**STEP) / (jnp.sqrt(second_new / (1.0 - BETA**STEP)) + EPSA)
    return (old - rate * (step + DECAY * old), first_new, second_new)


def round_kernel(sel, value_ref, out_ref):
    out_ref[...] = value_ref[...].astype(NARROW)


def rounded(sel, value):
    count, rows, width = value.shape
    spec = pl.BlockSpec((1, rows, width), lambda i, s: (i, 0, 0))
    return run(
        "rounded", round_kernel, sel, [value], [spec], shape_of(value.shape), spec, limit=58, grid=(count,)
    )


def square_kernel(body, share, near, sel, *refs):
    given, (sum_ref, bias_ref, out_ref) = refs[:-3], refs[-3:]
    first, second = given[: len(given) // 2], given[len(given) // 2 :]
    total = jnp.zeros((1, 1), WIDE)
    rows = []
    for layer, (given, at) in enumerate(((first, body), (second, body + 2 * share))):
        value = given[0][...].astype(WIDE)
        for ref in given[1:]:
            value = value + ref[...].astype(WIDE)
        sum_ref[layer] = value[:body]
        rows.append(value[at : at + 1] + value[at + 1 : at + 2])
        total = total + jnp.sum(value[:body] * value[:body], keepdims=True)
    mine = value[body : body + share] + value[body + share : body + 2 * share]
    width = sum_ref.shape[2]
    shard = bias_ref.shape[1]
    place = (sel[1] * near + sel[2]) * shard
    rows = jnp.concatenate(rows + [jnp.zeros((8 - len(rows), width), WIDE)], 0)
    own = pltpu.roll(rows, lax.rem(width - place, width), 1)[:2, :shard]
    bias_ref[...] = own
    total = total + jnp.sum(own * own, keepdims=True)
    lane = lax.broadcasted_iota(jnp.int32, (1, width), 1)
    line = jnp.zeros((1, width), WIDE)
    for k in range(3):
        part = total.astype(NARROW).astype(WIDE)
        line = jnp.where(lane == k, part, line)
        total = total - part
    top = mine.astype(NARROW).astype(WIDE)
    pieces = [top, mine - top, line]
    spare = out_ref.shape[1] - 2 * share - 1
    pieces += [jnp.zeros((spare, width), WIDE)] if spare else []
    payload = jnp.concatenate(pieces, 0).astype(NARROW)
    for d in range(out_ref.shape[0]):
        out_ref[d] = payload


def squares_of(sel, first, second, body, share, near, shard, devices):
    width = second[0].shape[1]
    ins = list(first) + list(second)
    rows = up(2 * share + 1, 8)
    outs = [shape_of((2, body, width), WIDE), shape_of((2, shard), WIDE), shape_of((devices, rows, width))]
    return run(
        "squares",
        functools.partial(square_kernel, body, share, near),
        sel,
        ins,
        [full(a.shape) for a in ins],
        outs,
        [full(o.shape) for o in outs],
        limit=24,
    )


def stacked_halves(value):
    return jnp.concatenate(split(value), 0)


def turn_kernel(sel, value_ref, basis_ref, out_ref):
    for i in range(value_ref.shape[0]):
        both = dot(stacked_halves(value_ref[i]), basis_ref[i])
        out_ref[i] = both[: both.shape[0] // 2] + both[both.shape[0] // 2 :]


def turn(sel, value, basis):
    return run(
        "turn",
        turn_kernel,
        sel,
        [value, basis],
        [full(a.shape) for a in (value, basis)],
        shape_of(value.shape, WIDE),
        full(value.shape),
        limit=24,
    )


def update_kernel(
    share, near, sel, turned_ref, parts_ref, basis_ref, old_ref, first_ref, second_ref,
    bias_ref, b_old_ref, b_first_ref, b_second_ref, h_old_ref, h_first_ref, h_second_ref,
    norm_ref, pair_ref, new_ref, low_ref, m_ref, v_ref, bn_ref, bm_ref, bv_ref, hn_ref, hm_ref, hv_ref, heads,
):
    classes, width = h_old_ref.shape[0], h_old_ref.shape[1] - 1
    far = parts_ref.shape[0] // (2 * near)
    squares = jnp.zeros((1, 1), WIDE)
    for f in range(far):
        for j in range(near):
            at = (f * near + j) * 2
            both = parts_ref[at].astype(WIDE), parts_ref[at + 1].astype(WIDE)
            spot = (j * far + f) * share
            one, two = (part[:share] + part[share : 2 * share] for part in both)
            heads[spot : spot + share] = one + two
            for part in both:
                squares = squares + jnp.sum(part[2 * share : 2 * share + 1, :LANES], keepdims=True)
    grad = heads[:classes]
    last = heads[classes : classes + 1, :LANES]
    lane = lax.broadcasted_iota(jnp.int32, (classes, LANES), 1)
    here = lane == lax.broadcasted_iota(jnp.int32, (classes, LANES), 0)
    grad_last = jnp.sum(jnp.where(here, last, 0.0), axis=1, keepdims=True)
    squares = squares + jnp.sum(grad * grad, keepdims=True) + jnp.sum(grad_last * grad_last, keepdims=True)
    loss, weight = last[:, classes : classes + 1], last[:, classes + 1 : classes + 2]
    norm = jnp.sqrt(squares) / weight
    norm_ref[...] = norm
    pair_ref[...] = jnp.where(lax.broadcasted_iota(jnp.int32, (1, 2), 1) == 0, loss, weight)
    factor = jnp.minimum(1.0, CLIP / norm) / weight
    bn_ref[...], bm_ref[...], bv_ref[...] = adamw(
        b_old_ref[...], b_first_ref[...], b_second_ref[...], bias_ref[...] * factor, LR_BIAS
    )
    for at, value in ((slice(0, width), grad), (slice(width, width + 1), grad_last)):
        hn_ref[:, at], hm_ref[:, at], hv_ref[:, at] = adamw(
            h_old_ref[:, at], h_first_ref[:, at], h_second_ref[:, at], value * factor, LR_HEAD
        )
    for i in range(turned_ref.shape[0]):
        grad = turned_ref[i] * factor
        first = BETA * first_ref[i] + (1.0 - BETA) * grad
        second = BETA * second_ref[i] + (1.0 - BETA) * grad * grad
        m_ref[i] = first
        v_ref[i] = second
        step = first / (1.0 - BETA**STEP) / (jnp.sqrt(second / (1.0 - BETA**STEP)) + EPSA)
        both = dot_nt(stacked_halves(step), basis_ref[i])
        back = both[: both.shape[0] // 2] + both[both.shape[0] // 2 :]
        new = old_ref[i] - LR_MAT * (back + DECAY * old_ref[i])
        new_ref[i] = new
        low_ref[i] = new.astype(NARROW)


def update(sel, share, near, *ins):
    mats, bias, head = ins[3], ins[7], ins[10]
    outs = [shape_of((1, 1), WIDE), shape_of((1, 2), WIDE), shape_of(mats.shape, WIDE), shape_of(mats.shape)]
    outs += [shape_of(mats.shape, WIDE)] * 2 + [shape_of(bias.shape, WIDE)] * 3 + [shape_of(head.shape, WIDE)] * 3
    rows = ins[1].shape[0] // 2 * share
    return run(
        "update",
        functools.partial(update_kernel, share, near),
        sel,
        ins,
        [full(a.shape) for a in ins],
        outs,
        [full(o.shape) for o in outs],
        [pltpu.VMEM((rows, head.shape[1] - 1), WIDE)],
        limit=24,
    )


def local(
    far,
    near,
    node_states,
    serve,
    neighbors,
    alpha,
    live,
    lam,
    labels,
    link_pair,
    mats,
    mats_m,
    mats_v,
    basis,
    bias,
    bias_m,
    bias_v,
    head,
    head_m,
    head_v,
):
    n = far * near
    branch = lax.axis_index("branch")
    both = ("far", "near")
    rows_dev, width = node_states.shape[1:]
    classes = head.shape[1]
    depth, kinds, _, shard, _ = mats.shape
    slots = serve.shape[1]
    cap = slots // n
    walk = Rows(rows_dev, slots)

    def pick(value):
        return lax.dynamic_index_in_dim(value, branch, 0, keepdims=False)

    def swap(value):
        return lax.ppermute(value, "branch", SWAP)

    def exchange(value, axes):
        return lax.all_to_all(value, axes, 0, 0, tiled=True)

    def hop(value, axis, size, k):
        return lax.ppermute(value, axis, [(i, i ^ k) for i in range(size)]) if k else value

    def spread(rows, count):
        return jnp.broadcast_to(rows[None], (count,) + rows.shape)

    places = (branch, lax.axis_index("far"), lax.axis_index("near"))
    sel = jnp.stack([p.astype(jnp.int32) for p in places])

    low = mats.astype(NARROW).reshape(depth, kinds, shard, width)

    def along_far():
        parts = [hop(low, "far", far, k) for k in range(far)]
        return [jnp.stack([part[layer] for part in parts]) for layer in range(depth)]

    def along_near(pieces):
        return [hop(pieces, "near", near, k) for k in range(near)]

    def join(own):
        other = [swap(piece) for piece in own]
        return list(own) + other if walk.whole and shard % 16 == 0 else assemble(sel, own, other)

    far_0, far_1 = along_far()

    send = take_rows(sel, node_states, serve, bias, n)
    far_0, send = lax.optimization_barrier((far_0, send))
    got = exchange(send, both)
    near_0 = along_near(far_0)
    near_0[1], serve, branch, head = lax.optimization_barrier((near_0[1], serve, branch, head))
    edges, edges_s = make_edges(sel, neighbors.transpose(0, 2, 1), alpha.transpose(0, 2, 1), serve)
    slots_0 = got[:, :cap].reshape(slots, width)
    own_bias = got[:, cap, : depth * shard].reshape(n, depth, shard).transpose(1, 0, 2).reshape(depth, width)
    other_bias = swap(own_bias)
    first = branch == 0
    biases = jnp.stack([jnp.where(first, own_bias, other_bias), jnp.where(first, other_bias, own_bias)], 1)
    biases = biases.astype(WIDE)
    agg = lax.dot_general(edges_s, twice(slots_0), (((0,), (0,)), ((), ())), preferred_element_type=WIDE)
    agg, near_0 = lax.optimization_barrier((agg, near_0))
    agg_0 = exchange(agg.astype(NARROW), both)
    weights = [join(near_0)]
    weights[0], far_1 = lax.optimization_barrier((weights[0], far_1))
    near_1 = along_near(far_1)
    share = -(-(classes + 1) // n)
    sel = jnp.concatenate([sel, pick(live)])

    h_h0, slots_1, m_h0, agg, weights[0] = halo_forward(sel, slots_0, agg_0, weights[0], biases[0], edges_s)
    agg, edges = lax.optimization_barrier((agg, edges))
    agg_1 = exchange(agg, both)
    h_0, x_1, m_0 = forward(walk, sel, node_states, edges, slots_0, weights[0], biases[0])
    weights.append(join(near_1))
    x_1, agg_1 = lax.optimization_barrier((x_1, agg_1))
    own_1, other_1, bias_1, bias_x1, d_x, spread_1, ds_h1, dn_h1, head_rows, weights[1] = last_layer(
        walk, sel, (near, far * share), x_1, edges, slots_1, weights[1], biases[1], (head.T, labels, lam), link_pair,
        agg_1,
    )
    returned = exchange(dn_h1, both)

    packed = pack(sel, far, near, own_1, swap(other_1), bias_1, swap(bias_x1), head_rows)
    *packed, spread_1 = lax.optimization_barrier((*packed, spread_1))
    sums_1 = [hop(piece, "near", near, k) for k, piece in enumerate(packed)]
    own_0, other_0, bias_0, bias_x0 = backward(
        back_first_step, walk, sel, [x_1, m_0, node_states], d_x, edges, h_0,
        [weights[0], h_h0, slots_0, agg_0, weights[1], spread_1, edges_s, returned, ds_h1, slots_1, m_h0],
        slots, False,
    )
    own_0, other_0, bias_x0, sums_1 = lax.optimization_barrier((own_0, other_0, bias_x0, sums_1))
    packed = pack(sel, far, near, own_0, swap(other_0), bias_0, swap(bias_x0), apart=False)
    packed, sums_1 = lax.optimization_barrier((packed, sums_1))
    sums_0 = exchange(packed, "near")
    body = kinds * shard
    parts_1 = [hop(piece, "far", far, k) for k, piece in enumerate(middle(sel, far, share, sums_1, True))]
    low_basis = rounded(sel, basis.reshape(depth * kinds, width, width))
    sums_0, low_basis = lax.optimization_barrier((sums_0, low_basis))
    parts_0 = [hop(piece, "far", far, k) for k, piece in enumerate(middle(sel, far, 0, sums_0, True))]

    sums, sum_bias, parts = squares_of(sel, parts_0, parts_1, body, share, near, shard, 2 * n)
    parts = exchange(parts, both + ("branch",))
    flat = (depth * kinds, shard, width)
    turned = turn(sel, sums.reshape(flat), low_basis)
    norm, loss_parts, mats_new, mats_low, first_new, second_new, *small = update(
        sel, share, near, turned, parts, low_basis,
        *(a.reshape(flat) for a in (mats, mats_m, mats_v)),
        sum_bias, *(a.reshape(depth, shard) for a in (bias, bias_m, bias_v)),
        *(a.T for a in (head, head_m, head_v)),
    )
    return (
        loss_parts[0],
        norm[0, 0],
        *(a.reshape(mats.shape) for a in (mats_new, mats_low, first_new, second_new)),
        *(a.reshape(bias.shape) for a in small[:3]),
        *(a.T for a in small[3:]),
    )


def solution(mesh):
    n = mesh.shape["rows"]
    near = 1 << (n.bit_length() // 2)
    far = n // near
    grid = Mesh(mesh.devices.reshape(far, near, 2), ("far", "near", "branch"))
    rows = ("far", "near")
    by_row = P(None, rows)
    by_row_last = P(None, rows, None)
    matrix = P(None, None, "branch", rows, None)
    vector = P(None, "branch", rows)
    return jax.shard_map(
        functools.partial(local, far, near),
        mesh=grid,
        in_specs=(by_row_last, by_row, by_row_last, by_row_last)
        + (by_row,) * 4
        + (matrix,) * 3
        + (P(None, None, "branch", None, None),)
        + (vector,) * 3
        + (P(),) * 3,
        out_specs=(P(), P()) + (matrix,) * 4 + (vector,) * 3 + (P(),) * 3,
        check_vma=False,
    )
```
